32 devices in a mesh: dp: 16 (over z, y, x), seq: 2 (over core).
Axes of the slice: x: 2, y: 2, z: 4, core: 2. Of those that a mesh axis runs over, the one named last changes fastest.
Arguments:
- layer_input: bfloat16 [48, 512, 768], P('dp', 'seq'), may hold values from -6 to 6
- gain_attn: bfloat16 [768], P(('dp', 'seq')), may hold values from 0.5 to 1.5
- w_query: bfloat16 [768, 768], P(('dp', 'seq')), may hold values from -0.109375 to 0.109375
- w_key: bfloat16 [768, 768], P(('dp', 'seq')), may hold values from -0.109375 to 0.109375
- w_value: bfloat16 [768, 768], P(('dp', 'seq')), may hold values from -0.21875 to 0.21875
- w_output: bfloat16 [768, 768], P(('dp', 'seq')), may hold values from -0.875 to 0.875
- bias_table: bfloat16 [384], P('dp'), may hold values from -6 to 6
- gain_ffn: bfloat16 [768], P(('dp', 'seq')), may hold values from 0.5 to 1.5
- ffn_in: bfloat16 [768, 3072], P(('dp', 'seq')), may hold values from -0.21875 to 0.21875
- ffn_out: bfloat16 [3072, 768], P(('dp', 'seq')), may hold values from -0.109375 to 0.109375
- buckets: int32 [1023], replicated, may hold values from 0 to 31
- keep_mask: int32 [48, 512], P('dp', 'seq'), may hold values from 0 to 1, as said below
- out_grad: bfloat16 [48, 512, 768], P('dp', 'seq'), may hold values from -6 to 6
Outputs:
- layer_out: bfloat16 [48, 512, 768], P('dp', 'seq')
- grad_input: bfloat16 [48, 512, 768], P('dp', 'seq')
- grad_gain_attn: float32 [768], P(('dp', 'seq'))
- grad_query: float32 [768, 768], P(('dp', 'seq'))
- grad_key: float32 [768, 768], P(('dp', 'seq'))
- grad_value: float32 [768, 768], P(('dp', 'seq'))
- grad_output: float32 [768, 768], P(('dp', 'seq'))
- grad_bias: float32 [384], P('dp')
- grad_gain_ffn: float32 [768], P(('dp', 'seq'))
- grad_ffn_in: float32 [768, 3072], P(('dp', 'seq'))
- grad_ffn_out: float32 [3072, 768], P(('dp', 'seq'))
The draws below stay inside these ranges and needn't reach their ends.
Inputs may be any that keep to these rules, and one draw needn't show every extreme that they name: `keep_mask`: each sequence's mask is ones up to its length and zeros after it; every length is 64 or more, and among the 3 sequences of each index of dp at least one has no padding.
All inputs are finite; a program needn't handle non-finite values.
Results may differ from the reference program's by a relative error of at most 0.014.
Values may be sent and summed in bfloat16 or wider, within the bound.
No kernel may reach another device: no remote copies, remote signals or barrier semaphores. Data moves between devices by JAX's collectives and lax.ppermute only.
A program may use at most 192 MiB of HBM per device.

```python
import math
import jax
import jax.numpy as jnp
from jax import lax

D = 768
HEADS = 12
FF = 3072
BUCKETS = 32
LEN = 512
SEQ_DEV = 3
SEQS = 48


def draw_keep_mask(key, part):
    key = jax.random.fold_in(key, 11)
    length_key, pick_key = jax.random.split(key)
    lengths = jax.random.randint(length_key, (SEQS,), LEN // 8, LEN + 1)
    chosen = jax.random.randint(pick_key, (SEQS // SEQ_DEV,), 0, SEQ_DEV)
    groups = jnp.arange(SEQS, dtype=jnp.int32)
    full_rows = groups % SEQ_DEV == jnp.repeat(chosen, SEQ_DEV)
    lengths = jnp.where(full_rows, LEN, lengths)
    positions = jnp.arange(LEN, dtype=jnp.int32)
    return (positions[None, :] < lengths[:, None]).astype(jnp.int32)


def with_ends(result, stream_key, low, largest):
    spot = [jax.random.randint(jax.random.fold_in(stream_key, axis), (), 0, length) for axis, length in enumerate(result.shape)]
    main_axis = result.shape.index(max(result.shape))
    neighbour = spot[:main_axis] + [(spot[main_axis] + 1) % result.shape[main_axis]] + spot[main_axis + 1:]
    return result.at[tuple(spot)].set(low).at[tuple(neighbour)].set(largest)


def with_spikes(values, own_key, source, target, parts, factor):
    owner, partner = [(jnp.arange(values.shape[dim]) // (values.shape[dim] // parts)).reshape([-1 if axis == dim else 1 for axis in range(values.ndim)]) for dim in (source, target)]
    chosen = jax.random.permutation(own_key, parts)[partner]
    strong = (owner == chosen) | (owner == (partner + parts // 2) % parts)
    return jnp.where(strong, factor * values, values)


def block_levels(rng, extent, cuts, smallest, high):
    level = 1.0
    for position, blocks in cuts:
        draws = jax.random.uniform(jax.random.fold_in(jax.random.fold_in(rng, 6), position), (blocks,), jnp.float32, smallest / len(cuts), high / len(cuts))
        level = level * jnp.repeat(jnp.exp(draws), extent[position] // blocks).reshape((-1,) + (1,) * (len(extent) - 1 - position))
    return level


def scatter_about(stream_key, extent, width, most, pieces=(), kind=jnp.bfloat16):
    factor_of = block_levels(stream_key, extent, pieces, -0.22, 0.18) if pieces else 1.0
    values = jax.random.normal(stream_key, extent, jnp.float32) * width * factor_of
    return jnp.minimum(jnp.maximum(values, -most), most).astype(kind)


def bell_draw_with(key, extent, spread, bound, shards, heavy, kind=jnp.bfloat16):
    array = spread * jax.random.normal(key, extent, jnp.float32)
    if shards:
        array = array * block_levels(key, extent, shards, -0.22, 0.18)
    return jnp.clip(with_spikes(array, jax.random.fold_in(key, 3), *heavy), -bound, bound).astype(kind)


def setup_inputs(seed: int = 0) -> dict:
    splits = jax.random.split(jax.random.key(seed), 14)
    return {
        "layer_input": bell_draw_with(splits[0], (SEQS, LEN, D), 1.0, 6.0, ((0, 16), (1, 2)), (0, 2, 16, 2.0)),
        "gain_attn": jnp.clip(1.0 + 0.1 * jax.random.normal(splits[1], (D,), jnp.float32), 0.5, 1.5).astype(jnp.bfloat16),
        "w_query": scatter_about(splits[2], (D, D), (4 * D) ** -0.5, 0.109375, ((0, 32),)),
        "w_key": scatter_about(splits[3], (D, D), (4 * D) ** -0.5, 0.109375, ((0, 32),)),
        "w_value": scatter_about(splits[4], (D, D), D ** -0.5, 0.21875, ((0, 32),)),
        "w_output": scatter_about(splits[5], (D, D), (D // 16) ** -0.5, 0.875, ((0, 32),)),
        "bias_table": scatter_about(splits[6], (HEADS * BUCKETS,), 1.0, 6.0, ((0, 16),)),
        "gain_ffn": jnp.clip(1.0 + 0.1 * jax.random.normal(splits[7], (D,), jnp.float32), 0.5, 1.5).astype(jnp.bfloat16),
        "ffn_in": scatter_about(splits[8], (D, FF), D ** -0.5, 0.21875, ((0, 32),)),
        "ffn_out": scatter_about(splits[9], (FF, D), FF ** -0.5, 0.109375, ((0, 32),)),
        "buckets": with_ends(jax.random.randint(splits[10], (2 * LEN - 1,), 0, BUCKETS), jax.random.fold_in(splits[10], 1), 0, BUCKETS - 1).astype(jnp.int32),
        "keep_mask": draw_keep_mask(jax.random.fold_in(splits[13], 71), 0),
        "out_grad": scatter_about(splits[12], (SEQS, LEN, D), 1.0, 6.0, ((0, 16), (1, 2))),
    }


EPSILON = 1e-06

@jax.custom_vjp
def low(v):
    return lax.optimization_barrier(v.astype(jnp.bfloat16)).astype(jnp.float32)

@jax.custom_vjp
def low_back(v):
    return v

def low_keep(v):
    return (low(v), None)

def low_pass(kept, grad):
    return (grad,)

def back_keep(v):
    return (v, None)

def back_low(kept, grad):
    return (low(grad),)
low.defvjp(low_keep, low_pass)
low_back.defvjp(back_keep, back_low)

def rms_norm(rows, gain):
    scale = lax.rsqrt(lax.optimization_barrier(jnp.mean(rows * rows, axis=-1, keepdims=True)) + EPSILON)
    return rows * scale * gain

def matmul(left, right, form):
    return jnp.einsum(form, left, right, precision=lax.Precision.HIGHEST)

def layer_block(params, block_x, block_keep, buckets):
    gain_attn, w_query, w_key, w_value, w_output, bias_table, gain_ffn, ffn_in, ffn_out = params
    seq_count, length, model_width = block_x.shape
    head_count = bias_table.shape[0] // BUCKETS
    head_dim = model_width // head_count
    normed = low(rms_norm(block_x, gain_attn))

    def project(weight):
        rows = low_back(low(matmul(normed, weight, 'nld,de->nle')))
        return rows.reshape(seq_count, length, head_count, head_dim)
    queries = project(w_query)
    key_rows = project(w_key)
    value_rows = project(w_value)
    per_offset = jnp.take(bias_table.reshape(head_count, BUCKETS), buckets, axis=1)
    positions = jnp.arange(length, dtype=jnp.int32)
    offsets = (positions[None, :] - positions[:, None] + (length - 1)).astype(jnp.int32)
    bias_grid = jnp.take(per_offset, offsets, axis=1)
    product = matmul(queries, key_rows, 'nihd,njhd->nhij')
    scores = low_back(product) + bias_grid[None] + (block_keep[:, None, None, :] - 1.0) * 1000000000.0
    row_max = lax.optimization_barrier(jnp.max(scores, axis=-1, keepdims=True))
    exp_scores = jnp.exp(scores - row_max)
    attn_probs = low(exp_scores / lax.optimization_barrier(jnp.sum(exp_scores, axis=-1, keepdims=True)))
    context = low_back(low(matmul(attn_probs, value_rows, 'nhij,njhd->nihd')))
    context = context.reshape(seq_count, length, model_width)
    middle = block_x + low_back(matmul(context, w_output, 'nld,de->nle'))
    normed_ffn = low(rms_norm(middle, gain_ffn))
    activated = low(jax.nn.gelu(low_back(matmul(normed_ffn, ffn_in, 'nld,df->nlf'))))
    return middle + low_back(matmul(activated, ffn_out, 'nlf,fd->nld'))

def reference(layer_input, gain_attn, w_query, w_key, w_value, w_output, bias_table, gain_ffn, ffn_in, ffn_out, buckets, keep_mask, out_grad):
    params = tuple((item.astype(jnp.float32) for item in (gain_attn, w_query, w_key, w_value, w_output, bias_table, gain_ffn, ffn_in, ffn_out)))
    seq_total, length, model_width = layer_input.shape
    per_block = math.gcd(seq_total, max(1, 4096 // length))
    blocks = seq_total // per_block
    x_blocks = layer_input.astype(jnp.float32).reshape(blocks, per_block, length, model_width)
    keep_blocks = keep_mask.astype(jnp.float32).reshape(blocks, per_block, length)
    block_step = jax.checkpoint(lambda params_in, block_x, block_keep: layer_block(params_in, block_x, block_keep, buckets))

    def whole(params_in, inputs):
        return lax.map(lambda block_pair: block_step(params_in, block_pair[0], block_pair[1]), (inputs, keep_blocks))
    layer_out, pullback = jax.vjp(whole, params, x_blocks)
    gradients, grad_input = pullback(out_grad.astype(jnp.float32).reshape(blocks, per_block, length, model_width))
    shape_out = (seq_total, length, model_width)
    return (layer_out.reshape(shape_out).astype(jnp.bfloat16), grad_input.reshape(shape_out).astype(jnp.bfloat16), gradients[0], gradients[1], gradients[2], gradients[3], gradients[4], gradients[5], gradients[6], gradients[7], gradients[8])
```

```python
import functools
import math

import jax
import jax.numpy as jnp
import numpy as np
from jax import lax
from jax.experimental import pallas as pl
from jax.experimental.pallas import tpu as pltpu
from jax.sharding import PartitionSpec as P

HEADS = 12
HEAD_DIM = 64
BUCKETS = 32
EPSILON = 1e-06
LANES = 128
BF = jnp.bfloat16
F32 = jnp.float32
GELU_A = math.sqrt(2.0 / math.pi)
GELU_B = 0.044715

ANY = pl.BlockSpec(memory_space=pl.ANY)
SMEM = pl.BlockSpec(memory_space=pltpu.SMEM)


def whole(shape):
    zeros = (0,) * len(shape)
    return pl.BlockSpec(shape, lambda *_: zeros)


def params(**extra):
    return pltpu.CompilerParams(vmem_limit_bytes=56 * 1024 * 1024, **extra)


def nn(a, b):
    return lax.dot_general(a, b, (((1,), (0,)), ((), ())), preferred_element_type=F32)


def nt(a, b):
    return lax.dot_general(a, b, (((1,), (1,)), ((), ())), preferred_element_type=F32)


def tn(a, b):
    return lax.dot_general(a, b, (((0,), (0,)), ((), ())), preferred_element_type=F32)


def flip(x, axis, bit, count):
    return lax.ppermute(x, axis, [(i, i ^ bit) for i in range(count)])


def gather_pieces(block, cut, dp):
    have = block[None]
    bit = 4
    while bit < dp:
        have = jnp.concatenate([have, flip(have, "dp", bit, dp)], axis=0)
        bit *= 2
    left, right = have[..., :cut], have[..., cut:]
    left_x = flip(left, "dp", 1, dp)
    right_y = flip(right, "dp", 2, dp)
    left_y = flip(left, "dp", 2, dp)
    right_x = flip(right, "dp", 1, dp)
    left_xy = flip(left_x, "dp", 2, dp)
    right_xy = flip(right_y, "dp", 1, dp)
    return [left, left_x, left_y, left_xy], [right, right_x, right_y, right_xy]


def scatter_pieces(left_send, left_keep, right_send, right_keep, dp):
    def add(a, b):
        return (a.astype(F32) + b.astype(F32)).astype(BF)

    left = add(left_keep, flip(left_send, "dp", 2, dp))
    right = add(right_keep, flip(right_send, "dp", 1, dp))
    left = add(left[0], flip(left[1], "dp", 1, dp))
    right = add(right[0], flip(right[1], "dp", 2, dp))
    have = jnp.concatenate([left, right], axis=-1)
    bit = dp // 2
    while bit >= 4:
        half = have.shape[0] // 2
        have = add(have[:half], flip(have[half:], "dp", bit, dp))
        bit //= 2
    return have[0]


def other_core(x):
    return lax.ppermute(x, "seq", [(0, 1), (1, 0)])


def start_blocks(refs, pos, rows, dst, cols, sems):
    copies = []
    at = 0
    for ref in refs:
        for b in range(ref.shape[0]):
            row = pl.multiple_of(pos[at] * rows, rows)
            src = ref.at[b] if cols is None else ref.at[b, :, pl.ds(*cols)]
            copies.append(pltpu.make_async_copy(src, dst.at[pl.ds(row, rows)], sems.at[at]))
            at += 1
    for copy in copies:
        copy.start()
    return copies


def qkv_kernel(meta, pos, x_own, x_oth, buckets, hsel, bsel, *rest, rows, cut, width, nl, nr):
    left, right = rest[:nl], rest[nl : nl + nr]
    q_ref, k_ref, v_ref, norm_ref, misc, peroff, w, sem_l, sem_r, wl, wr = rest[nl + nr :]
    s = meta[0]
    half = width // 2
    depth = w.shape[0]

    @pl.when(pl.program_id(0) == 0)
    def _():
        copies = start_blocks(left, pos, rows, wl, None, sem_l)
        copies += start_blocks(right, pos, rows, wr, None, sem_r)
        for copy in copies:
            copy.wait()
        w[:, :cut] = wl[...]
        w[:, cut:] = wr[...]
        extra = w[:, 3 * half :].astype(F32)
        misc[...] = extra.T[:8]
        spread = (extra[:, 2:3] * bsel[...]).astype(BF)
        table = nn(hsel[s].astype(BF), spread)
        one_hot = (
            lax.broadcasted_iota(jnp.int32, (LANES, buckets.shape[1]), 0) == buckets[...]
        ).astype(F32)
        peroff[...] = nn(table.astype(BF), one_hot.astype(BF))

    gain = misc[0:1, :]
    count = x_own.shape[1]
    for side, x_ref in ((0, x_own), (1, x_oth)):
        x = x_ref[0].astype(F32)
        scale = lax.rsqrt(jnp.mean(x * x, axis=-1, keepdims=True) + EPSILON)
        normed = (x * scale * gain).astype(BF)
        at = pl.ds(pl.multiple_of((s if side == 0 else 1 - s) * count, count), count)
        norm_ref[0, at, :] = normed
        q_ref[0, at, :] = nn(normed, w[:, :half]).astype(BF)
        k_ref[0, at, :] = nn(normed, w[:, half : 2 * half]).astype(BF)
        v_ref[0, at, :] = nn(normed, w[:, 2 * half : 3 * half]).astype(BF)


def lane_half(shape, which):
    lane = lax.broadcasted_iota(jnp.int32, shape, 1)
    return (lane < HEAD_DIM) if which == 0 else (lane >= HEAD_DIM)


def attend_kernel(meta, q_ref, k_ref, v_ref, mask_ref, peroff, own_ref, oth_ref, e_ref, inv_ref, grid, ctx):
    s = meta[0]
    hp = pl.program_id(0)
    length = q_ref.shape[1]
    step = LANES
    span = grid.shape[-1]

    @pl.when(pl.program_id(1) == 0)
    def _():
        for hh in range(2):
            row = peroff[pl.ds(2 * hp + hh, 1), :]
            wide = jnp.broadcast_to(row, (step, span))
            grid[hh] = pltpu.roll(wide, span - step + 1, 1, stride=1, stride_axis=0)

    q, k, v, mask = q_ref[0], k_ref[0], v_ref[0], mask_ref[0]
    zero = jnp.zeros((), BF)
    one = jnp.ones((), BF)
    first = lane_half((length, LANES), 0)
    sums = []
    for hh in range(2):
        keep = first if hh == 0 else ~first
        q_head = jnp.where(keep, q, zero)
        v_head = jnp.where(keep, v, one)
        parts = []
        for a in range(length // step):
            base = length - step - a * step
            scores = nt(q_head[a * step : (a + 1) * step], k)
            scores = scores + grid[hh, :, base : base + length] + mask
            top = jnp.max(scores, axis=-1, keepdims=True)
            low = jnp.exp(scores - top).astype(BF)
            e_ref[0, 0, hh, a * step : (a + 1) * step, :] = low
            parts.append(nn(low, v_head))
        sums.append(jnp.concatenate(parts, axis=0))
    num = jnp.where(first, sums[0], sums[1])
    den = pltpu.roll(jnp.where(first, sums[1], sums[0]), HEAD_DIM, 1)
    inv = 1.0 / den
    inv_ref[0] = inv
    ctx[...] = (num * inv).astype(BF)
    half = length // 2
    own_ref[0] = ctx[pl.ds(pl.multiple_of(s * half, half), half), :]
    oth_ref[0] = ctx[pl.ds(pl.multiple_of((1 - s) * half, half), half), :]


def middle_kernel(meta, pos, x_ref, own_ref, oth_ref, misc, *rest, rows, nb):
    own_w, oth_w = rest[:nb], rest[nb : 2 * nb]
    mid_ref, norm_ref, w, sem_a, sem_b = rest[2 * nb :]
    s = meta[0]
    half = w.shape[2]

    @pl.when(pl.program_id(0) == 0)
    def _():
        copies = start_blocks(own_w, pos, rows, w.at[s], None, sem_a)
        copies += start_blocks(oth_w, pos, rows, w.at[1 - s], None, sem_b)
        for copy in copies:
            copy.wait()

    x = x_ref[0].astype(F32)
    own, oth = own_ref[0], oth_ref[0]
    at_own = pl.ds(pl.multiple_of(s * half, half), half)
    at_oth = pl.ds(pl.multiple_of((1 - s) * half, half), half)
    parts = []
    for c in range(2):
        part = nn(own, w[c, at_own, :]) + nn(oth, w[c, at_oth, :])
        parts.append(x[:, c * half : (c + 1) * half] + part)
    middle = jnp.concatenate(parts, axis=-1)
    mid_ref[0] = middle
    scale = lax.rsqrt(jnp.mean(middle * middle, axis=-1, keepdims=True) + EPSILON)
    norm_ref[0] = (middle * scale * misc[1:2, :]).astype(BF)


def hidden_kernel(pos, own_ref, oth_ref, *rest, rows, cols, nl, nr):
    left, right = rest[:nl], rest[nl : nl + nr]
    act_ref, slope_ref, w, sem_l, sem_r, wl, wr = rest[nl + nr :]

    @pl.when(pl.program_id(0) == 0)
    def _():
        copies = start_blocks(left, pos, rows, wl, cols, sem_l)
        copies += start_blocks(right, pos, rows, wr, None, sem_r)
        for copy in copies:
            copy.wait()
        w[:, : wl.shape[1]] = wl[...]
        w[:, wl.shape[1] :] = wr[...]

    count = own_ref.shape[1]
    width = w.shape[1]
    step = 512 if width % 512 == 0 else width
    for side, ref in ((0, own_ref), (1, oth_ref)):
        for c in range(0, width, step):
            v = nn(ref[0], w[:, c : c + step])
            square = v * v
            t = jnp.tanh(v * (GELU_A + (GELU_A * GELU_B) * square))
            half_up = 0.5 + 0.5 * t
            slope = half_up + (0.5 * v) * (1.0 - t * t) * (GELU_A + (3.0 * GELU_A * GELU_B) * square)
            act_ref[0, side * count : (side + 1) * count, c : c + step] = (v * half_up).astype(BF)
            slope_ref[0, side * count : (side + 1) * count, c : c + step] = slope.astype(BF)


def wgrad_kernel(meta, *rest, na, nb, rows, cut, dp, cols):
    a_refs, b_refs = rest[:na], rest[na : na + nb]
    ls, lk, rs, rk, total = rest[na + nb :]
    mb = a_refs[0].shape[-1]
    i = pl.program_id(0)
    acc = None
    for a_ref, b_ref in zip(a_refs, b_refs):
        a = a_ref[...].reshape(-1, mb)
        b = b_ref[...].reshape(a.shape[0], -1)
        part = tn(a, b)
        acc = part if acc is None else acc + part
    total[pl.ds(pl.multiple_of(i * mb, mb), mb), :] = acc

    @pl.when(i == pl.num_programs(0) - 1)
    def _():
        store_relative(meta, total, ls, lk, rs, rk, rows, cut, dp)


def store_relative(meta, total, ls, lk, rs, rk, rows, cut, dp):
    d = meta[1]
    for rel in range(dp):
        x, y, high = rel & 1, (rel >> 1) & 1, rel >> 2
        at = pl.ds(pl.multiple_of((d ^ rel) * rows, rows), rows)
        (ls if y else lk)[x, high] = total[at, :cut].astype(BF)
        (rs if x else rk)[y, high] = total[at, cut:].astype(BF)


def ffn_back_kernel(pos, g_own, g_oth, slope_ref, w_in, *rest, rows, nl, nr):
    left, right = rest[:nl], rest[nl : nl + nr]
    pre_ref, own_ref, oth_ref, w, sem_l, sem_r, wl, wr = rest[nl + nr :]

    @pl.when(pl.program_id(0) == 0)
    def _():
        copies = start_blocks(left, pos, rows, wl, None, sem_l)
        copies += start_blocks(right, pos, rows, wr, None, sem_r)
        for copy in copies:
            copy.wait()
        w[:, : wl.shape[1]] = wl[...]
        w[:, wl.shape[1] :] = wr[...]

    count = g_own.shape[1]
    width = w.shape[0]
    step = 512 if width % 512 == 0 else width
    for side, ref in ((0, g_own), (1, g_oth)):
        g = ref[0]
        for c in range(0, width, step):
            grad = nt(g, w[c : c + step, :])
            slope = slope_ref[0, side * count : (side + 1) * count, c : c + step].astype(F32)
            pre_ref[0, side * count : (side + 1) * count, c : c + step] = (grad * slope).astype(BF)
        back = nt(pre_ref[0, side * count : (side + 1) * count, :], w_in[...])
        if side == 0:
            own_ref[0] = back
        else:
            oth_ref[0] = back.astype(BF)


def ffn_out_kernel(act_ref, w, own_ref, oth_ref):
    count = own_ref.shape[1]
    own_ref[0] = nn(act_ref[0, :count, :], w[...])
    oth_ref[0] = nn(act_ref[0, count:, :], w[...]).astype(BF)


def middle_back_kernel(meta, g_ref, mid_ref, own_ref, oth_ref, misc, w, gm_ref, low_ref, cown_ref, coth_ref):
    s = meta[0]
    half = w.shape[2]
    middle = mid_ref[0]
    scale = lax.rsqrt(jnp.mean(middle * middle, axis=-1, keepdims=True) + EPSILON)
    grad = own_ref[0] + oth_ref[0].astype(F32)
    scaled = grad * misc[1:2, :]
    inner = jnp.mean(scaled * middle, axis=-1, keepdims=True)
    grad_middle = g_ref[0].astype(F32) + scale * scaled - middle * (scale * scale * scale) * inner
    gm_ref[0] = grad_middle
    low = grad_middle.astype(BF)
    low_ref[0] = low
    for ref, which in ((cown_ref, s), (coth_ref, 1 - s)):
        at = pl.ds(pl.multiple_of(which * half, half), half)
        out = nt(low[:, :half], w[0, at, :]) + nt(low[:, half:], w[1, at, :])
        ref[0] = out.astype(BF)


def wo_grad_kernel(meta, own_ref, oth_ref, low_ref, keep_ref, send_ref, total, *, rows, dp):
    s, d = meta[0], meta[1]
    half = own_ref.shape[-1]
    low = low_ref[...].reshape(-1, low_ref.shape[-1])
    for ref, which in ((own_ref, s), (oth_ref, 1 - s)):
        at = pl.ds(pl.multiple_of(which * half, half), half)
        grad = tn(ref[...].reshape(low.shape[0], half), low)
        total[0, at, :] = grad[:, :half]
        total[1, at, :] = grad[:, half:]
    for rel in range(dp):
        at = pl.ds(pl.multiple_of((d ^ rel) * rows, rows), rows)
        keep_ref[rel] = total[s, at, :].astype(BF)
        send_ref[rel] = total[1 - s, at, :].astype(BF)


def attend_back_kernel(meta, q_ref, k_ref, v_ref, e_ref, inv_ref, own_ref, oth_ref, dq_ref, dk_ref, dv_ref, off_ref, diag, dctx):
    s = meta[0]
    length = q_ref.shape[1]
    half = length // 2
    step = LANES
    n = pl.program_id(1)
    dctx[pl.ds(pl.multiple_of(s * half, half), half), :] = own_ref[0]
    dctx[pl.ds(pl.multiple_of((1 - s) * half, half), half), :] = oth_ref[0]

    @pl.when(n == 0)
    def _():
        diag[...] = jnp.zeros_like(diag)

    q, k, v, inv = q_ref[0], k_ref[0], v_ref[0], inv_ref[0]
    scaled = (dctx[...].astype(F32) * inv).astype(BF)
    zero = jnp.zeros((), BF)
    first = lane_half((length, LANES), 0)
    dq_parts = [None] * (length // step)
    dk = jnp.zeros((length, LANES), F32)
    dv = jnp.zeros((length, LANES), F32)
    for hh in range(2):
        keep = first if hh == 0 else ~first
        q_head, k_head, c_head = (jnp.where(keep, x, zero) for x in (q, k, scaled))
        lane = hh * HEAD_DIM
        for a in range(length // step):
            at = slice(a * step, (a + 1) * step)
            base = length - step - a * step
            low = e_ref[0, 0, hh, at, :]
            e = low.astype(F32)
            term = e * nt(c_head[at], v)
            delta = jnp.sum(term, axis=-1, keepdims=True) * inv[at, lane : lane + 1]
            grad = term - e * delta
            diag[hh, :, base : base + length] += grad
            grad_low = grad.astype(BF)
            part = nn(grad_low, k_head)
            dq_parts[a] = part if hh == 0 else dq_parts[a] + part
            dk = dk + tn(grad_low, q_head[at])
            dv = dv + tn(low, c_head[at])
    dq_ref[0] = jnp.concatenate(dq_parts, axis=0).astype(BF)
    dk_ref[0] = dk.astype(BF)
    dv_ref[0] = dv.astype(BF)

    @pl.when(n == pl.num_programs(1) - 1)
    def _():
        span = diag.shape[-1]
        for hh in range(2):
            acc = jnp.zeros((8, span), F32)
            for g in range(step // 8):
                rows = diag[hh, 8 * g : 8 * g + 8, :]
                shift = step - 8 - 8 * g
                acc = acc + (pltpu.roll(rows, shift, 1) if shift else rows)
            out = acc[7:8]
            for b in range(7):
                out = out + pltpu.roll(acc[b : b + 1], 7 - b, 1)
            off_ref[0, hh : hh + 1, :] = out


def qkv_grad_kernel(meta, norm_ref, dq_ref, dk_ref, dv_ref, off_ref, buckets, hsel, bsel, ls, lk, rs, rk, total, *, rows, cut, dp):
    s = meta[0]
    i = pl.program_id(0)
    mb = norm_ref.shape[-1]
    half = dq_ref.shape[-1]
    a = norm_ref[...].reshape(-1, mb)
    at = pl.ds(pl.multiple_of(i * mb, mb), mb)
    for c, ref in enumerate((dq_ref, dk_ref, dv_ref)):
        total[at, c * half : (c + 1) * half] = tn(a, ref[...].reshape(a.shape[0], half))

    @pl.when(i == pl.num_programs(0) - 1)
    def _():
        one_hot = (
            lax.broadcasted_iota(jnp.int32, (LANES, buckets.shape[1]), 0) == buckets[...]
        ).astype(F32)
        per_bucket = lax.dot_general(
            off_ref[...], one_hot, (((1,), (1,)), ((), ())), precision=lax.Precision.HIGHEST, preferred_element_type=F32
        )
        spread = lax.dot_general(
            hsel[s], per_bucket, (((0,), (0,)), ((), ())), precision=lax.Precision.HIGHEST, preferred_element_type=F32
        )
        column = jnp.sum(spread * bsel[...], axis=-1, keepdims=True)
        total[:, 3 * half :] = jnp.broadcast_to(column, (column.shape[0], LANES))
        store_relative(meta, total, ls, lk, rs, rk, rows, cut, dp)


def input_grad_kernel(meta, dq_ref, dk_ref, dv_ref, w, own_ref, oth_ref):
    s = meta[0]
    half = dq_ref.shape[-1]
    count = own_ref.shape[1]
    for side, ref in ((0, own_ref), (1, oth_ref)):
        at = pl.ds(pl.multiple_of((s if side == 0 else 1 - s) * count, count), count)
        out = nt(dq_ref[0, at, :], w[:, :half])
        out = out + nt(dk_ref[0, at, :], w[:, half : 2 * half])
        out = out + nt(dv_ref[0, at, :], w[:, 2 * half : 3 * half])
        ref[0] = out.astype(ref.dtype)


def last_kernel(x_ref, gm_ref, own_ref, oth_ref, misc, out_ref):
    x = x_ref[0].astype(F32)
    scale = lax.rsqrt(jnp.mean(x * x, axis=-1, keepdims=True) + EPSILON)
    scaled = (own_ref[0] + oth_ref[0].astype(F32)) * misc[0:1, :]
    inner = jnp.mean(scaled * x, axis=-1, keepdims=True)
    out_ref[0] = (gm_ref[0] + scale * scaled - x * (scale * scale * scale) * inner).astype(BF)


def body(
    layer_input,
    gain_attn,
    w_query,
    w_key,
    w_value,
    w_output,
    bias_table,
    gain_ffn,
    ffn_in,
    ffn_out,
    buckets,
    keep_mask,
    out_grad,
):
    dp = lax.axis_size("dp")
    s = lax.axis_index("seq")
    d = lax.axis_index("dp")
    nseq, count, width = layer_input.shape
    length = 2 * count
    span = 2 * length
    half = width // 2
    shard = w_query.shape[0]
    rows = 2 * shard
    hid_rows = ffn_out.shape[0]
    hid = hid_rows * dp
    table_rows = bias_table.shape[0]
    tok = nseq * length
    pairs = half // LANES
    meta = jnp.stack([s, d]).astype(jnp.int32)
    aligned = rows % 16 == 0 and hid_rows % 16 == 0

    def sds(shape, dtype=BF):
        return jax.ShapeDtypeStruct(shape, dtype)

    def columns(h):
        cut = [lax.dynamic_slice_in_dim(w, h * half, half, 1) for w in (w_query, w_key, w_value)]
        table = jnp.pad(bias_table, (0, shard - table_rows))
        extra = jnp.stack([gain_attn, gain_ffn, table], axis=1)
        extra = jnp.pad(extra, ((0, 0), (0, LANES - 3)))
        out_cols = lax.dynamic_slice_in_dim(w_output, h * half, half, 1)
        in_cols = lax.dynamic_index_in_dim(ffn_in.reshape(shard, dp, 2, hid_rows), h, 2, keepdims=False)
        return jnp.concatenate(cut + [extra, out_cols, in_cols.reshape(shard, hid)], axis=1)

    mine, theirs = columns(s), other_core(columns(1 - s))
    joined = jnp.where(s == 0, jnp.concatenate([mine, theirs]), jnp.concatenate([theirs, mine]))
    x_oth = other_core(layer_input)
    g_oth = other_core(out_grad)
    keep_oth = other_core(keep_mask.astype(BF))
    keep = keep_mask.astype(BF)
    keep = jnp.where(s == 0, jnp.concatenate([keep, keep_oth], 1), jnp.concatenate([keep_oth, keep], 1))
    mask = ((keep.astype(F32) - 1.0) * 1e9)[:, None, :]
    first_cols = 3 * half + LANES
    first_cut = (first_cols // LANES // 2) * LANES
    second_cut = ((half + hid) // LANES // 2) * LANES
    third_cut = (width // LANES // 2) * LANES

    first_l, first_r = gather_pieces(joined[:, :first_cols], first_cut, dp)
    second_l, second_r = gather_pieces(joined[:, first_cols:], second_cut, dp)
    third_l, third_r = gather_pieces(ffn_out, third_cut, dp)

    high = dp // 4
    relative = np.array([(h << 2) | low for low in range(4) for h in range(high)], np.int32)
    pos = (d ^ jnp.asarray(relative)).astype(jnp.int32)

    def settle(pieces, cols=None):
        if aligned:
            return pieces
        every = jnp.concatenate(pieces, axis=0)
        order = jnp.argsort(pos)
        return [every[order].reshape(1, -1, every.shape[-1])]

    if not aligned:
        pos_k, rows_k, hid_rows_k, nblk, dp_k = jnp.zeros((1,), jnp.int32), width, hid, 1, 1
    else:
        pos_k, rows_k, hid_rows_k, nblk, dp_k = pos, rows, hid_rows, dp, dp

    feature = np.arange(width)
    chunk, within = feature // rows, feature % rows
    entry = np.where(within % shard < table_rows, table_rows * chunk + within % shard, -1)
    head, bucket = entry // BUCKETS, entry % BUCKETS
    half_heads = HEADS // 2
    hsel = np.zeros((2, 8, width), np.float32)
    bsel = np.zeros((width, LANES), np.float32)
    for f in range(width):
        if entry[f] >= 0:
            hsel[head[f] // half_heads, head[f] % half_heads, f] = 1.0
            bsel[f, bucket[f]] = 1.0
    bsel_once = jnp.asarray(np.where(within[:, None] < shard, bsel, 0.0))
    hsel, bsel = jnp.asarray(hsel), jnp.asarray(bsel)
    padded = jnp.concatenate([buckets, jnp.full((span - buckets.shape[0],), -1, jnp.int32)])[None]

    a_l, a_r = settle(first_l), settle(first_r)
    seq_block = lambda shape: pl.BlockSpec((1,) + shape, lambda n: (n, 0, 0))
    q, k, v, normed_attn, misc, peroff, w_qkv = pl.pallas_call(
        functools.partial(
            qkv_kernel, rows=rows_k, cut=first_cut, width=width, nl=len(a_l), nr=len(a_r)
        ),
        grid=(nseq,),
        in_specs=[SMEM, SMEM, seq_block((count, width)), seq_block((count, width)), whole((1, span)), whole(hsel.shape), whole(bsel.shape)]
        + [ANY] * (len(a_l) + len(a_r)),
        out_specs=[seq_block((length, half))] * 3
        + [seq_block((length, width)), whole((8, width)), whole((8, span)), whole((width, first_cols))],
        out_shape=[sds((nseq, length, half))] * 3
        + [sds((nseq, length, width)), sds((8, width), F32), sds((8, span), F32), sds((width, first_cols))],
        scratch_shapes=[
            pltpu.SemaphoreType.DMA((nblk,)),
            pltpu.SemaphoreType.DMA((nblk,)),
            pltpu.VMEM((width, first_cut), BF),
            pltpu.VMEM((width, first_cols - first_cut), BF),
        ],
        compiler_params=params(),
        name="qkv",
    )(meta, pos_k, layer_input, x_oth, padded, hsel, bsel_once, *a_l, *a_r)

    pair = pl.BlockSpec((1, length, LANES), lambda h, n: (n, 0, h))
    pair_half = pl.BlockSpec((1, count, LANES), lambda h, n: (n, 0, h))
    e_block = pl.BlockSpec((1, 1, 2, length, length), lambda h, n: (n, h, 0, 0, 0))
    ctx_own, ctx_send, expo, inv = pl.pallas_call(
        attend_kernel,
        grid=(pairs, nseq),
        in_specs=[SMEM, pair, pair, pair, pl.BlockSpec((1, 1, length), lambda h, n: (n, 0, 0)), whole((8, span))],
        out_specs=[pair_half, pair_half, e_block, pair],
        out_shape=[
            sds((nseq, count, half)),
            sds((nseq, count, half)),
            sds((nseq, pairs, 2, length, length)),
            sds((nseq, length, half), F32),
        ],
        scratch_shapes=[pltpu.VMEM((2, LANES, span), F32), pltpu.VMEM((length, LANES), BF)],
        compiler_params=params(),
        name="attend",
    )(meta, q, k, v, mask, peroff)
    ctx_oth = other_core(ctx_send)

    wo_own = jnp.concatenate([x[..., :half] for x in second_l], axis=0)
    wo_oth = other_core(wo_own)
    wo_own, wo_oth = settle([wo_own]), settle([wo_oth])
    middle, normed_ffn, w_o = pl.pallas_call(
        functools.partial(middle_kernel, rows=rows_k, nb=1),
        grid=(nseq,),
        in_specs=[SMEM, SMEM, seq_block((count, width)), seq_block((count, half)), seq_block((count, half)), whole((8, width)), ANY, ANY],
        out_specs=[seq_block((count, width)), seq_block((count, width)), whole((2, width, half))],
        out_shape=[sds((nseq, count, width), F32), sds((nseq, count, width)), sds((2, width, half))],
        scratch_shapes=[pltpu.SemaphoreType.DMA((nblk,)), pltpu.SemaphoreType.DMA((nblk,))],
        compiler_params=params(),
        name="middle",
    )(meta, pos_k, layer_input, ctx_own, ctx_oth, misc, *wo_own, *wo_oth)
    normed_oth = other_core(normed_ffn)

    b_l, b_r = settle(second_l), settle(second_r)
    act, slope, w_in = pl.pallas_call(
        functools.partial(
            hidden_kernel, rows=rows_k, cols=(half, second_cut - half), nl=len(b_l), nr=len(b_r)
        ),
        grid=(nseq,),
        in_specs=[SMEM, seq_block((count, width)), seq_block((count, width))] + [ANY] * (len(b_l) + len(b_r)),
        out_specs=[seq_block((length, hid)), seq_block((length, hid)), whole((width, hid))],
        out_shape=[sds((nseq, length, hid)), sds((nseq, length, hid)), sds((width, hid))],
        scratch_shapes=[
            pltpu.SemaphoreType.DMA((nblk,)),
            pltpu.SemaphoreType.DMA((nblk,)),
            pltpu.VMEM((width, second_cut - half), BF),
            pltpu.VMEM((width, half + hid - second_cut), BF),
        ],
        compiler_params=params(),
        name="hidden",
    )(pos_k, normed_ffn, normed_oth, *b_l, *b_r)

    def block_outs(block_rows, cut, cols):
        if aligned:
            left, right = (2, high, block_rows, cut), (2, high, block_rows, cols - cut)
            return [left, left, right, right]
        return [(dp * block_rows, cols)]

    def in_relative(parts, block_rows, cut):
        if aligned:
            return parts
        blocks = parts[0].reshape(dp, block_rows, -1)[pos].reshape(2, 2, high, block_rows, -1)
        left, right = blocks[..., :cut], blocks[..., cut:]
        return left[1], left[0], right[:, 1], right[:, 0]

    def whole_wgrad(meta, *rest, na, nb, **_):
        a_refs, b_refs = rest[:na], rest[na : na + nb]
        out = rest[na + nb]
        acc = None
        for a_ref, b_ref in zip(a_refs, b_refs):
            a = a_ref[...].reshape(-1, a_ref.shape[-1])
            part = tn(a, b_ref[...].reshape(a.shape[0], -1))
            acc = part if acc is None else acc + part
        out[...] = acc.astype(BF)

    def wgrad(a_list, b_list, block_rows, cut, name):
        m, cols = a_list[0].shape[-1], b_list[0].shape[-1]
        mb = 384
        shapes = block_outs(block_rows, cut, cols)
        kernel = wgrad_kernel if aligned else whole_wgrad
        out_specs = [whole(x) for x in shapes] if aligned else [pl.BlockSpec((mb, cols), lambda i: (i, 0))]
        return in_relative(
            pl.pallas_call(
                functools.partial(kernel, na=len(a_list), nb=len(b_list), rows=block_rows, cut=cut, dp=dp, cols=cols),
                grid=(m // mb,),
                in_specs=[SMEM]
                + [pl.BlockSpec(a.shape[:2] + (mb,), lambda i: (0, 0, i)) for a in a_list]
                + [whole(b.shape) for b in b_list],
                out_specs=out_specs,
                out_shape=[sds(x) for x in shapes],
                scratch_shapes=[pltpu.VMEM((m, cols), F32)] if aligned else [],
                compiler_params=params(),
                name=name,
            )(meta, *a_list, *b_list),
            block_rows,
            cut,
        )

    act_own, act_oth = act[:, :count], act[:, count:]
    grad_out_parts = wgrad([act_own, act_oth], [out_grad, g_oth], hid_rows, third_cut, "grad_ffn_out")
    grad_ffn_out = scatter_pieces(*grad_out_parts, dp).astype(F32)

    c_l, c_r = settle(third_l), settle(third_r)
    grad_pre, back_own, back_send, w_out = pl.pallas_call(
        functools.partial(ffn_back_kernel, rows=hid_rows_k, nl=len(c_l), nr=len(c_r)),
        grid=(nseq,),
        in_specs=[SMEM, seq_block((count, width)), seq_block((count, width)), seq_block((length, hid)), whole((width, hid))]
        + [ANY] * (len(c_l) + len(c_r)),
        out_specs=[seq_block((length, hid)), seq_block((count, width)), seq_block((count, width)), whole((hid, width))],
        out_shape=[sds((nseq, length, hid)), sds((nseq, count, width), F32), sds((nseq, count, width)), sds((hid, width))],
        scratch_shapes=[
            pltpu.SemaphoreType.DMA((nblk,)),
            pltpu.SemaphoreType.DMA((nblk,)),
            pltpu.VMEM((hid, third_cut), BF),
            pltpu.VMEM((hid, width - third_cut), BF),
        ],
        compiler_params=params(),
        name="ffn_back",
    )(pos_k, out_grad, g_oth, slope, w_in, *c_l, *c_r)
    back_oth = other_core(back_send)

    pre_own, pre_oth = grad_pre[:, :count], grad_pre[:, count:]
    in_cut = (hid // LANES // 2) * LANES
    grad_in_parts = wgrad([normed_ffn, normed_oth], [pre_own, pre_oth], rows, in_cut, "grad_ffn_in")
    grad_in_block = scatter_pieces(*grad_in_parts, dp)

    out_own, out_send = pl.pallas_call(
        ffn_out_kernel,
        grid=(nseq,),
        in_specs=[seq_block((length, hid)), whole((hid, width))],
        out_specs=[seq_block((count, width)), seq_block((count, width))],
        out_shape=[sds((nseq, count, width), F32), sds((nseq, count, width))],
        compiler_params=params(),
        name="ffn_out",
    )(act, w_out)
    layer_out = (middle + out_own + other_core(out_send).astype(F32)).astype(BF)

    grad_middle, middle_low, dctx_own, dctx_send = pl.pallas_call(
        middle_back_kernel,
        grid=(nseq,),
        in_specs=[SMEM] + [seq_block((count, width))] * 4 + [whole((8, width)), whole((2, width, half))],
        out_specs=[seq_block((count, width)), seq_block((count, width)), seq_block((count, half)), seq_block((count, half))],
        out_shape=[
            sds((nseq, count, width), F32),
            sds((nseq, count, width)),
            sds((nseq, count, half)),
            sds((nseq, count, half)),
        ],
        compiler_params=params(),
        name="middle_back",
    )(meta, out_grad, middle, back_own, back_oth, misc, w_o)
    dctx_oth = other_core(dctx_send)

    rel_meta = meta if aligned else jnp.stack([s, jnp.zeros_like(d)]).astype(jnp.int32)
    wo_keep, wo_send = pl.pallas_call(
        functools.partial(wo_grad_kernel, rows=rows_k, dp=dp_k),
        out_shape=[sds((dp_k, rows_k, half))] * 2,
        in_specs=[SMEM, whole(ctx_own.shape), whole(ctx_oth.shape), whole(middle_low.shape)],
        out_specs=[whole((dp_k, rows_k, half))] * 2,
        scratch_shapes=[pltpu.VMEM((2, width, half), F32)],
        grid=(1,),
        compiler_params=params(),
        name="grad_output",
    )(rel_meta, ctx_own, ctx_oth, middle_low)
    wo_sum = (wo_keep.astype(F32) + other_core(wo_send).astype(F32)).astype(BF)
    if not aligned:
        wo_sum = wo_sum.reshape(dp, rows, half)[d ^ jnp.arange(dp)]
    wo_cut = (half // LANES // 2) * LANES
    by_bits = wo_sum.reshape(high, 2, 2, rows, half)
    wo_left = jnp.swapaxes(by_bits[..., :wo_cut], 0, 2)
    wo_right = jnp.moveaxis(by_bits[..., wo_cut:], 0, 2)
    wo_parts = (wo_left[:, 1], wo_left[:, 0], wo_right[:, 1], wo_right[:, 0])
    wo_block = scatter_pieces(*wo_parts, dp)

    dq, dk, dv, off = pl.pallas_call(
        attend_back_kernel,
        grid=(pairs, nseq),
        in_specs=[SMEM, pair, pair, pair, e_block, pair, pair_half, pair_half],
        out_specs=[pair, pair, pair, pl.BlockSpec((1, 2, span), lambda h, n: (h, 0, 0))],
        out_shape=[sds((nseq, length, half))] * 3 + [sds((pairs, 2, span), F32)],
        scratch_shapes=[pltpu.VMEM((2, LANES, span), F32), pltpu.VMEM((length, LANES), BF)],
        compiler_params=params(),
        name="attend_back",
    )(meta, q, k, v, expo, inv, dctx_own, dctx_oth)
    off = jnp.pad(off.reshape(half_heads, span), ((0, 8 - half_heads), (0, 0)))

    mb = 384
    shapes = block_outs(rows, first_cut, first_cols)
    whole_shapes = shapes if aligned else [(width, first_cols)]

    def qkv_whole(meta, *rest):
        ins, out, total = rest[:8], rest[8], rest[9]
        qkv_grad_kernel(meta, *ins, None, None, None, None, total, rows=width, cut=first_cut, dp=0)
        out[...] = total[...].astype(BF)

    qkv_parts = in_relative(
        pl.pallas_call(
            functools.partial(qkv_grad_kernel, rows=rows, cut=first_cut, dp=dp) if aligned else qkv_whole,
            grid=(width // mb,),
            in_specs=[SMEM, pl.BlockSpec((nseq, length, mb), lambda i: (0, 0, i))]
            + [whole((nseq, length, half))] * 3
            + [whole((8, span)), whole((1, span)), whole(hsel.shape), whole(bsel.shape)],
            out_specs=[whole(x) for x in whole_shapes],
            out_shape=[sds(x) for x in whole_shapes],
            scratch_shapes=[pltpu.VMEM((width, first_cols), F32)],
            compiler_params=params(),
            name="grad_qkv",
        )(meta, normed_attn, dq, dk, dv, off, padded, hsel, bsel),
        rows,
        first_cut,
    )
    qkv_block = scatter_pieces(*qkv_parts, dp)

    dn_own, dn_send = pl.pallas_call(
        input_grad_kernel,
        grid=(nseq,),
        in_specs=[SMEM] + [seq_block((length, half))] * 3 + [whole((width, first_cols))],
        out_specs=[seq_block((count, width)), seq_block((count, width))],
        out_shape=[sds((nseq, count, width), F32), sds((nseq, count, width))],
        compiler_params=params(),
        name="input_grad",
    )(meta, dq, dk, dv, w_qkv)
    grad_input = pl.pallas_call(
        last_kernel,
        grid=(nseq,),
        in_specs=[seq_block((count, width))] * 4 + [whole((8, width))],
        out_specs=seq_block((count, width)),
        out_shape=sds((nseq, count, width)),
        compiler_params=params(),
        name="last",
    )(layer_input, grad_middle, dn_own, other_core(dn_send), misc)

    def both_cores(block):
        mine = lax.dynamic_slice_in_dim(block, s * shard, shard, 0)
        theirs = other_core(lax.dynamic_slice_in_dim(block, (1 - s) * shard, shard, 0))
        first, last = jnp.where(s == 0, mine, theirs), jnp.where(s == 0, theirs, mine)
        return first.astype(F32), last.astype(F32)

    in_first, in_last = both_cores(grad_in_block)
    grad_ffn_in = jnp.stack(
        [in_first.reshape(shard, dp, hid_rows), in_last.reshape(shard, dp, hid_rows)], axis=2
    ).reshape(shard, 2 * hid)
    wo_first, wo_last = both_cores(wo_block)
    grad_output = jnp.concatenate([wo_first, wo_last], axis=1)
    qkv_first, qkv_last = both_cores(qkv_block)
    grad_query, grad_key, grad_value = (
        jnp.concatenate([x[:, c * half : (c + 1) * half] for x in (qkv_first, qkv_last)], axis=1)
        for c in range(3)
    )
    grad_gain_attn = sum(
        jnp.sum(w.astype(F32) * g, axis=1)
        for w, g in ((w_query, grad_query), (w_key, grad_key), (w_value, grad_value))
    ) / gain_attn.astype(F32)
    grad_gain_ffn = jnp.sum(ffn_in.astype(F32) * grad_ffn_in, axis=1) / gain_ffn.astype(F32)
    bias_cols = jnp.where(2 * d < dp, qkv_first[:, 3 * half], qkv_last[:, 3 * half])
    grad_bias = bias_cols[:table_rows]
    return (
        layer_out,
        grad_input,
        grad_gain_attn,
        grad_query,
        grad_key,
        grad_value,
        grad_output,
        grad_bias,
        grad_gain_ffn,
        grad_ffn_in,
        grad_ffn_out,
    )


def solution(mesh):
    both = ("dp", "seq")
    return jax.shard_map(
        body,
        mesh=mesh,
        in_specs=(
            P("dp", "seq", None),
            P(both),
            P(both, None),
            P(both, None),
            P(both, None),
            P(both, None),
            P("dp"),
            P(both),
            P(both, None),
            P(both, None),
            P(),
            P("dp", "seq"),
            P("dp", "seq", None),
        ),
        out_specs=(
            P("dp", "seq", None),
            P("dp", "seq", None),
            P(both),
            P(both, None),
            P(both, None),
            P(both, None),
            P(both, None),
            P("dp"),
            P(both),
            P(both, None),
            P(both, None),
        ),
        check_vma=False,
    )
```

```python
import functools
import math

import jax
import jax.numpy as jnp
import numpy as np
from jax import lax
from jax.experimental import pallas as pl
from jax.experimental.pallas import tpu as pltpu
from jax.sharding import PartitionSpec as P

HEADS = 12
HEAD_DIM = 64
BUCKETS = 32
EPSILON = 1e-06
LANES = 128
BF = jnp.bfloat16
F32 = jnp.float32
GELU_A = math.sqrt(2.0 / math.pi)
GELU_B = 0.044715

ANY = pl.BlockSpec(memory_space=pl.ANY)
SMEM = pl.BlockSpec(memory_space=pltpu.SMEM)


def whole(shape):
    zeros = (0,) * len(shape)
    return pl.BlockSpec(shape, lambda *_: zeros)


def params(mib=16):
    return pltpu.CompilerParams(vmem_limit_bytes=mib * 1024 * 1024)


MICROS = {
    "qkv": 10, "attend": 25, "middle": 7, "hidden": 12, "grad_ffn_out": 9, "grad_ffn_in": 9, "ffn_back": 15, "ffn_out": 8,
    "middle_back": 7, "grad_output": 4, "attend_back": 35, "grad_qkv": 10, "input_grad": 8, "last": 5,
}


def cost(name):
    return pl.CostEstimate(flops=int(MICROS[name] * 1.15e9), bytes_accessed=0, transcendentals=0)


def nn(a, b):
    return lax.dot_general(a, b, (((1,), (0,)), ((), ())), preferred_element_type=F32)


def nt(a, b):
    return lax.dot_general(a, b, (((1,), (1,)), ((), ())), preferred_element_type=F32)


def tn(a, b):
    return lax.dot_general(a, b, (((0,), (0,)), ((), ())), preferred_element_type=F32)


def flip(x, axis, bit, count):
    return lax.ppermute(x, axis, [(i, i ^ bit) for i in range(count)])


def after(values, *others):
    return lax.optimization_barrier((values, others))[0]


def meet(values, *fields):
    held = [[getattr(owner, name) for name in names.split()] for owner, names in fields]
    values, held = lax.optimization_barrier((values, held))
    for (owner, names), got in zip(fields, held):
        for name, value in zip(names.split(), got):
            setattr(owner, name, value)
    return values


def bit_groups(dp):
    bits, groups = dp.bit_length() - 3, []
    at = 2
    while bits > 0:
        groups.append((1 << at, 1 << min(bits, 2)))
        at, bits = at + 2, bits - 2
    return groups


class Gather:
    def __init__(self, block, cut, dp):
        self.have, self.cut, self.dp = block[None], cut, dp

    def high(self):
        for bit, size in bit_groups(self.dp):
            got = [flip(self.have, "dp", bit * k, self.dp) for k in range(1, size)]
            self.have, self.got = jnp.concatenate([self.have] + got, axis=0), got

    def first(self):
        self.left, self.right = self.have[..., : self.cut], self.have[..., self.cut :]
        self.left_x = flip(self.left, "dp", 1, self.dp)
        self.right_y = flip(self.right, "dp", 2, self.dp)

    def second(self):
        self.left = jnp.concatenate([self.left, self.left_x], axis=0)
        self.right = jnp.concatenate([self.right, self.right_y], axis=0)
        self.left_far = flip(self.left, "dp", 2, self.dp)
        self.right_far = flip(self.right, "dp", 1, self.dp)

    def pieces(self):
        return [self.left, self.left_far], [self.right, self.right_far]


class Scatter:
    def __init__(self, parts, dp):
        self.left_send, self.left_keep, self.right_send, self.right_keep = parts
        self.dp, self.groups = dp, bit_groups(dp)

    @staticmethod
    def add(*terms):
        return sum(x.astype(F32) for x in terms).astype(BF)

    def first(self):
        self.left_got = flip(self.left_send, "dp", 2, self.dp)
        self.right_got = flip(self.right_send, "dp", 1, self.dp)

    def second(self):
        self.left = self.add(self.left_keep, self.left_got)
        self.right = self.add(self.right_keep, self.right_got)
        self.left_got = flip(self.left[1], "dp", 1, self.dp)
        self.right_got = flip(self.right[1], "dp", 2, self.dp)

    def join(self):
        left = self.add(self.left[0], self.left_got)
        right = self.add(self.right[0], self.right_got)
        self.have = jnp.concatenate([left, right], axis=-1)

    def send(self):
        bit, size = self.groups.pop()
        parts = self.have.reshape((size, -1) + self.have.shape[1:])
        self.keep = parts[0]
        self.got = [flip(parts[k], "dp", bit * k, self.dp) for k in range(1, size)]

    def take(self):
        self.have = self.add(self.keep, *self.got)

    def rest(self):
        while self.groups:
            self.send()
            self.take()
        return self.have[0]


def other_core(x):
    return lax.ppermute(x, "seq", [(0, 1), (1, 0)])


def start_blocks(refs, pos, side, rows, dst, cols, sems):
    copies = []
    at = 0
    for ref in refs:
        for b in range(ref.shape[0]):
            row = pl.multiple_of(pos[side, at] * rows, rows)
            src = ref.at[b] if cols is None else ref.at[b, :, pl.ds(*cols)]
            copies.append(pltpu.make_async_copy(src, dst.at[pl.ds(row, rows)], sems.at[at]))
            at += 1
    for copy in copies:
        copy.start()
    return copies


def qkv_kernel(meta, pos, x_own, x_oth, buckets, hsel, bsel, *rest, rows, cut, width, nl, nr):
    left, right = rest[:nl], rest[nl : nl + nr]
    q_ref, k_ref, v_ref, norm_ref, misc, peroff, w, sem_l, sem_r, wl, wr = rest[nl + nr :]
    s = meta[0]
    half = width // 2
    depth = w.shape[0]

    @pl.when(pl.program_id(0) == 0)
    def _():
        copies = start_blocks(left, pos, 0, rows, wl, None, sem_l)
        copies += start_blocks(right, pos, 1, rows, wr, None, sem_r)
        for copy in copies:
            copy.wait()
        w[:, :cut] = wl[...]
        w[:, cut:] = wr[...]
        extra = w[:, 3 * half :].astype(F32)
        misc[...] = extra.T[:8]
        spread = (extra[:, 2:3] * bsel[...]).astype(BF)
        table = nn(hsel[s].astype(BF), spread)
        one_hot = (
            lax.broadcasted_iota(jnp.int32, (LANES, buckets.shape[1]), 0) == buckets[...]
        ).astype(F32)
        peroff[...] = nn(table.astype(BF), one_hot.astype(BF))

    gain = misc[0:1, :]
    count = x_own.shape[1]
    for side, x_ref in ((0, x_own), (1, x_oth)):
        x = x_ref[0].astype(F32)
        scale = lax.rsqrt(jnp.mean(x * x, axis=-1, keepdims=True) + EPSILON)
        normed = (x * scale * gain).astype(BF)
        at = pl.ds(pl.multiple_of((s if side == 0 else 1 - s) * count, count), count)
        norm_ref[0, at, :] = normed
        q_ref[0, at, :] = nn(normed, w[:, :half]).astype(BF)
        k_ref[0, at, :] = nn(normed, w[:, half : 2 * half]).astype(BF)
        v_ref[0, at, :] = nn(normed, w[:, 2 * half : 3 * half]).astype(BF)


def lane_half(shape, which):
    lane = lax.broadcasted_iota(jnp.int32, shape, 1)
    return (lane < HEAD_DIM) if which == 0 else (lane >= HEAD_DIM)


def attend_kernel(meta, q_ref, k_ref, v_ref, mask_ref, peroff, own_ref, oth_ref, e_ref, inv_ref, grid, ctx, table):
    s = meta[0]
    hp = pl.program_id(0)
    length = q_ref.shape[1]
    step = LANES
    rows = step // 2
    span = grid.shape[-1]

    @pl.when(pl.program_id(1) == 0)
    def _():
        for hh in range(2):
            row = peroff[pl.ds(2 * hp + hh, 1), :]
            wide = jnp.broadcast_to(row, (step, span))
            grid[hh] = pltpu.roll(wide, span - step + 1, 1, stride=1, stride_axis=0)

    q, k, v, mask = q_ref[0], k_ref[0], v_ref[0], mask_ref[0]
    zero = jnp.zeros((), BF)
    one = jnp.ones((), BF)
    first = lane_half((length, LANES), 0)
    for hh in range(2):
        table[hh] = nt(jnp.where(first if hh == 0 else ~first, q, zero), k)
    sums = []
    for hh in range(2):
        for at in range(0, length, rows):
            base, within = length - step - at // step * step, at % step
            bias = grid[hh, within : within + rows, base : base + length]
            scores = table[hh, at : at + rows] + (bias + mask)
            top = jnp.max(scores, axis=-1, keepdims=True)
            e_ref[0, 0, hh, at : at + rows, :] = jnp.exp(scores - top).astype(BF)
        sums.append(nn(e_ref[0, 0, hh], jnp.where(first if hh == 0 else ~first, v, one)))
    num = jnp.where(first, sums[0], sums[1])
    den = pltpu.roll(jnp.where(first, sums[1], sums[0]), HEAD_DIM, 1)
    inv = 1.0 / den
    inv_ref[0] = inv
    ctx[...] = (num * inv).astype(BF)
    half = length // 2
    own_ref[0] = ctx[pl.ds(pl.multiple_of(s * half, half), half), :]
    oth_ref[0] = ctx[pl.ds(pl.multiple_of((1 - s) * half, half), half), :]


def middle_kernel(meta, pos, x_ref, own_ref, oth_ref, misc, *rest, rows, nb):
    own_w, oth_w = rest[:nb], rest[nb : 2 * nb]
    mid_ref, norm_ref, w, sem_a, sem_b = rest[2 * nb :]
    s = meta[0]
    half = w.shape[2]

    @pl.when(pl.program_id(0) == 0)
    def _():
        copies = start_blocks(own_w, pos, 0, rows, w.at[s], None, sem_a)
        copies += start_blocks(oth_w, pos, 0, rows, w.at[1 - s], None, sem_b)
        for copy in copies:
            copy.wait()

    x = x_ref[0].astype(F32)
    own, oth = own_ref[0], oth_ref[0]
    at_own = pl.ds(pl.multiple_of(s * half, half), half)
    at_oth = pl.ds(pl.multiple_of((1 - s) * half, half), half)
    parts = []
    for c in range(2):
        part = nn(own, w[c, at_own, :]) + nn(oth, w[c, at_oth, :])
        parts.append(x[:, c * half : (c + 1) * half] + part)
    middle = jnp.concatenate(parts, axis=-1)
    mid_ref[0] = middle
    scale = lax.rsqrt(jnp.mean(middle * middle, axis=-1, keepdims=True) + EPSILON)
    norm_ref[0] = (middle * scale * misc[1:2, :]).astype(BF)


def hidden_kernel(pos, own_ref, oth_ref, *rest, rows, cols, nl, nr):
    left, right = rest[:nl], rest[nl : nl + nr]
    act_ref, slope_ref, w, sem_l, sem_r, wl, wr = rest[nl + nr :]

    @pl.when(pl.program_id(0) == 0)
    def _():
        copies = start_blocks(left, pos, 0, rows, wl, cols, sem_l)
        copies += start_blocks(right, pos, 1, rows, wr, None, sem_r)
        for copy in copies:
            copy.wait()
        w[:, : wl.shape[1]] = wl[...]
        w[:, wl.shape[1] :] = wr[...]

    count = own_ref.shape[1]
    width = w.shape[1]
    step = 512 if width % 512 == 0 else width
    for side, ref in ((0, own_ref), (1, oth_ref)):
        for c in range(0, width, step):
            v = nn(ref[0], w[:, c : c + step])
            square = v * v
            t = jnp.tanh(v * (GELU_A + (GELU_A * GELU_B) * square))
            half_up = 0.5 + 0.5 * t
            slope = half_up + (0.5 * v) * (1.0 - t * t) * (GELU_A + (3.0 * GELU_A * GELU_B) * square)
            act_ref[0, side * count : (side + 1) * count, c : c + step] = (v * half_up).astype(BF)
            slope_ref[0, side * count : (side + 1) * count, c : c + step] = slope.astype(BF)


def wgrad_kernel(meta, *rest, na, nb, rows, cut, dp, cols):
    a_refs, b_refs = rest[:na], rest[na : na + nb]
    ls, lk, rs, rk, total = rest[na + nb :]
    mb = a_refs[0].shape[-1]
    i = pl.program_id(0)
    acc = None
    for a_ref, b_ref in zip(a_refs, b_refs):
        a = a_ref[...].reshape(-1, mb)
        b = b_ref[...].reshape(a.shape[0], -1)
        part = tn(a, b)
        acc = part if acc is None else acc + part
    total[pl.ds(pl.multiple_of(i * mb, mb), mb), :] = acc

    @pl.when(i == pl.num_programs(0) - 1)
    def _():
        store_relative(meta, total, ls, lk, rs, rk, rows, cut, dp)


def store_relative(meta, total, ls, lk, rs, rk, rows, cut, dp):
    d = meta[1]
    for rel in range(dp):
        x, y, high = rel & 1, (rel >> 1) & 1, rel >> 2
        at = pl.ds(pl.multiple_of((d ^ rel) * rows, rows), rows)
        (ls if y else lk)[x, high] = total[at, :cut].astype(BF)
        (rs if x else rk)[y, high] = total[at, cut:].astype(BF)


def ffn_back_kernel(pos, g_own, g_oth, slope_ref, w_in, *rest, rows, nl, nr):
    left, right = rest[:nl], rest[nl : nl + nr]
    pre_ref, own_ref, oth_ref, w, sem_l, sem_r, wl, wr = rest[nl + nr :]

    @pl.when(pl.program_id(0) == 0)
    def _():
        copies = start_blocks(left, pos, 0, rows, wl, None, sem_l)
        copies += start_blocks(right, pos, 1, rows, wr, None, sem_r)
        for copy in copies:
            copy.wait()
        w[:, : wl.shape[1]] = wl[...]
        w[:, wl.shape[1] :] = wr[...]

    count = g_own.shape[1]
    width = w.shape[0]
    step = 512 if width % 512 == 0 else width
    for side, ref in ((0, g_own), (1, g_oth)):
        g = ref[0]
        for c in range(0, width, step):
            grad = nt(g, w[c : c + step, :])
            slope = slope_ref[0, side * count : (side + 1) * count, c : c + step].astype(F32)
            pre_ref[0, side * count : (side + 1) * count, c : c + step] = (grad * slope).astype(BF)
        back = nt(pre_ref[0, side * count : (side + 1) * count, :], w_in[...])
        if side == 0:
            own_ref[0] = back
        else:
            oth_ref[0] = back.astype(BF)


def ffn_out_kernel(act_ref, w, own_ref, oth_ref):
    count = own_ref.shape[1]
    own_ref[0] = nn(act_ref[0, :count, :], w[...])
    oth_ref[0] = nn(act_ref[0, count:, :], w[...]).astype(BF)


def middle_back_kernel(meta, g_ref, mid_ref, own_ref, oth_ref, misc, w, gm_ref, low_ref, cown_ref, coth_ref):
    s = meta[0]
    half = w.shape[2]
    middle = mid_ref[0]
    scale = lax.rsqrt(jnp.mean(middle * middle, axis=-1, keepdims=True) + EPSILON)
    grad = own_ref[0] + oth_ref[0].astype(F32)
    scaled = grad * misc[1:2, :]
    inner = jnp.mean(scaled * middle, axis=-1, keepdims=True)
    grad_middle = g_ref[0].astype(F32) + scale * scaled - middle * (scale * scale * scale) * inner
    gm_ref[0] = grad_middle
    low = grad_middle.astype(BF)
    low_ref[0] = low
    for ref, which in ((cown_ref, s), (coth_ref, 1 - s)):
        at = pl.ds(pl.multiple_of(which * half, half), half)
        out = nt(low[:, :half], w[0, at, :]) + nt(low[:, half:], w[1, at, :])
        ref[0] = out.astype(BF)


def wo_grad_kernel(meta, own_ref, oth_ref, low_ref, keep_ref, send_ref, total, *, rows, dp):
    s, d = meta[0], meta[1]
    half = own_ref.shape[-1]
    low = low_ref[...].reshape(-1, low_ref.shape[-1])
    for ref, which in ((own_ref, s), (oth_ref, 1 - s)):
        at = pl.ds(pl.multiple_of(which * half, half), half)
        grad = tn(ref[...].reshape(low.shape[0], half), low)
        total[0, at, :] = grad[:, :half]
        total[1, at, :] = grad[:, half:]
    for rel in range(dp):
        at = pl.ds(pl.multiple_of((d ^ rel) * rows, rows), rows)
        keep_ref[rel] = total[s, at, :].astype(BF)
        send_ref[rel] = total[1 - s, at, :].astype(BF)


def attend_back_kernel(meta, q_ref, k_ref, v_ref, e_ref, inv_ref, own_ref, oth_ref, dq_ref, dk_ref, dv_ref, off_ref, diag, dctx, table, low):
    s = meta[0]
    length = q_ref.shape[1]
    half = length // 2
    step = LANES
    rows = step // 4
    n = pl.program_id(1)
    dctx[pl.ds(pl.multiple_of(s * half, half), half), :] = own_ref[0]
    dctx[pl.ds(pl.multiple_of((1 - s) * half, half), half), :] = oth_ref[0]

    @pl.when(n == 0)
    def _():
        diag[...] = jnp.zeros_like(diag)

    q, k, v, inv = q_ref[0], k_ref[0], v_ref[0], inv_ref[0]
    scaled = (dctx[...].astype(F32) * inv).astype(BF)
    zero = jnp.zeros((), BF)
    first = lane_half((length, LANES), 0)
    for hh in range(2):
        table[hh] = nt(jnp.where(first if hh == 0 else ~first, scaled, zero), v)
    q_t, c_t = q.astype(F32).T.astype(BF), scaled.astype(F32).T.astype(BF)
    dq, dk, dv = [], [], []
    for hh in range(2):
        lane = hh * HEAD_DIM
        for at in range(0, length, rows):
            base, within = length - step - at // step * step, at % step
            e = e_ref[0, 0, hh, at : at + rows, :].astype(F32)
            term = e * table[hh, at : at + rows]
            delta = jnp.sum(term, axis=-1, keepdims=True) * inv[at : at + rows, lane : lane + 1]
            grad = term - e * delta
            diag[hh, within : within + rows, base : base + length] += grad
            low[hh, at : at + rows] = grad.astype(BF)
        grad_low = low[hh]
        dq.append(nn(grad_low, jnp.where(first if hh == 0 else ~first, k, zero)))
        dk.append(nn(q_t[lane : lane + HEAD_DIM], grad_low))
        dv.append(nn(c_t[lane : lane + HEAD_DIM], e_ref[0, 0, hh]))
    dq_ref[0] = (dq[0] + dq[1]).astype(BF)
    dk_ref[0] = jnp.concatenate(dk, axis=0).T.astype(BF)
    dv_ref[0] = jnp.concatenate(dv, axis=0).T.astype(BF)

    @pl.when(n == pl.num_programs(1) - 1)
    def _():
        span = diag.shape[-1]
        for hh in range(2):
            acc = jnp.zeros((8, span), F32)
            for g in range(step // 8):
                rows = diag[hh, 8 * g : 8 * g + 8, :]
                shift = step - 8 - 8 * g
                acc = acc + (pltpu.roll(rows, shift, 1) if shift else rows)
            out = acc[7:8]
            for b in range(7):
                out = out + pltpu.roll(acc[b : b + 1], 7 - b, 1)
            off_ref[0, hh : hh + 1, :] = out


def qkv_grad_kernel(meta, norm_ref, dq_ref, dk_ref, dv_ref, off_ref, buckets, hsel, bsel, ls, lk, rs, rk, total, *, rows, cut, dp):
    s = meta[0]
    i = pl.program_id(0)
    mb = norm_ref.shape[-1]
    half = dq_ref.shape[-1]
    a = norm_ref[...].reshape(-1, mb)
    at = pl.ds(pl.multiple_of(i * mb, mb), mb)
    for c, ref in enumerate((dq_ref, dk_ref, dv_ref)):
        total[at, c * half : (c + 1) * half] = tn(a, ref[...].reshape(a.shape[0], half))

    @pl.when(i == pl.num_programs(0) - 1)
    def _():
        one_hot = (
            lax.broadcasted_iota(jnp.int32, (LANES, buckets.shape[1]), 0) == buckets[...]
        ).astype(F32)
        per_bucket = lax.dot_general(
            off_ref[...], one_hot, (((1,), (1,)), ((), ())), precision=lax.Precision.HIGHEST, preferred_element_type=F32
        )
        spread = lax.dot_general(
            hsel[s], per_bucket, (((0,), (0,)), ((), ())), precision=lax.Precision.HIGHEST, preferred_element_type=F32
        )
        column = jnp.sum(spread * bsel[...], axis=-1, keepdims=True)
        total[:, 3 * half :] = jnp.broadcast_to(column, (column.shape[0], LANES))
        store_relative(meta, total, ls, lk, rs, rk, rows, cut, dp)


def input_grad_kernel(meta, dq_ref, dk_ref, dv_ref, w, own_ref, oth_ref):
    s = meta[0]
    half = dq_ref.shape[-1]
    count = own_ref.shape[1]
    for side, ref in ((0, own_ref), (1, oth_ref)):
        at = pl.ds(pl.multiple_of((s if side == 0 else 1 - s) * count, count), count)
        out = nt(dq_ref[0, at, :], w[:, :half])
        out = out + nt(dk_ref[0, at, :], w[:, half : 2 * half])
        out = out + nt(dv_ref[0, at, :], w[:, 2 * half : 3 * half])
        ref[0] = out.astype(ref.dtype)


def last_kernel(x_ref, gm_ref, own_ref, oth_ref, misc, out_ref):
    x = x_ref[0].astype(F32)
    scale = lax.rsqrt(jnp.mean(x * x, axis=-1, keepdims=True) + EPSILON)
    scaled = (own_ref[0] + oth_ref[0].astype(F32)) * misc[0:1, :]
    inner = jnp.mean(scaled * x, axis=-1, keepdims=True)
    out_ref[0] = (gm_ref[0] + scale * scaled - x * (scale * scale * scale) * inner).astype(BF)


def body(
    layer_input,
    gain_attn,
    w_query,
    w_key,
    w_value,
    w_output,
    bias_table,
    gain_ffn,
    ffn_in,
    ffn_out,
    buckets,
    keep_mask,
    out_grad,
):
    dp = lax.axis_size("dp")
    s = lax.axis_index("seq")
    d = lax.axis_index("dp")
    nseq, count, width = layer_input.shape
    length = 2 * count
    span = 2 * length
    half = width // 2
    shard = w_query.shape[0]
    rows = 2 * shard
    hid_rows = ffn_out.shape[0]
    hid = hid_rows * dp
    table_rows = bias_table.shape[0]
    tok = nseq * length
    pairs = half // LANES
    meta = jnp.stack([s, d]).astype(jnp.int32)
    aligned = rows % 16 == 0 and hid_rows % 16 == 0

    def sds(shape, dtype=BF):
        return jax.ShapeDtypeStruct(shape, dtype)

    def far(shape, dtype=BF):
        return pltpu.HBM(shape, dtype)

    def first_columns(h):
        cut = [lax.dynamic_slice_in_dim(w, h * half, half, 1) for w in (w_query, w_key, w_value)]
        table = jnp.pad(bias_table, (0, shard - table_rows))
        extra = jnp.stack([gain_attn, gain_ffn, table], axis=1)
        extra = jnp.pad(extra, ((0, 0), (0, LANES - 3)))
        return jnp.concatenate(cut + [extra], axis=1)

    def second_columns(h):
        out_cols = lax.dynamic_slice_in_dim(w_output, h * half, half, 1)
        in_cols = lax.dynamic_index_in_dim(ffn_in.reshape(shard, dp, 2, hid_rows), h, 2, keepdims=False)
        return jnp.concatenate([out_cols, in_cols.reshape(shard, hid)], axis=1)

    def swapped(mine, theirs):
        theirs = other_core(theirs)
        return jnp.where(s == 0, jnp.concatenate([mine, theirs]), jnp.concatenate([theirs, mine]))

    first_cols = 3 * half + LANES
    second_cols = half + hid
    first_cut = (first_cols // LANES // 2) * LANES
    second_cut = (second_cols // LANES // 2) * LANES
    third_cut = (width // LANES // 2) * LANES

    first = Gather(swapped(first_columns(s), first_columns(1 - s)), first_cut, dp)
    first.high()
    x_oth = other_core(layer_input)
    second_block = swapped(second_columns(s), second_columns(1 - s))
    x_oth, second_block = meet((x_oth, second_block), (first, "have"))
    second = Gather(second_block, second_cut, dp)
    first.first()
    second.high()
    meet((), (first, "left right left_x right_y"))
    first.second()
    g_oth = other_core(out_grad)
    keep_oth = other_core(keep_mask.astype(BF))
    keep = keep_mask.astype(BF)
    keep = jnp.where(s == 0, jnp.concatenate([keep, keep_oth], 1), jnp.concatenate([keep_oth, keep], 1))
    mask = ((keep.astype(F32) - 1.0) * 1e9)[:, None, :]
    x_oth, ffn_out = meet((x_oth, ffn_out), (first, "left right left_far right_far"), (second, "have"))
    second.first()
    third = Gather(ffn_out, third_cut, dp)
    third.high()

    high = dp // 4
    orders = [np.array([(h << 2) | low for low in lows for h in range(high)], np.int32) for lows in ((0, 1, 2, 3), (0, 2, 1, 3))]
    pos_l, pos_r = ((d ^ jnp.asarray(order)).astype(jnp.int32) for order in orders)
    pos = pos_l

    def settle(pieces, places=pos_l):
        if aligned:
            return pieces
        every = jnp.concatenate(pieces, axis=0)
        order = jnp.argsort(places)
        return [every[order].reshape(1, -1, every.shape[-1])]

    def settle_both(gather):
        left, right = gather.pieces()
        return settle(left), settle(right, pos_r)

    if not aligned:
        pos_k, rows_k, hid_rows_k, nblk, dp_k = jnp.zeros((2, 1), jnp.int32), width, hid, 1, 1
    else:
        pos_k, rows_k, hid_rows_k, nblk, dp_k = jnp.stack([pos_l, pos_r]), rows, hid_rows, dp, dp

    feature = np.arange(width)
    chunk, within = feature // rows, feature % rows
    entry = np.where(within % shard < table_rows, table_rows * chunk + within % shard, -1)
    head, bucket = entry // BUCKETS, entry % BUCKETS
    half_heads = HEADS // 2
    hsel = np.zeros((2, 8, width), np.float32)
    bsel = np.zeros((width, LANES), np.float32)
    for f in range(width):
        if entry[f] >= 0:
            hsel[head[f] // half_heads, head[f] % half_heads, f] = 1.0
            bsel[f, bucket[f]] = 1.0
    bsel_once = jnp.asarray(np.where(within[:, None] < shard, bsel, 0.0))
    hsel, bsel = jnp.asarray(hsel), jnp.asarray(bsel)
    padded = jnp.concatenate([buckets, jnp.full((span - buckets.shape[0],), -1, jnp.int32)])[None]

    a_l, a_r = settle_both(first)

    seq_block = lambda shape: pl.BlockSpec((1,) + shape, lambda n: (n, 0, 0))
    q, k, v, normed_attn, misc, peroff, w_qkv = pl.pallas_call(
        functools.partial(
            qkv_kernel, rows=rows_k, cut=first_cut, width=width, nl=len(a_l), nr=len(a_r)
        ),
        grid=(nseq,),
        in_specs=[SMEM, SMEM, seq_block((count, width)), seq_block((count, width)), whole((1, span)), whole(hsel.shape), whole(bsel.shape)]
        + [ANY] * (len(a_l) + len(a_r)),
        out_specs=[seq_block((length, half))] * 3
        + [seq_block((length, width)), whole((8, width)), whole((8, span)), whole((width, first_cols))],
        out_shape=[sds((nseq, length, half))] * 3
        + [far((nseq, length, width)), sds((8, width), F32), sds((8, span), F32), far((width, first_cols))],
        scratch_shapes=[
            pltpu.SemaphoreType.DMA((nblk,)),
            pltpu.SemaphoreType.DMA((nblk,)),
            pltpu.VMEM((width, first_cut), BF),
            pltpu.VMEM((width, first_cols - first_cut), BF),
        ],
        compiler_params=params(),
        name="qkv",
        cost_estimate=cost("qkv"),
    )(meta, pos_k, layer_input, x_oth, padded, hsel, bsel_once, *a_l, *a_r)

    q, k, v = meet((q, k, v), (second, "left right left_x right_y"))
    second.second()
    pair = pl.BlockSpec((1, length, LANES), lambda h, n: (n, 0, h))
    pair_half = pl.BlockSpec((1, count, LANES), lambda h, n: (n, 0, h))
    e_block = pl.BlockSpec((1, 1, 2, length, length), lambda h, n: (n, h, 0, 0, 0))
    ctx_own, ctx_send, expo, inv = pl.pallas_call(
        attend_kernel,
        grid=(pairs, nseq),
        in_specs=[SMEM, pair, pair, pair, pl.BlockSpec((1, 1, length), lambda h, n: (n, 0, 0)), whole((8, span))],
        out_specs=[pair_half, pair_half, e_block, pair],
        out_shape=[
            sds((nseq, count, half)),
            sds((nseq, count, half)),
            far((nseq, pairs, 2, length, length)),
            far((nseq, length, half), F32),
        ],
        scratch_shapes=[
            pltpu.VMEM((2, LANES, span), F32),
            pltpu.VMEM((length, LANES), BF),
            pltpu.VMEM((2, length, length), F32),
        ],
        compiler_params=params(),
        name="attend",
        cost_estimate=cost("attend"),
    )(meta, q, k, v, mask, peroff)
    ctx_own, ctx_send = meet((ctx_own, ctx_send), (second, "left right left_far right_far"), (third, "have"))
    third.first()
    ctx_oth = other_core(ctx_send)

    wo_own = jnp.concatenate([x[..., :half] for x in second.pieces()[0]], axis=0)
    wo_oth = other_core(wo_own)
    wo_own, wo_oth = settle([wo_own]), settle([wo_oth])
    middle, normed_ffn, w_o = pl.pallas_call(
        functools.partial(middle_kernel, rows=rows_k, nb=1),
        grid=(nseq,),
        in_specs=[SMEM, SMEM, seq_block((count, width)), seq_block((count, half)), seq_block((count, half)), whole((8, width)), ANY, ANY],
        out_specs=[seq_block((count, width)), seq_block((count, width)), whole((2, width, half))],
        out_shape=[far((nseq, count, width), F32), sds((nseq, count, width)), far((2, width, half))],
        scratch_shapes=[pltpu.SemaphoreType.DMA((nblk,)), pltpu.SemaphoreType.DMA((nblk,))],
        compiler_params=params(),
        name="middle",
        cost_estimate=cost("middle"),
    )(meta, pos_k, layer_input, ctx_own, ctx_oth, misc, *wo_own, *wo_oth)
    middle, normed_ffn = meet((middle, normed_ffn), (third, "left right left_x right_y"))
    third.second()
    normed_oth = other_core(normed_ffn)

    b_l, b_r = settle_both(second)
    act, slope, w_in = pl.pallas_call(
        functools.partial(
            hidden_kernel, rows=rows_k, cols=(half, second_cut - half), nl=len(b_l), nr=len(b_r)
        ),
        grid=(nseq,),
        in_specs=[SMEM, seq_block((count, width)), seq_block((count, width))] + [ANY] * (len(b_l) + len(b_r)),
        out_specs=[seq_block((length, hid)), seq_block((length, hid)), whole((width, hid))],
        out_shape=[sds((nseq, length, hid)), sds((nseq, length, hid)), sds((width, hid))],
        scratch_shapes=[
            pltpu.SemaphoreType.DMA((nblk,)),
            pltpu.SemaphoreType.DMA((nblk,)),
            pltpu.VMEM((width, second_cut - half), BF),
            pltpu.VMEM((width, half + hid - second_cut), BF),
        ],
        compiler_params=params(),
        name="hidden",
        cost_estimate=cost("hidden"),
    )(pos_k, normed_ffn, normed_oth, *b_l, *b_r)

    def block_outs(block_rows, cut, cols):
        if aligned:
            left, right = (2, high, block_rows, cut), (2, high, block_rows, cols - cut)
            return [left, left, right, right]
        return [(dp * block_rows, cols)]

    def in_relative(parts, block_rows, cut):
        if aligned:
            return parts
        blocks = parts[0].reshape(dp, block_rows, -1)[pos].reshape(2, 2, high, block_rows, -1)
        left, right = blocks[..., :cut], blocks[..., cut:]
        return left[1], left[0], right[:, 1], right[:, 0]

    def whole_wgrad(meta, *rest, na, nb, **_):
        a_refs, b_refs = rest[:na], rest[na : na + nb]
        out = rest[na + nb]
        acc = None
        for a_ref, b_ref in zip(a_refs, b_refs):
            a = a_ref[...].reshape(-1, a_ref.shape[-1])
            part = tn(a, b_ref[...].reshape(a.shape[0], -1))
            acc = part if acc is None else acc + part
        out[...] = acc.astype(BF)

    def wgrad(a_list, b_list, block_rows, cut, name):
        m, cols = a_list[0].shape[-1], b_list[0].shape[-1]
        mb = 384
        shapes = block_outs(block_rows, cut, cols)
        kernel = wgrad_kernel if aligned else whole_wgrad
        out_specs = [whole(x) for x in shapes] if aligned else [pl.BlockSpec((mb, cols), lambda i: (i, 0))]
        return in_relative(
            pl.pallas_call(
                functools.partial(kernel, na=len(a_list), nb=len(b_list), rows=block_rows, cut=cut, dp=dp, cols=cols),
                grid=(m // mb,),
                in_specs=[SMEM]
                + [pl.BlockSpec(a.shape[:2] + (mb,), lambda i: (0, 0, i)) for a in a_list]
                + [whole(b.shape) for b in b_list],
                out_specs=out_specs,
                out_shape=[sds(x) for x in shapes],
                scratch_shapes=[pltpu.VMEM((m, cols), F32)] if aligned else [],
                compiler_params=params(),
                name=name,
                cost_estimate=cost(name),
            )(meta, *a_list, *b_list),
            block_rows,
            cut,
        )

    act_own, act_oth = act[:, :count], act[:, count:]
    grad_out_parts = wgrad([act_own, act_oth], [out_grad, g_oth], hid_rows, third_cut, "grad_ffn_out")
    grad_out_parts, slope, act = meet((grad_out_parts, slope, act), (third, "left right left_far right_far"))
    out_sum = Scatter(grad_out_parts, dp)
    out_sum.first()

    c_l, c_r = settle_both(third)
    grad_pre, back_own, back_send, w_out = pl.pallas_call(
        functools.partial(ffn_back_kernel, rows=hid_rows_k, nl=len(c_l), nr=len(c_r)),
        grid=(nseq,),
        in_specs=[SMEM, seq_block((count, width)), seq_block((count, width)), seq_block((length, hid)), whole((width, hid))]
        + [ANY] * (len(c_l) + len(c_r)),
        out_specs=[seq_block((length, hid)), seq_block((count, width)), seq_block((count, width)), whole((hid, width))],
        out_shape=[sds((nseq, length, hid)), sds((nseq, count, width), F32), sds((nseq, count, width)), far((hid, width))],
        scratch_shapes=[
            pltpu.SemaphoreType.DMA((nblk,)),
            pltpu.SemaphoreType.DMA((nblk,)),
            pltpu.VMEM((hid, third_cut), BF),
            pltpu.VMEM((hid, width - third_cut), BF),
        ],
        compiler_params=params(),
        name="ffn_back",
        cost_estimate=cost("ffn_back"),
    )(pos_k, out_grad, g_oth, slope, w_in, *c_l, *c_r)
    grad_pre, back_own, back_send = meet((grad_pre, back_own, back_send), (out_sum, "left_got right_got"))
    out_sum.second()
    back_oth = other_core(back_send)

    pre_own, pre_oth = grad_pre[:, :count], grad_pre[:, count:]
    in_cut = (hid // LANES // 2) * LANES
    grad_in_parts = wgrad([normed_ffn, normed_oth], [pre_own, pre_oth], rows, in_cut, "grad_ffn_in")
    grad_in_parts, back_own, back_oth = meet((grad_in_parts, back_own, back_oth), (out_sum, "left_got right_got"))
    out_sum.join()
    out_sum.send()

    grad_middle, middle_low, dctx_own, dctx_send = pl.pallas_call(
        middle_back_kernel,
        grid=(nseq,),
        in_specs=[SMEM] + [seq_block((count, width))] * 4 + [whole((8, width)), whole((2, width, half))],
        out_specs=[seq_block((count, width)), seq_block((count, width)), seq_block((count, half)), seq_block((count, half))],
        out_shape=[
            sds((nseq, count, width), F32),
            sds((nseq, count, width)),
            sds((nseq, count, half)),
            sds((nseq, count, half)),
        ],
        compiler_params=params(),
        name="middle_back",
        cost_estimate=cost("middle_back"),
    )(meta, out_grad, middle, back_own, back_oth, misc, w_o)
    dctx_oth = other_core(dctx_send)

    rel_meta = meta if aligned else jnp.stack([s, jnp.zeros_like(d)]).astype(jnp.int32)
    wo_keep, wo_send = pl.pallas_call(
        functools.partial(wo_grad_kernel, rows=rows_k, dp=dp_k),
        out_shape=[sds((dp_k, rows_k, half))] * 2,
        in_specs=[SMEM, whole(ctx_own.shape), whole(ctx_oth.shape), whole(middle_low.shape)],
        out_specs=[whole((dp_k, rows_k, half))] * 2,
        scratch_shapes=[pltpu.VMEM((2, width, half), F32)],
        grid=(1,),
        compiler_params=params(),
        name="grad_output",
        cost_estimate=cost("grad_output"),
    )(rel_meta, ctx_own, ctx_oth, middle_low)
    wo_sum = (wo_keep.astype(F32) + other_core(wo_send).astype(F32)).astype(BF)
    if not aligned:
        wo_sum = wo_sum.reshape(dp, rows, half)[d ^ jnp.arange(dp)]
    wo_cut = (half // LANES // 2) * LANES
    by_bits = wo_sum.reshape(high, 2, 2, rows, half)
    wo_left = jnp.swapaxes(by_bits[..., :wo_cut], 0, 2)
    wo_right = jnp.moveaxis(by_bits[..., wo_cut:], 0, 2)
    wo_parts = (wo_left[:, 1], wo_left[:, 0], wo_right[:, 1], wo_right[:, 0])
    wo_parts, dctx_own, dctx_oth, act = meet((wo_parts, dctx_own, dctx_oth, act))
    in_sum = Scatter([jnp.concatenate(pair, axis=-1) for pair in zip(grad_in_parts, wo_parts)], dp)
    in_sum.first()

    dq, dk, dv, off = pl.pallas_call(
        attend_back_kernel,
        grid=(pairs, nseq),
        in_specs=[SMEM, pair, pair, pair, e_block, pair, pair_half, pair_half],
        out_specs=[pair, pair, pair, pl.BlockSpec((1, 2, span), lambda h, n: (h, 0, 0))],
        out_shape=[sds((nseq, length, half))] * 3 + [sds((pairs, 2, span), F32)],
        scratch_shapes=[
            pltpu.VMEM((2, LANES, span), F32),
            pltpu.VMEM((length, LANES), BF),
            pltpu.VMEM((2, length, length), F32),
            pltpu.VMEM((2, length, length), BF),
        ],
        compiler_params=params(),
        name="attend_back",
        cost_estimate=cost("attend_back"),
    )(meta, q, k, v, expo, inv, dctx_own, dctx_oth)
    dq, dk, dv, off = meet(
        (dq, dk, dv, off), (out_sum, "got"), (in_sum, "left_got right_got")
    )
    out_sum.take()
    in_sum.second()
    off = jnp.pad(off.reshape(half_heads, span), ((0, 8 - half_heads), (0, 0)))
    out_block = out_sum.rest()

    mb = 384
    shapes = block_outs(rows, first_cut, first_cols)
    whole_shapes = shapes if aligned else [(width, first_cols)]

    def qkv_whole(meta, *rest):
        ins, out, total = rest[:8], rest[8], rest[9]
        qkv_grad_kernel(meta, *ins, None, None, None, None, total, rows=width, cut=first_cut, dp=0)
        out[...] = total[...].astype(BF)

    qkv_parts = in_relative(
        pl.pallas_call(
            functools.partial(qkv_grad_kernel, rows=rows, cut=first_cut, dp=dp) if aligned else qkv_whole,
            grid=(width // mb,),
            in_specs=[SMEM, pl.BlockSpec((nseq, length, mb), lambda i: (0, 0, i))]
            + [whole((nseq, length, half))] * 3
            + [whole((8, span)), whole((1, span)), whole(hsel.shape), whole(bsel.shape)],
            out_specs=[whole(x) for x in whole_shapes],
            out_shape=[sds(x) for x in whole_shapes],
            scratch_shapes=[pltpu.VMEM((width, first_cols), F32)],
            compiler_params=params(),
            name="grad_qkv",
        cost_estimate=cost("grad_qkv"),
        )(meta, normed_attn, dq, dk, dv, off, padded, hsel, bsel),
        rows,
        first_cut,
    )
    qkv_parts, dq, dk, dv = meet((qkv_parts, dq, dk, dv), (in_sum, "left_got right_got"))
    qkv_sum = Scatter(qkv_parts, dp)
    qkv_sum.first()
    in_sum.join()
    in_sum.send()

    out_own, out_send = pl.pallas_call(
        ffn_out_kernel,
        grid=(nseq,),
        in_specs=[seq_block((length, hid)), whole((hid, width))],
        out_specs=[seq_block((count, width)), seq_block((count, width))],
        out_shape=[sds((nseq, count, width), F32), sds((nseq, count, width))],
        compiler_params=params(),
        name="ffn_out",
        cost_estimate=cost("ffn_out"),
    )(act, w_out)
    layer_out = (middle + out_own + other_core(out_send).astype(F32)).astype(BF)

    dn_own, dn_send = pl.pallas_call(
        input_grad_kernel,
        grid=(nseq,),
        in_specs=[SMEM] + [seq_block((length, half))] * 3 + [whole((width, first_cols))],
        out_specs=[seq_block((count, width)), seq_block((count, width))],
        out_shape=[sds((nseq, count, width), F32), sds((nseq, count, width))],
        compiler_params=params(),
        name="input_grad",
        cost_estimate=cost("input_grad"),
    )(meta, dq, dk, dv, w_qkv)
    dn_own, dn_oth, layer_out = meet((dn_own, other_core(dn_send), layer_out), (qkv_sum, "left_got right_got"))
    qkv_sum.second()
    grad_input = pl.pallas_call(
        last_kernel,
        grid=(nseq,),
        in_specs=[seq_block((count, width))] * 4 + [whole((8, width))],
        out_specs=seq_block((count, width)),
        out_shape=sds((nseq, count, width)),
        compiler_params=params(),
        name="last",
        cost_estimate=cost("last"),
    )(layer_input, grad_middle, dn_own, dn_oth, misc)

    grad_input = meet(grad_input, (qkv_sum, "left_got right_got"), (in_sum, "got"))
    qkv_sum.join()
    in_sum.take()
    qkv_block, in_wo_block = qkv_sum.rest(), in_sum.rest()
    grad_ffn_out = out_block.astype(F32)

    def both_cores(block):
        mine = lax.dynamic_slice_in_dim(block, s * shard, shard, 0)
        theirs = other_core(lax.dynamic_slice_in_dim(block, (1 - s) * shard, shard, 0))
        first, last = jnp.where(s == 0, mine, theirs), jnp.where(s == 0, theirs, mine)
        return first.astype(F32), last.astype(F32)

    in_first, in_last = both_cores(in_wo_block)
    wo_first, wo_last = (
        jnp.concatenate([x[:, in_cut : in_cut + wo_cut], x[:, wo_cut + hid :]], axis=1) for x in (in_first, in_last)
    )
    in_first, in_last = (
        jnp.concatenate([x[:, :in_cut], x[:, in_cut + wo_cut : wo_cut + hid]], axis=1) for x in (in_first, in_last)
    )
    grad_ffn_in = jnp.stack(
        [in_first.reshape(shard, dp, hid_rows), in_last.reshape(shard, dp, hid_rows)], axis=2
    ).reshape(shard, 2 * hid)
    grad_output = jnp.concatenate([wo_first, wo_last], axis=1)
    qkv_first, qkv_last = both_cores(qkv_block)
    grad_query, grad_key, grad_value = (
        jnp.concatenate([x[:, c * half : (c + 1) * half] for x in (qkv_first, qkv_last)], axis=1)
        for c in range(3)
    )
    grad_gain_attn = sum(
        jnp.sum(w.astype(F32) * g, axis=1)
        for w, g in ((w_query, grad_query), (w_key, grad_key), (w_value, grad_value))
    ) / gain_attn.astype(F32)
    grad_gain_ffn = jnp.sum(ffn_in.astype(F32) * grad_ffn_in, axis=1) / gain_ffn.astype(F32)
    bias_cols = jnp.where(2 * d < dp, qkv_first[:, 3 * half], qkv_last[:, 3 * half])
    grad_bias = bias_cols[:table_rows]
    return (
        layer_out,
        grad_input,
        grad_gain_attn,
        grad_query,
        grad_key,
        grad_value,
        grad_output,
        grad_bias,
        grad_gain_ffn,
        grad_ffn_in,
        grad_ffn_out,
    )


def solution(mesh):
    both = ("dp", "seq")
    return jax.shard_map(
        body,
        mesh=mesh,
        in_specs=(
            P("dp", "seq", None),
            P(both),
            P(both, None),
            P(both, None),
            P(both, None),
            P(both, None),
            P("dp"),
            P(both),
            P(both, None),
            P(both, None),
            P(),
            P("dp", "seq"),
            P("dp", "seq", None),
        ),
        out_specs=(
            P("dp", "seq", None),
            P("dp", "seq", None),
            P(both),
            P(both, None),
            P(both, None),
            P(both, None),
            P(both, None),
            P("dp"),
            P(both),
            P(both, None),
            P(both, None),
        ),
        check_vma=False,
    )
```

```python
import functools
import math

import jax
import jax.numpy as jnp
import numpy as np
from jax import lax
from jax.experimental import pallas as pl
from jax.experimental.pallas import tpu as pltpu
from jax.sharding import PartitionSpec as P

HEADS = 12
HEAD_DIM = 64
BUCKETS = 32
EPSILON = 1e-06
LANES = 128
BF = jnp.bfloat16
F32 = jnp.float32
GELU_A = math.sqrt(2.0 / math.pi)
GELU_B = 0.044715

ANY = pl.BlockSpec(memory_space=pl.ANY)
SMEM = pl.BlockSpec(memory_space=pltpu.SMEM)
FAR = pl.BlockSpec(memory_space=pltpu.HBM)


def whole(shape):
    zeros = (0,) * len(shape)
    return pl.BlockSpec(shape, lambda *_: zeros)


def params(mib=6):
    return pltpu.CompilerParams(vmem_limit_bytes=mib * 1024 * 1024)


MICROS = {
    "qkv": 7, "attend": 10, "middle": 4, "hidden": 8, "grad_ffn_out": 5, "grad_ffn_in": 5, "ffn_back": 9, "ffn_out": 5,
    "middle_back": 4, "grad_output": 2, "attend_back": 14, "grad_qkv": 5, "input_grad": 5, "last": 3, "finish": 1,
}


def cost(name):
    return pl.CostEstimate(flops=int(MICROS[name] * 1e4), bytes_accessed=0, transcendentals=0)


def nn(a, b):
    return lax.dot_general(a, b, (((1,), (0,)), ((), ())), preferred_element_type=F32)


def nt(a, b):
    return lax.dot_general(a, b, (((1,), (1,)), ((), ())), preferred_element_type=F32)


def tn(a, b):
    return lax.dot_general(a, b, (((0,), (0,)), ((), ())), preferred_element_type=F32)


def flip(x, axis, bit, count):
    return lax.ppermute(x, axis, [(i, i ^ bit) for i in range(count)])


def after(values, *others):
    return lax.optimization_barrier((values, others))[0]


def meet(values, *fields):
    held = [[getattr(owner, name) for name in names.split()] for owner, names in fields]
    values, held = lax.optimization_barrier((values, held))
    for (owner, names), got in zip(fields, held):
        for name, value in zip(names.split(), got):
            setattr(owner, name, value)
    return values


def bit_groups(dp):
    bits, groups = dp.bit_length() - 3, []
    at = 2
    while bits > 0:
        groups.append((1 << at, 1 << min(bits, 2)))
        at, bits = at + 2, bits - 2
    return groups


def small(kernel, inputs, shapes, name, dtype=BF):
    return pl.pallas_call(
        kernel,
        in_specs=[SMEM if x.ndim == 1 else pl.BlockSpec(memory_space=pltpu.VMEM) for x in inputs],
        out_specs=[pl.BlockSpec(memory_space=pltpu.VMEM)] * len(shapes),
        out_shape=[jax.ShapeDtypeStruct(x, dtype) for x in shapes],
        compiler_params=params(),
        name=name,
        cost_estimate=pl.CostEstimate(flops=10**4, bytes_accessed=0, transcendentals=0),
    )(*inputs)


def total_of(refs, at, dtype=BF):
    return functools.reduce(lambda x, y: x + y, (ref[at].astype(F32) for ref in refs)).astype(dtype)


def merge(sides, size, joined, name, dtype=BF):
    counts = [len(side) for side in sides]
    k, rows, _ = sides[0][0].shape
    widths = [side[0].shape[2] for side in sides]
    part = k // size
    shapes = [(part, rows, sum(widths))] * size if joined else [(part, rows, w) for w in widths for _ in range(size)]

    def kernel(*refs):
        ins, outs = refs[: sum(counts)], refs[sum(counts) :]
        at, lane = 0, 0
        for i, (count, width) in enumerate(zip(counts, widths)):
            for j in range(k):
                out = outs[j // part] if joined else outs[i * size + j // part]
                out[j % part, :, lane : lane + width] = total_of(ins[at : at + count], j, dtype)
            at += count
            lane = lane + width if joined else 0

    return small(kernel, [x for side in sides for x in side], shapes, name, dtype)


def stack(pieces, cut, name):
    ks = [x.shape[0] for x in pieces]
    rows, cols = pieces[0].shape[1:]

    def kernel(*refs):
        left, right = refs[len(ks) :]
        at = 0
        for ref, k in zip(refs, ks):
            left[at : at + k] = ref[:, :, :cut]
            right[at : at + k] = ref[:, :, cut:]
            at += k

    return small(kernel, pieces, [(sum(ks), rows, cut), (sum(ks), rows, cols - cut)], name)


def pair_up(a, b, c, d, name):
    k = a.shape[0]

    def kernel(a_ref, b_ref, c_ref, d_ref, ab, cd):
        ab[:k], ab[k:] = a_ref[...], b_ref[...]
        cd[:k], cd[k:] = c_ref[...], d_ref[...]

    return small(kernel, (a, b, c, d), [(2 * k,) + a.shape[1:], (2 * k,) + c.shape[1:]], name)


def with_output_columns(parts, keep, got, cut):
    count, _, half = keep.shape
    widths = [x.shape[-1] for x in parts]
    extra = (cut, cut, half - cut, half - cut)
    shapes = [x.shape[:-1] + (w + more,) for x, w, more in zip(parts, widths, extra)]

    def kernel(*refs):
        ins, keep_ref, got_ref, outs = refs[:4], refs[4], refs[5], refs[6:]
        for ref, out, w in zip(ins, outs, widths):
            out[..., :w] = ref[...]
        for rel in range(count):
            x, y, high = rel & 1, (rel >> 1) & 1, rel >> 2
            block = total_of((keep_ref, got_ref), rel)
            i = 0 if y else 1
            outs[i][x, high, :, widths[i] :] = block[:, :cut]
            i = 2 if x else 3
            outs[i][y, high, :, widths[i] :] = block[:, cut:]

    return small(kernel, (*parts, keep, got), shapes, "output_parts")


class Gather:
    def __init__(self, block, cut, dp):
        self.have, self.cut, self.dp = block[None], cut, dp
        self.near = None

    def begin(self):
        self.near = flip(self.have, "dp", 4, self.dp)

    def high(self):
        self.got = []
        groups = bit_groups(self.dp)
        for i, (bit, size) in enumerate(groups):
            first = [self.near] if bit == 4 and self.near is not None else [flip(self.have, "dp", bit, self.dp)]
            self.got = first + [flip(self.have, "dp", bit * k, self.dp) for k in range(2, size)]
            if i + 1 < len(groups):
                self.have = jnp.concatenate([self.have] + self.got, axis=0)

    def first(self):
        self.left, self.right = stack([self.have] + self.got, self.cut, "stack")
        self.left_x = flip(self.left, "dp", 1, self.dp)
        self.right_y = flip(self.right, "dp", 2, self.dp)

    def second(self):
        self.left, self.right = pair_up(self.left, self.left_x, self.right, self.right_y, "pair_up")
        self.left_far = flip(self.left, "dp", 2, self.dp)
        self.right_far = flip(self.right, "dp", 1, self.dp)

    def pieces(self):
        return [self.left, self.left_far], [self.right, self.right_far]


class Scatter:
    def __init__(self, parts, dp):
        flat = [x.reshape((-1,) + x.shape[2:]) for x in parts]
        self.left_send, self.left_keep, self.right_send, self.right_keep = flat
        self.dp, self.groups = dp, bit_groups(dp)

    def first(self):
        self.left_got = flip(self.left_send, "dp", 2, self.dp)
        self.right_got = flip(self.right_send, "dp", 1, self.dp)

    def second(self):
        self.left, self.left_send, self.right, self.right_send = merge(
            [[self.left_keep, self.left_got], [self.right_keep, self.right_got]], 2, False, "add_second"
        )
        self.left_got = flip(self.left_send, "dp", 1, self.dp)
        self.right_got = flip(self.right_send, "dp", 2, self.dp)

    def spread(self, sides):
        bit, size = self.groups.pop()
        self.keep, *parts = merge(sides, size, True, "add_high")
        self.got = [flip(x, "dp", bit * (k + 1), self.dp) for k, x in enumerate(parts)]

    def high(self):
        self.spread([[self.left, self.left_got], [self.right, self.right_got]])

    def rest(self, dtype=BF):
        while self.groups:
            self.spread([[self.keep] + self.got])
        return merge([[self.keep] + self.got], 1, True, "add_last", dtype)[0][0]


def other_core(x):
    return lax.ppermute(x, "seq", [(0, 1), (1, 0)])


def place(refs, pos, side, rows, dst, lane, skip=0):
    at = 0
    for ref in refs:
        cols = ref.shape[2] - skip
        for b in range(ref.shape[0]):
            row = pl.multiple_of(pos[side, at] * rows, rows)
            dst[pl.ds(row, rows), lane : lane + cols] = ref[b, :, skip:]
            at += 1


def first_kernel(meta, wq, wk, wv, extra, mine, theirs, held, sems):
    s = meta[0]
    half = wq.shape[1] // 2
    copies = [pltpu.make_async_copy(ref, held.at[c], sems.at[c]) for c, ref in enumerate((wq, wk, wv))]
    for copy in copies:
        copy.start()
    for copy in copies:
        copy.wait()
    for c in range(3):
        low, top = held[c, :, :half], held[c, :, half:]
        mine[:, c * half : (c + 1) * half] = jnp.where(s == 0, low, top)
        theirs[:, c * half : (c + 1) * half] = jnp.where(s == 0, top, low)
    mine[:, 3 * half :] = extra[...]
    theirs[:, 3 * half :] = extra[...]


def qkv_kernel(meta, pos, x_own, x_oth, buckets, hsel, bsel, *rest, rows, cut, width, nl, nr):
    left, right = rest[:nl], rest[nl : nl + nr]
    q_ref, k_ref, v_ref, norm_ref, misc, peroff, w_far, w, sem = rest[nl + nr :]
    s = meta[0]
    half = width // 2
    n = pl.program_id(0)
    copy = pltpu.make_async_copy(w, w_far, sem)

    @pl.when(n == 0)
    def _():
        place(left, pos, 0, rows, w, 0)
        place(right, pos, 1, rows, w, cut)
        copy.start()
        extra = w[:, 3 * half :].astype(F32)
        misc[...] = extra.T[:8]
        spread = (extra[:, 2:3] * bsel[...]).astype(BF)
        table = nn(hsel[s].astype(BF), spread)
        one_hot = (
            lax.broadcasted_iota(jnp.int32, (LANES, buckets.shape[1]), 0) == buckets[...]
        ).astype(F32)
        peroff[...] = nn(table.astype(BF), one_hot.astype(BF))

    gain = misc[0:1, :]
    count = x_own.shape[1]
    for side, x_ref in ((0, x_own), (1, x_oth)):
        x = x_ref[0].astype(F32)
        scale = lax.rsqrt(jnp.mean(x * x, axis=-1, keepdims=True) + EPSILON)
        normed = (x * scale * gain).astype(BF)
        at = pl.ds(pl.multiple_of((s if side == 0 else 1 - s) * count, count), count)
        norm_ref[0, at, :] = normed
        q_ref[0, at, :] = nn(normed, w[:, :half]).astype(BF)
        k_ref[0, at, :] = nn(normed, w[:, half : 2 * half]).astype(BF)
        v_ref[0, at, :] = nn(normed, w[:, 2 * half : 3 * half]).astype(BF)

    @pl.when(n == pl.num_programs(0) - 1)
    def _():
        copy.wait()


def lane_half(shape, which):
    lane = lax.broadcasted_iota(jnp.int32, shape, 1)
    return (lane < HEAD_DIM) if which == 0 else (lane >= HEAD_DIM)


def attend_kernel(meta, q_ref, k_ref, v_ref, mask_ref, peroff, own_ref, oth_ref, e_far, inv_far, grid, ctx, table, e_buf, inv_buf, sems, inv_sems):
    s = meta[0]
    nseq, length, width = q_ref.shape
    step = LANES
    rows = step // 2
    half = length // 2
    span = grid.shape[-1]
    zero, one = jnp.zeros((), BF), jnp.ones((), BF)
    first = lane_half((length, LANES), 0)
    heads = width // HEAD_DIM
    for h in range(heads):
        wide = jnp.broadcast_to(peroff[h : h + 1, :], (step, span))
        grid[h] = pltpu.roll(wide, span - step + 1, 1, stride=1, stride_axis=0)
    items = [(hp, n, hh) for hp in range(heads // 2) for n in range(nseq) for hh in range(2)]

    def product(i):
        hp, n, hh = items[i]
        lanes = slice(hp * LANES, (hp + 1) * LANES)
        head = jnp.where(first if hh == 0 else ~first, q_ref[n, :, lanes], zero)
        table[i % 2] = nt(head, k_ref[n, :, lanes])

    def stores(i):
        hp, n, _ = items[2 * i]
        inv_dst = inv_far.at[n, :, pl.ds(hp * LANES, LANES)]
        return (
            pltpu.make_async_copy(e_buf.at[i % 3], e_far.at[n, hp], sems.at[i % 3]),
            pltpu.make_async_copy(inv_buf.at[i % 3], inv_dst, inv_sems.at[i % 3]),
        )

    product(0)
    sums = [None, None]
    for i, (hp, n, hh) in enumerate(items):
        lanes = slice(hp * LANES, (hp + 1) * LANES)
        e_ref = e_buf.at[i // 2 % 3]
        if i + 1 < len(items):
            product(i + 1)
        if hh == 0 and i >= 6:
            for copy in stores(i // 2 - 3):
                copy.wait()
        for at in range(0, length, rows):
            base, within = length - step - at // step * step, at % step
            bias = grid[2 * hp + hh, within : within + rows, base : base + length]
            scores = table[i % 2, at : at + rows] + (bias + mask_ref[n])
            top = jnp.max(scores, axis=-1, keepdims=True)
            e_ref[hh, at : at + rows, :] = jnp.exp(scores - top).astype(BF)
        sums[hh] = nn(e_ref[hh], jnp.where(first if hh == 0 else ~first, v_ref[n, :, lanes], one))
        if hh == 1:
            num = jnp.where(first, sums[0], sums[1])
            den = pltpu.roll(jnp.where(first, sums[1], sums[0]), HEAD_DIM, 1)
            inv = 1.0 / den
            inv_buf[i // 2 % 3] = inv
            for copy in stores(i // 2):
                copy.start()
            ctx[...] = (num * inv).astype(BF)
            own_ref[n, :, lanes] = ctx[pl.ds(pl.multiple_of(s * half, half), half), :]
            oth_ref[n, :, lanes] = ctx[pl.ds(pl.multiple_of((1 - s) * half, half), half), :]
    for i in range(max(0, len(items) // 2 - 3), len(items) // 2):
        for copy in stores(i):
            copy.wait()


def middle_kernel(meta, pos, x_ref, own_ref, oth_ref, misc, own_w, oth_w, mid_far, norm_ref, w_far, w, mid, sem, mid_sems, *, rows):
    s = meta[0]
    half = w.shape[2]
    place([own_w], pos, 0, rows, w.at[s], 0)
    place([oth_w], pos, 0, rows, w.at[1 - s], 0)
    copy = pltpu.make_async_copy(w, w_far, sem)
    copy.start()
    at_own = pl.ds(pl.multiple_of(s * half, half), half)
    at_oth = pl.ds(pl.multiple_of((1 - s) * half, half), half)
    for n in range(x_ref.shape[0]):
        x = x_ref[n].astype(F32)
        parts = []
        for c in range(2):
            part = nn(own_ref[n], w[c, at_own, :]) + nn(oth_ref[n], w[c, at_oth, :])
            parts.append(x[:, c * half : (c + 1) * half] + part)
        middle = jnp.concatenate(parts, axis=-1)
        mid[n] = middle
        pltpu.make_async_copy(mid.at[n], mid_far.at[n], mid_sems.at[n]).start()
        scale = lax.rsqrt(jnp.mean(middle * middle, axis=-1, keepdims=True) + EPSILON)
        norm_ref[n] = (middle * scale * misc[1:2, :]).astype(BF)
    copy.wait()
    for n in range(x_ref.shape[0]):
        pltpu.make_async_copy(mid.at[n], mid_far.at[n], mid_sems.at[n]).wait()


def hidden_kernel(pos, own_ref, oth_ref, *rest, rows, skip, cut, nl, nr):
    left, right = rest[:nl], rest[nl : nl + nr]
    act_ref, slope_ref, w = rest[nl + nr :]

    @pl.when(pl.program_id(0) == 0)
    def _():
        place(left, pos, 0, rows, w, 0, skip)
        place(right, pos, 1, rows, w, cut - skip)

    count = own_ref.shape[1]
    width = w.shape[1]
    step = 768
    for side, ref in ((0, own_ref), (1, oth_ref)):
        at = slice(side * count, (side + 1) * count)
        for c in range(0, width, step):
            v = nn(ref[0], w[:, c : c + step])
            square = v * v
            p = 0.5 + 0.5 * jnp.tanh(v * (GELU_A + (GELU_A * GELU_B) * square))
            act = v * p
            slope = p + act * ((1.0 - p) * (2.0 * GELU_A + (6.0 * GELU_A * GELU_B) * square))
            act_ref[0, at, c : c + step] = act.astype(BF)
            slope_ref[0, at, c : c + step] = slope.astype(BF)


def wgrad_kernel(meta, *rest, rows, cut, dp, na=1):
    a_refs, b_ref, rest = rest[:na], rest[na], rest[na + 1 :]
    grad, at = 0.0, 0
    for a_ref in a_refs:
        a = a_ref[...].reshape(-1, a_ref.shape[-1])
        b = b_ref[:, at : at + a_ref.shape[1], :].reshape(a.shape[0], -1)
        grad, at = grad + tn(a, b), at + a_ref.shape[1]
    if dp == 0:
        rest[0][...] = grad.astype(BF)
    else:
        rest[-1][...] = grad.astype(BF)
        store_relative(meta, rest[-1], *rest[:4], rows, cut, dp)


def store_relative(meta, total, ls, lk, rs, rk, rows, cut, dp):
    d = meta[1]
    for rel in range(dp):
        x, y, high = rel & 1, (rel >> 1) & 1, rel >> 2
        at = pl.ds(pl.multiple_of((d ^ rel) * rows, rows), rows)
        (ls if y else lk)[x, high] = total[at, :cut]
        (rs if x else rk)[y, high] = total[at, cut:]


def ffn_back_kernel(pos, g_ref, act_ref, slope_ref, w_in, *rest, rows, cut, nl, nr):
    left, right = rest[:nl], rest[nl : nl + nr]
    pre_ref, own_ref, oth_ref, out_own, out_oth, w = rest[nl + nr :]

    @pl.when(pl.program_id(0) == 0)
    def _():
        place(left, pos, 0, rows, w, 0)
        place(right, pos, 1, rows, w, cut)

    count = own_ref.shape[1]
    width = w.shape[0]
    step = 512
    for c in range(0, width, step):
        grad = nt(g_ref[0], w[c : c + step, :])
        pre_ref[0, :, c : c + step] = (grad * slope_ref[0, :, c : c + step].astype(F32)).astype(BF)
    oth_ref[0] = nt(pre_ref[0, count:, :], w_in[...]).astype(BF)
    own_ref[0] = nt(pre_ref[0, :count, :], w_in[...])
    out_own[0] = nn(act_ref[0, :count, :], w[...])
    out_oth[0] = nn(act_ref[0, count:, :], w[...]).astype(BF)


def middle_back_kernel(meta, g_ref, mid_ref, own_ref, oth_ref, misc, w, gm_ref, low_ref, cown_ref, coth_ref):
    s = meta[0]
    half = w.shape[2]
    middle = mid_ref[0]
    scale = lax.rsqrt(jnp.mean(middle * middle, axis=-1, keepdims=True) + EPSILON)
    grad = own_ref[0] + oth_ref[0].astype(F32)
    scaled = grad * misc[1:2, :]
    inner = jnp.mean(scaled * middle, axis=-1, keepdims=True)
    grad_middle = g_ref[0].astype(F32) + scale * scaled - middle * (scale * scale * scale) * inner
    gm_ref[0] = grad_middle
    low = grad_middle.astype(BF)
    low_ref[0] = low
    for ref, which in ((cown_ref, s), (coth_ref, 1 - s)):
        at = pl.ds(pl.multiple_of(which * half, half), half)
        out = nt(low[:, :half], w[0, at, :]) + nt(low[:, half:], w[1, at, :])
        ref[0] = out.astype(BF)


def wo_grad_kernel(meta, own_ref, oth_ref, low_ref, keep_ref, send_ref, total, *, rows, dp):
    s, d = meta[0], meta[1]
    half = own_ref.shape[-1]
    low = low_ref[...].reshape(-1, low_ref.shape[-1])
    for ref, which in ((own_ref, s), (oth_ref, 1 - s)):
        at = pl.ds(pl.multiple_of(which * half, half), half)
        grad = tn(ref[...].reshape(low.shape[0], half), low)
        total[0, at, :] = grad[:, :half]
        total[1, at, :] = grad[:, half:]
    for rel in range(dp):
        at = pl.ds(pl.multiple_of((d ^ rel) * rows, rows), rows)
        keep_ref[rel] = total[s, at, :].astype(BF)
        send_ref[rel] = total[1 - s, at, :].astype(BF)


def attend_back_kernel(meta, q_ref, k_ref, v_ref, e_ref, inv_ref, own_ref, oth_ref, dq_ref, dk_ref, dv_ref, off_ref, diag, dctx, table, low):
    s = meta[0]
    nseq, length, width = q_ref.shape
    half = length // 2
    step = LANES
    rows = step // 4
    span = diag.shape[-1]
    zero = jnp.zeros((), BF)
    first = lane_half((length, LANES), 0)
    for hp in range(width // LANES):
        lanes = slice(hp * LANES, (hp + 1) * LANES)
        diag[...] = jnp.zeros_like(diag)
        for n in range(nseq):
            q, k, v, inv = (ref[n, :, lanes] for ref in (q_ref, k_ref, v_ref, inv_ref))
            dctx[pl.ds(pl.multiple_of(s * half, half), half), :] = own_ref[n, :, lanes]
            dctx[pl.ds(pl.multiple_of((1 - s) * half, half), half), :] = oth_ref[n, :, lanes]
            scaled = (dctx[...].astype(F32) * inv).astype(BF)
            for hh in range(2):
                table[hh] = nt(jnp.where(first if hh == 0 else ~first, scaled, zero), v)
            q_t, c_t = q.astype(F32).T.astype(BF), scaled.astype(F32).T.astype(BF)
            dq, dk, dv = [], [], []
            for hh in range(2):
                lane = hh * HEAD_DIM
                for at in range(0, length, rows):
                    base, within = length - step - at // step * step, at % step
                    e = e_ref[n, hp, hh, at : at + rows, :].astype(F32)
                    term = e * table[hh, at : at + rows]
                    delta = jnp.sum(term, axis=-1, keepdims=True) * inv[at : at + rows, lane : lane + 1]
                    grad = term - e * delta
                    diag[hh, within : within + rows, base : base + length] += grad
                    low[hh, at : at + rows] = grad.astype(BF)
                grad_low = low[hh]
                dq.append(nn(grad_low, jnp.where(first if hh == 0 else ~first, k, zero)))
                dk.append(nn(q_t[lane : lane + HEAD_DIM], grad_low))
                dv.append(nn(c_t[lane : lane + HEAD_DIM], e_ref[n, hp, hh]))
            dq_ref[n, :, lanes] = (dq[0] + dq[1]).astype(BF)
            dk_ref[n, :, lanes] = jnp.concatenate(dk, axis=0).T.astype(BF)
            dv_ref[n, :, lanes] = jnp.concatenate(dv, axis=0).T.astype(BF)
        for hh in range(2):
            acc = jnp.zeros((8, span), F32)
            for g in range(step // 8):
                part = diag[hh, 8 * g : 8 * g + 8, :]
                shift = step - 8 - 8 * g
                acc = acc + (pltpu.roll(part, shift, 1) if shift else part)
            out = acc[7:8]
            for b in range(7):
                out = out + pltpu.roll(acc[b : b + 1], 7 - b, 1)
            off_ref[2 * hp + hh : 2 * hp + hh + 1, :] = out
    off_ref[width // HEAD_DIM :, :] = jnp.zeros((off_ref.shape[0] - width // HEAD_DIM, span), F32)


def qkv_grad_kernel(meta, norm_ref, dq_ref, dk_ref, dv_ref, off_ref, buckets, hsel, bsel, *rest, rows, cut, dp):
    s = meta[0]
    half = dq_ref.shape[-1]
    a = norm_ref[...].reshape(-1, norm_ref.shape[-1])
    total = rest[0] if dp == 0 else rest[-1]
    for c, ref in enumerate((dq_ref, dk_ref, dv_ref)):
        total[:, c * half : (c + 1) * half] = tn(a, ref[...].reshape(a.shape[0], half)).astype(BF)
    one_hot = (
        lax.broadcasted_iota(jnp.int32, (LANES, buckets.shape[1]), 0) == buckets[...]
    ).astype(F32)
    per_bucket = lax.dot_general(
        off_ref[...], one_hot, (((1,), (1,)), ((), ())), precision=lax.Precision.HIGHEST, preferred_element_type=F32
    )
    spread = lax.dot_general(
        hsel[s], per_bucket, (((0,), (0,)), ((), ())), precision=lax.Precision.HIGHEST, preferred_element_type=F32
    )
    column = jnp.sum(spread * bsel[...], axis=-1, keepdims=True)
    total[:, 3 * half :] = jnp.broadcast_to(column, (column.shape[0], LANES)).astype(BF)
    if dp:
        store_relative(meta, total, *rest[:4], rows, cut, dp)


def input_grad_kernel(meta, dq_ref, dk_ref, dv_ref, w, own_ref, oth_ref):
    s = meta[0]
    half = dq_ref.shape[-1]
    count = own_ref.shape[1]
    for side, ref in ((0, own_ref), (1, oth_ref)):
        at = pl.ds(pl.multiple_of((s if side == 0 else 1 - s) * count, count), count)
        out = nt(dq_ref[0, at, :], w[:, :half])
        out = out + nt(dk_ref[0, at, :], w[:, half : 2 * half])
        out = out + nt(dv_ref[0, at, :], w[:, 2 * half : 3 * half])
        ref[0] = out.astype(ref.dtype)


def last_kernel(x_ref, gm_ref, own_ref, oth_ref, mid_ref, top_ref, top_oth_ref, misc, out_ref, top_out):
    top_out[0] = (mid_ref[0] + top_ref[0] + top_oth_ref[0].astype(F32)).astype(BF)
    x = x_ref[0].astype(F32)
    scale = lax.rsqrt(jnp.mean(x * x, axis=-1, keepdims=True) + EPSILON)
    scaled = (own_ref[0] + oth_ref[0].astype(F32)) * misc[0:1, :]
    inner = jnp.mean(scaled * x, axis=-1, keepdims=True)
    out_ref[0] = (gm_ref[0] + scale * scaled - x * (scale * scale * scale) * inner).astype(BF)


def finish_kernel(meta, mine_ref, oth_ref, wq_ref, wk_ref, wv_ref, gain_ref, gq_ref, gk_ref, gv_ref, gain_out, bias_out, square, *, dp, table_rows):
    s, d = meta[0], meta[1]
    shard = mine_ref.shape[0]
    width = wq_ref.shape[1]
    half = width // 2
    mine, oth = mine_ref[...].astype(F32), oth_ref[...].astype(F32)
    low, top = jnp.where(s == 0, mine, oth), jnp.where(s == 0, oth, mine)
    total = jnp.zeros((shard, 1), F32)
    for c, (w_ref, out) in enumerate(((wq_ref, gq_ref), (wk_ref, gk_ref), (wv_ref, gv_ref))):
        grad = jnp.concatenate([x[:, c * half : (c + 1) * half] for x in (low, top)], axis=1)
        out[...] = grad
        total = total + jnp.sum(w_ref[...].astype(F32) * grad, axis=1, keepdims=True)
    lane = lax.broadcasted_iota(jnp.int32, (shard, LANES), 1)
    bias = jnp.where(2 * d < dp, low[:, 3 * half :], top[:, 3 * half :])
    square[...] = jnp.zeros_like(square)
    square[:shard, :] = jnp.where(lane == 0, total, bias)
    turned = square[...].T
    gain_out[...] = turned[0:1, :shard] / gain_ref[...].astype(F32)
    bias_out[...] = turned[1:2, :table_rows]


def finish_in_kernel(meta, mine_ref, oth_ref, w_ref, gain_ref, in_ref, out_ref, gain_out, square, *, in_cut, wo_cut, hid_rows, dp):
    s = meta[0]
    shard = mine_ref.shape[0]
    hid = hid_rows * dp
    mine, oth = mine_ref[...].astype(F32), oth_ref[...].astype(F32)
    halves = jnp.where(s == 0, mine, oth), jnp.where(s == 0, oth, mine)
    for c in range(dp):
        at = c * hid_rows
        at = at if at < in_cut else at + wo_cut
        for core, half in enumerate(halves):
            to = (2 * c + core) * hid_rows
            in_ref[:, to : to + hid_rows] = half[:, at : at + hid_rows]
    parts = [x[:, cut] for x in halves for cut in (slice(in_cut, in_cut + wo_cut), slice(hid + wo_cut, None))]
    out_ref[...] = jnp.concatenate(parts, axis=1)
    total = jnp.sum(w_ref[...].astype(F32) * in_ref[...], axis=1, keepdims=True)
    square[...] = jnp.zeros_like(square)
    square[:shard, :] = jnp.broadcast_to(total, (shard, LANES))
    gain_out[...] = square[...].T[0:1, :shard] / gain_ref[...].astype(F32)


def body(
    layer_input,
    gain_attn,
    w_query,
    w_key,
    w_value,
    w_output,
    bias_table,
    gain_ffn,
    ffn_in,
    ffn_out,
    buckets,
    keep_mask,
    out_grad,
):
    dp = lax.axis_size("dp")
    s = lax.axis_index("seq")
    d = lax.axis_index("dp")
    nseq, count, width = layer_input.shape
    length = 2 * count
    span = 2 * length
    half = width // 2
    shard = w_query.shape[0]
    rows = 2 * shard
    hid_rows = ffn_out.shape[0]
    hid = hid_rows * dp
    table_rows = bias_table.shape[0]
    tok = nseq * length
    pairs = half // LANES
    meta = jnp.stack([s, d]).astype(jnp.int32)
    aligned = rows % 16 == 0 and hid_rows % 16 == 0

    def sds(shape, dtype=BF):
        return jax.ShapeDtypeStruct(shape, dtype)

    def far(shape, dtype=BF):
        return pltpu.HBM(shape, dtype)

    table = jnp.pad(bias_table, (0, shard - table_rows))
    extra_columns = jnp.pad(jnp.stack([gain_attn, gain_ffn, table], axis=1), ((0, 0), (0, LANES - 3)))

    def second_columns(h):
        out_cols = lax.dynamic_slice_in_dim(w_output, h * half, half, 1)
        in_cols = lax.dynamic_index_in_dim(ffn_in.reshape(shard, dp, 2, hid_rows), h, 2, keepdims=False)
        return jnp.concatenate([out_cols, in_cols.reshape(shard, hid)], axis=1)

    def swapped(mine, theirs):
        theirs = other_core(theirs)
        return jnp.where(s == 0, jnp.concatenate([mine, theirs]), jnp.concatenate([theirs, mine]))

    first_cols = 3 * half + LANES
    second_cols = half + hid
    first_cut = (first_cols // LANES // 2) * LANES
    second_cut = (second_cols // LANES // 2) * LANES
    third_cut = (width // LANES // 2) * LANES

    first_mine, first_theirs = pl.pallas_call(
        first_kernel,
        in_specs=[SMEM, FAR, FAR, FAR, pl.BlockSpec(memory_space=pltpu.VMEM)],
        out_specs=[pl.BlockSpec(memory_space=pltpu.VMEM)] * 2,
        out_shape=[sds((shard, first_cols))] * 2,
        scratch_shapes=[pltpu.VMEM((3, shard, width), BF), pltpu.SemaphoreType.DMA((3,))],
        compiler_params=params(),
        name="first_columns",
    )(meta, w_query, w_key, w_value, extra_columns)
    first = Gather(swapped(first_mine, first_theirs), first_cut, dp)
    first.high()
    x_oth = other_core(after(layer_input, first.have))
    second_block = swapped(second_columns(s), second_columns(1 - s))
    x_oth, second_block = meet((x_oth, second_block), (first, "have got"))
    second = Gather(second_block, second_cut, dp)
    first.first()
    second.begin()
    meet((), (first, "left right left_x right_y"), (second, "near"))
    first.second()
    second.high()
    g_oth = other_core(out_grad)
    keep_oth = other_core(keep_mask.astype(BF))
    keep = keep_mask.astype(BF)
    keep = jnp.where(s == 0, jnp.concatenate([keep, keep_oth], 1), jnp.concatenate([keep_oth, keep], 1))
    mask = ((keep.astype(F32) - 1.0) * 1e9)[:, None, :]
    g_both = jnp.concatenate([out_grad, g_oth], axis=1)

    high = dp // 4
    orders = [np.array([(h << 2) | low for low in lows for h in range(high)], np.int32) for lows in ((0, 1, 2, 3), (0, 2, 1, 3))]
    pos_l, pos_r = ((d ^ jnp.asarray(order)).astype(jnp.int32) for order in orders)
    pos = pos_l

    def settle(pieces, places=pos_l):
        if aligned:
            return pieces
        every = jnp.concatenate(pieces, axis=0)
        order = jnp.argsort(places)
        return [every[order].reshape(1, -1, every.shape[-1])]

    def settle_both(gather):
        left, right = gather.pieces()
        return settle(left), settle(right, pos_r)

    if not aligned:
        pos_k, rows_k, hid_rows_k, nblk, dp_k = jnp.zeros((2, 1), jnp.int32), width, hid, 1, 1
    else:
        pos_k, rows_k, hid_rows_k, nblk, dp_k = jnp.stack([pos_l, pos_r]), rows, hid_rows, dp, dp

    feature = np.arange(width)
    chunk, within = feature // rows, feature % rows
    entry = np.where(within % shard < table_rows, table_rows * chunk + within % shard, -1)
    head, bucket = entry // BUCKETS, entry % BUCKETS
    half_heads = HEADS // 2
    hsel = np.zeros((2, 8, width), np.float32)
    bsel = np.zeros((width, LANES), np.float32)
    for f in range(width):
        if entry[f] >= 0:
            hsel[head[f] // half_heads, head[f] % half_heads, f] = 1.0
            bsel[f, bucket[f]] = 1.0
    bsel_once = jnp.asarray(np.where(within[:, None] < shard, bsel, 0.0))
    hsel, bsel = jnp.asarray(hsel), jnp.asarray(bsel)
    padded = jnp.concatenate([buckets, jnp.full((span - buckets.shape[0],), -1, jnp.int32)])[None]

    seq_block = lambda shape: pl.BlockSpec((1,) + shape, lambda n: (n, 0, 0))
    VMEM = pl.BlockSpec(memory_space=pltpu.VMEM)
    rel = dp if aligned else 0

    def block_shapes(block_rows, cut, cols):
        if aligned:
            left, right = (2, high, block_rows, cut), (2, high, block_rows, cols - cut)
            return [left, left, right, right]
        return [(dp * block_rows, cols)]

    def in_relative(parts, block_rows, cut):
        if aligned:
            return parts
        blocks = parts[0].reshape(dp, block_rows, -1)[pos_l].reshape(2, 2, high, block_rows, -1)
        left, right = blocks[..., :cut], blocks[..., cut:]
        return left[1], left[0], right[:, 1], right[:, 0]

    def gradient(kernel, inputs, block_rows, cut, cols, name, earlier=()):
        shapes = block_shapes(block_rows, cut, cols)

        def ordered(meta_ref, *refs):
            kernel(meta_ref, *refs[len(earlier) :], rows=block_rows, cut=cut, dp=rel)

        parts = pl.pallas_call(
            ordered,
            in_specs=[SMEM] + [ANY] * len(earlier) + [VMEM] * len(inputs),
            out_specs=[VMEM] * len(shapes),
            out_shape=[sds(x) for x in shapes],
            scratch_shapes=[pltpu.VMEM((dp * block_rows, cols), BF)] if aligned else [],
            compiler_params=params(10),
            name=name,
            cost_estimate=cost(name),
        )(meta, *earlier, *inputs)
        return in_relative(parts, block_rows, cut)

    x_oth, ffn_out, mask, g_both = meet(
        (x_oth, ffn_out, mask, g_both), (first, "left right left_far right_far"), (second, "have got")
    )
    second.first()
    third = Gather(ffn_out, third_cut, dp)
    left, right = settle_both(first)
    q, k, v, normed_attn, misc, peroff, w_qkv = pl.pallas_call(
        functools.partial(qkv_kernel, rows=rows_k, cut=first_cut, width=width, nl=len(left), nr=len(right)),
        grid=(nseq,),
        in_specs=[SMEM, SMEM, seq_block((count, width)), seq_block((count, width)), whole((1, span)), whole(hsel.shape), whole(bsel.shape)]
        + [whole(x.shape) for x in left + right],
        out_specs=[seq_block((length, half))] * 3 + [seq_block((length, width)), whole((8, width)), whole((8, span)), ANY],
        out_shape=[sds((nseq, length, half))] * 3
        + [far((nseq, length, width)), sds((8, width), F32), sds((8, span), F32), far((width, first_cols))],
        scratch_shapes=[pltpu.VMEM((width, first_cols), BF), pltpu.SemaphoreType.DMA],
        compiler_params=params(8),
        name="qkv",
        cost_estimate=cost("qkv"),
    )(meta, pos_k, layer_input, x_oth, padded, hsel, bsel_once, *left, *right)

    q, k, v = meet((q, k, v), (second, "left right left_x right_y"))
    second.second()
    third.high()
    ctx_own, ctx_send, expo, inv = pl.pallas_call(
        attend_kernel,
        in_specs=[SMEM] + [VMEM] * 5,
        out_specs=[VMEM, VMEM, ANY, ANY],
        out_shape=[
            sds((nseq, count, half)),
            sds((nseq, count, half)),
            far((nseq, pairs, 2, length, length)),
            far((nseq, length, half), F32),
        ],
        scratch_shapes=[
            pltpu.VMEM((half_heads, LANES, span), F32),
            pltpu.VMEM((length, LANES), BF),
            pltpu.VMEM((2, length, length), F32),
            pltpu.VMEM((3, 2, length, length), BF),
            pltpu.VMEM((3, length, LANES), F32),
            pltpu.SemaphoreType.DMA((3,)),
            pltpu.SemaphoreType.DMA((3,)),
        ],
        compiler_params=params(12),
        name="attend",
        cost_estimate=cost("attend"),
    )(meta, q, k, v, mask, peroff)

    ctx_own, ctx_send = meet((ctx_own, ctx_send), (second, "left right left_far right_far"), (third, "have got"))
    ctx_oth = other_core(ctx_send)
    wo_own = stack(second.pieces()[0], half, "output_columns")[0]
    wo_oth = other_core(wo_own)
    third.first()
    wo_own, wo_oth = settle([wo_own])[0], settle([wo_oth])[0]
    middle, normed_own, w_o = pl.pallas_call(
        functools.partial(middle_kernel, rows=rows_k),
        in_specs=[SMEM, SMEM] + [VMEM] * 6,
        out_specs=[ANY, VMEM, ANY],
        out_shape=[far((nseq, count, width), F32), sds((nseq, count, width)), far((2, width, half))],
        scratch_shapes=[
            pltpu.VMEM((2, width, half), BF),
            pltpu.VMEM((nseq, count, width), F32),
            pltpu.SemaphoreType.DMA,
            pltpu.SemaphoreType.DMA((nseq,)),
        ],
        compiler_params=params(8),
        name="middle",
        cost_estimate=cost("middle"),
    )(meta, pos_k, layer_input, ctx_own, ctx_oth, misc, wo_own, wo_oth)

    middle, normed_own = meet((middle, normed_own), (third, "left right left_x right_y"))
    third.second()
    normed_oth = other_core(normed_own)
    left, right = settle_both(second)
    act, slope, w_in = pl.pallas_call(
        functools.partial(hidden_kernel, rows=rows_k, skip=half, cut=second_cut, nl=len(left), nr=len(right)),
        grid=(nseq,),
        in_specs=[SMEM, seq_block((count, width)), seq_block((count, width))] + [whole(x.shape) for x in left + right],
        out_specs=[seq_block((length, hid)), seq_block((length, hid)), whole((width, hid))],
        out_shape=[sds((nseq, length, hid)), sds((nseq, length, hid)), sds((width, hid))],
        compiler_params=params(),
        name="hidden",
        cost_estimate=cost("hidden"),
    )(pos_k, normed_own, normed_oth, *left, *right)
    out_parts = gradient(wgrad_kernel, (act, g_both), hid_rows, third_cut, width, "grad_ffn_out")

    out_parts, slope, act = meet((out_parts, slope, act), (third, "left right left_far right_far"))
    out_sum = Scatter(out_parts, dp)
    out_sum.first()
    left, right = settle_both(third)
    seq_half = seq_block((count, width))
    grad_pre, back_own, back_send, out_own, out_send = pl.pallas_call(
        functools.partial(ffn_back_kernel, rows=hid_rows_k, cut=third_cut, nl=len(left), nr=len(right)),
        grid=(nseq,),
        in_specs=[SMEM, seq_block((length, width)), seq_block((length, hid)), seq_block((length, hid)), whole((width, hid))]
        + [whole(x.shape) for x in left + right],
        out_specs=[seq_block((length, hid))] + [seq_half] * 4,
        out_shape=[sds((nseq, length, hid)), sds((nseq, count, width), F32), sds((nseq, count, width))]
        + [far((nseq, count, width), F32), far((nseq, count, width))],
        scratch_shapes=[pltpu.VMEM((hid, width), BF)],
        input_output_aliases={3: 0},
        compiler_params=params(8),
        name="ffn_back",
        cost_estimate=cost("ffn_back"),
    )(pos_k, g_both, act, slope, w_in, *left, *right)

    grad_pre, back_own, back_send, out_own, out_send = meet(
        (grad_pre, back_own, back_send, out_own, out_send), (out_sum, "left_got right_got")
    )
    out_sum.second()
    back_oth, out_oth = other_core(back_send), other_core(out_send)
    in_cut = (hid // LANES // 2) * LANES
    in_parts = gradient(
        functools.partial(wgrad_kernel, na=2),
        (normed_own, normed_oth, grad_pre),
        rows,
        in_cut,
        hid,
        "grad_ffn_in",
        (out_sum.left_send, out_sum.right_send),
    )

    in_parts, back_own, back_oth, out_oth = meet(
        (in_parts, back_own, back_oth, out_oth), (out_sum, "left_got right_got")
    )
    out_sum.high()
    grad_middle, middle_low, dctx_own, dctx_send = pl.pallas_call(
        middle_back_kernel,
        grid=(nseq,),
        in_specs=[SMEM] + [seq_block((count, width))] * 4 + [whole((8, width)), whole((2, width, half))],
        out_specs=[seq_block((count, width)), seq_block((count, width)), seq_block((count, half)), seq_block((count, half))],
        out_shape=[
            sds((nseq, count, width), F32),
            sds((nseq, count, width)),
            sds((nseq, count, half)),
            sds((nseq, count, half)),
        ],
        compiler_params=params(),
        name="middle_back",
        cost_estimate=cost("middle_back"),
    )(meta, out_grad, middle, back_own, back_oth, misc, w_o)
    dctx_oth = other_core(dctx_send)
    rel_meta = meta if aligned else jnp.stack([s, jnp.zeros_like(d)]).astype(jnp.int32)
    wo_keep, wo_send = pl.pallas_call(
        functools.partial(wo_grad_kernel, rows=rows_k, dp=dp_k),
        out_shape=[sds((dp_k, rows_k, half))] * 2,
        in_specs=[SMEM] + [VMEM] * 3,
        out_specs=[VMEM] * 2,
        scratch_shapes=[pltpu.VMEM((2, width, half), F32)],
        compiler_params=params(),
        name="grad_output",
        cost_estimate=cost("grad_output"),
    )(rel_meta, ctx_own, ctx_oth, middle_low)
    wo_got = other_core(wo_send)
    if not aligned:
        wo_keep, wo_got = (x.reshape(dp, rows, half)[d ^ jnp.arange(dp)] for x in (wo_keep, wo_got))
    wo_cut = (half // LANES // 2) * LANES

    wo_keep, wo_got, dctx_own, dctx_oth = meet((wo_keep, wo_got, dctx_own, dctx_oth))
    in_sum = Scatter(with_output_columns(in_parts, wo_keep, wo_got, wo_cut), dp)
    in_sum.first()
    dq, dk, dv, off = pl.pallas_call(
        attend_back_kernel,
        in_specs=[SMEM] + [VMEM] * 7,
        out_specs=[VMEM] * 4,
        out_shape=[sds((nseq, length, half))] * 3 + [sds((8, span), F32)],
        scratch_shapes=[
            pltpu.VMEM((2, LANES, span), F32),
            pltpu.VMEM((length, LANES), BF),
            pltpu.VMEM((2, length, length), F32),
            pltpu.VMEM((2, length, length), BF),
        ],
        compiler_params=params(8),
        name="attend_back",
        cost_estimate=cost("attend_back"),
    )(meta, q, k, v, expo, inv, dctx_own, dctx_oth)
    dq, dk, dv, off = meet((dq, dk, dv, off), (out_sum, "got"), (in_sum, "left_got right_got"))
    in_sum.second()
    qkv_parts = gradient(
        qkv_grad_kernel,
        (normed_attn, dq, dk, dv, off, padded, hsel, bsel),
        rows,
        first_cut,
        first_cols,
        "grad_qkv",
        (in_sum.left_send, in_sum.right_send),
    )

    qkv_parts, dq, dk, dv, w_qkv = meet((qkv_parts, dq, dk, dv, w_qkv), (in_sum, "left_got right_got"))
    qkv_sum = Scatter(qkv_parts, dp)
    qkv_sum.first()
    in_sum.high()
    dn_own, dn_send = pl.pallas_call(
        input_grad_kernel,
        grid=(nseq,),
        in_specs=[SMEM] + [seq_block((length, half))] * 3 + [whole((width, first_cols))],
        out_specs=[seq_half] * 2,
        out_shape=[sds((nseq, count, width), F32), sds((nseq, count, width))],
        compiler_params=params(),
        name="input_grad",
        cost_estimate=cost("input_grad"),
    )(meta, dq, dk, dv, w_qkv)
    dn_own, dn_send, in_sum.got[:2] = meet((dn_own, dn_send, in_sum.got[:2]), (qkv_sum, "left_got right_got"))
    qkv_sum.second()
    grad_ffn_out = out_sum.rest(F32)
    grad_ffn_out, dn_send = meet((grad_ffn_out, dn_send), (qkv_sum, "left_got right_got"), (in_sum, "got"))
    qkv_sum.high()
    dn_oth = other_core(dn_send)
    kept = [pltpu.with_memory_space_constraint(x, pltpu.HBM) for x in (grad_middle, middle, out_own, out_oth)]
    part = pl.BlockSpec((1, count // 2, width), lambda n, i: (n, i, 0))
    grad_input, layer_out = pl.pallas_call(
        last_kernel,
        grid=(nseq, 2),
        in_specs=[part] * 7 + [whole((8, width))],
        out_specs=[part] * 2,
        out_shape=[sds((nseq, count, width))] * 2,
        compiler_params=params(),
        name="last",
        cost_estimate=cost("last"),
    )(layer_input, kept[0], dn_own, dn_oth, *kept[1:], misc)
    grad_input, layer_out = meet((grad_input, layer_out), (qkv_sum, "got"), (in_sum, "keep got"))

    def both_cores(block):
        mine = lax.dynamic_slice_in_dim(block, s * shard, shard, 0)
        return mine, other_core(lax.dynamic_slice_in_dim(block, (1 - s) * shard, shard, 0))

    mine, theirs = both_cores(in_sum.rest())
    grad_ffn_in, grad_output, gain_ffn_row = pl.pallas_call(
        functools.partial(finish_in_kernel, in_cut=in_cut, wo_cut=wo_cut, hid_rows=hid_rows, dp=dp),
        in_specs=[SMEM] + [VMEM] * 4,
        out_specs=[VMEM] * 3,
        out_shape=[sds((shard, 2 * hid), F32), sds((shard, width), F32), sds((1, shard), F32)],
        scratch_shapes=[pltpu.VMEM((LANES, LANES), F32)],
        compiler_params=params(),
        name="finish_in",
        cost_estimate=cost("finish"),
    )(meta, mine, theirs, ffn_in, gain_ffn[None])
    mine, theirs = both_cores(qkv_sum.rest())
    grad_query, grad_key, grad_value, gain_row, bias_row = pl.pallas_call(
        functools.partial(finish_kernel, dp=dp, table_rows=table_rows),
        in_specs=[SMEM] + [VMEM] * 6,
        out_specs=[VMEM] * 5,
        out_shape=[sds((shard, width), F32)] * 3 + [sds((1, shard), F32), sds((1, table_rows), F32)],
        scratch_shapes=[pltpu.VMEM((LANES, LANES), F32)],
        compiler_params=params(),
        name="finish",
        cost_estimate=cost("finish"),
    )(meta, mine, theirs, w_query, w_key, w_value, gain_attn[None])
    return (
        layer_out,
        grad_input,
        gain_row.reshape(shard),
        grad_query,
        grad_key,
        grad_value,
        grad_output,
        bias_row.reshape(table_rows),
        gain_ffn_row.reshape(shard),
        grad_ffn_in,
        grad_ffn_out,
    )


def solution(mesh):
    both = ("dp", "seq")
    return jax.shard_map(
        body,
        mesh=mesh,
        in_specs=(
            P("dp", "seq", None),
            P(both),
            P(both, None),
            P(both, None),
            P(both, None),
            P(both, None),
            P("dp"),
            P(both),
            P(both, None),
            P(both, None),
            P(),
            P("dp", "seq"),
            P("dp", "seq", None),
        ),
        out_specs=(
            P("dp", "seq", None),
            P("dp", "seq", None),
            P(both),
            P(both, None),
            P(both, None),
            P(both, None),
            P(both, None),
            P("dp"),
            P(both),
            P(both, None),
            P(both, None),
        ),
        check_vma=False,
    )
```

```python
import functools
import math

import jax
import jax.numpy as jnp
import numpy as np
from jax import lax
from jax.experimental import pallas as pl
from jax.experimental.pallas import tpu as pltpu
from jax.sharding import PartitionSpec as P

HEADS = 12
HEAD_DIM = 64
BUCKETS = 32
EPSILON = 1e-06
LANES = 128
BF = jnp.bfloat16
F32 = jnp.float32
GELU_A = math.sqrt(2.0 / math.pi)
GELU_B = 0.044715

ANY = pl.BlockSpec(memory_space=pl.ANY)
SMEM = pl.BlockSpec(memory_space=pltpu.SMEM)
FAR = pl.BlockSpec(memory_space=pltpu.HBM)


def whole(shape):
    zeros = (0,) * len(shape)
    return pl.BlockSpec(shape, lambda *_: zeros)


def params(mib=6):
    return pltpu.CompilerParams(vmem_limit_bytes=mib * 1024 * 1024)


MICROS = {
    "qkv": 7, "attend": 10, "middle": 4, "hidden": 8, "grad_ffn_out": 5, "grad_ffn_in": 5, "ffn_back": 9, "ffn_out": 5,
    "middle_back": 4, "grad_output": 2, "attend_back": 14, "grad_qkv": 5, "input_grad": 5, "last": 3, "finish": 1,
}


def cost(name):
    return pl.CostEstimate(flops=int(MICROS[name] * 1e4), bytes_accessed=0, transcendentals=0)


def nn(a, b):
    return lax.dot_general(a, b, (((1,), (0,)), ((), ())), preferred_element_type=F32)


def nt(a, b):
    return lax.dot_general(a, b, (((1,), (1,)), ((), ())), preferred_element_type=F32)


def tn(a, b):
    return lax.dot_general(a, b, (((0,), (0,)), ((), ())), preferred_element_type=F32)


def flip(x, axis, bit, count):
    return lax.ppermute(x, axis, [(i, i ^ bit) for i in range(count)])


def after(values, *others):
    return lax.optimization_barrier((values, others))[0]


def meet(values, *fields):
    held = [[getattr(owner, name) for name in names.split()] for owner, names in fields]
    values, held = lax.optimization_barrier((values, held))
    for (owner, names), got in zip(fields, held):
        for name, value in zip(names.split(), got):
            setattr(owner, name, value)
    return values


def bit_groups(dp, most=2):
    bits, groups = dp.bit_length() - 3, []
    at = 2
    while bits > 0:
        groups.append((1 << at, 1 << min(bits, most)))
        at, bits = at + most, bits - most
    return groups


def small(kernel, inputs, shapes, name, dtype=BF):
    return pl.pallas_call(
        kernel,
        in_specs=[SMEM if x.ndim == 1 else pl.BlockSpec(memory_space=pltpu.VMEM) for x in inputs],
        out_specs=[pl.BlockSpec(memory_space=pltpu.VMEM)] * len(shapes),
        out_shape=[jax.ShapeDtypeStruct(x, dtype) for x in shapes],
        compiler_params=params(),
        name=name,
        cost_estimate=pl.CostEstimate(flops=10**4, bytes_accessed=0, transcendentals=0),
    )(*inputs)


def total_of(refs, at, dtype=BF):
    return functools.reduce(lambda x, y: x + y, (ref[at].astype(F32) for ref in refs)).astype(dtype)


def merge(sides, size, joined, name, dtype=BF):
    counts = [len(side) for side in sides]
    k, rows, _ = sides[0][0].shape
    widths = [side[0].shape[2] for side in sides]
    part = k // size
    shapes = [(part, rows, sum(widths))] * size if joined else [(part, rows, w) for w in widths for _ in range(size)]

    def kernel(*refs):
        ins, outs = refs[: sum(counts)], refs[sum(counts) :]
        at, lane = 0, 0
        for i, (count, width) in enumerate(zip(counts, widths)):
            for j in range(k):
                out = outs[j // part] if joined else outs[i * size + j // part]
                out[j % part, :, lane : lane + width] = total_of(ins[at : at + count], j, dtype)
            at += count
            lane = lane + width if joined else 0

    return small(kernel, [x for side in sides for x in side], shapes, name, dtype)


def stack(pieces, cut, name):
    ks = [x.shape[0] for x in pieces]
    rows, cols = pieces[0].shape[1:]

    def kernel(*refs):
        left, right = refs[len(ks) :]
        at = 0
        for ref, k in zip(refs, ks):
            left[at : at + k] = ref[:, :, :cut]
            right[at : at + k] = ref[:, :, cut:]
            at += k

    return small(kernel, pieces, [(sum(ks), rows, cut), (sum(ks), rows, cols - cut)], name)


def pair_up(a, b, c, d, name):
    k = a.shape[0]

    def kernel(a_ref, b_ref, c_ref, d_ref, ab, cd):
        ab[:k], ab[k:] = a_ref[...], b_ref[...]
        cd[:k], cd[k:] = c_ref[...], d_ref[...]

    return small(kernel, (a, b, c, d), [(2 * k,) + a.shape[1:], (2 * k,) + c.shape[1:]], name)


def with_output_columns(parts, keep, got, cut):
    count, _, half = keep.shape
    widths = [x.shape[-1] for x in parts]
    extra = (cut, cut, half - cut, half - cut)
    shapes = [x.shape[:-1] + (w + more,) for x, w, more in zip(parts, widths, extra)]

    def kernel(*refs):
        ins, keep_ref, got_ref, outs = refs[:4], refs[4], refs[5], refs[6:]
        for ref, out, w in zip(ins, outs, widths):
            out[..., :w] = ref[...]
        for rel in range(count):
            x, y, high = rel & 1, (rel >> 1) & 1, rel >> 2
            block = total_of((keep_ref, got_ref), rel)
            i = 0 if y else 1
            outs[i][x, high, :, widths[i] :] = block[:, :cut]
            i = 2 if x else 3
            outs[i][y, high, :, widths[i] :] = block[:, cut:]

    return small(kernel, (*parts, keep, got), shapes, "output_parts")


class Gather:
    def __init__(self, block, cut, dp):
        self.have, self.cut, self.dp = block[None], cut, dp
        self.near = None

    def begin(self):
        self.near = flip(self.have, "dp", 4, self.dp)

    def high(self):
        self.got = []
        groups = bit_groups(self.dp)
        for i, (bit, size) in enumerate(groups):
            first = [self.near] if bit == 4 and self.near is not None else [flip(self.have, "dp", bit, self.dp)]
            self.got = first + [flip(self.have, "dp", bit * k, self.dp) for k in range(2, size)]
            if i + 1 < len(groups):
                self.have = jnp.concatenate([self.have] + self.got, axis=0)

    def first(self):
        self.left, self.right = stack([self.have] + self.got, self.cut, "stack")
        self.left_x = flip(self.left, "dp", 1, self.dp)
        self.right_y = flip(self.right, "dp", 2, self.dp)

    def second(self):
        self.left, self.right = pair_up(self.left, self.left_x, self.right, self.right_y, "pair_up")
        self.left_far = flip(self.left, "dp", 2, self.dp)
        self.right_far = flip(self.right, "dp", 1, self.dp)

    def pieces(self):
        return [self.left, self.left_far], [self.right, self.right_far]


class Scatter:
    def __init__(self, parts, dp, most=2):
        flat = [x.reshape((-1,) + x.shape[2:]) for x in parts]
        self.left_send, self.left_keep, self.right_send, self.right_keep = flat
        self.dp, self.groups = dp, bit_groups(dp, most)

    def first(self):
        self.left_got = flip(self.left_send, "dp", 2, self.dp)
        self.right_got = flip(self.right_send, "dp", 1, self.dp)

    def second(self):
        self.left, self.left_send, self.right, self.right_send = merge(
            [[self.left_keep, self.left_got], [self.right_keep, self.right_got]], 2, False, "add_second"
        )
        self.left_got = flip(self.left_send, "dp", 1, self.dp)
        self.right_got = flip(self.right_send, "dp", 2, self.dp)

    def spread(self, sides):
        bit, size = self.groups.pop()
        self.keep, *parts = merge(sides, size, True, "add_high")
        self.got = [flip(x, "dp", bit * (k + 1), self.dp) for k, x in enumerate(parts)]

    def high(self):
        self.spread([[self.left, self.left_got], [self.right, self.right_got]])

    def halves(self, meta, shard):
        while self.groups:
            self.spread([[self.keep] + self.got])
        terms = [self.keep] + self.got

        def kernel(meta_ref, *refs):
            ins, (mine, theirs) = refs[:-2], refs[-2:]
            total = functools.reduce(lambda x, y: x + y, (ref[0].astype(F32) for ref in ins))
            low, top = total[:shard], total[shard:]
            mine[...] = jnp.where(meta_ref[0] == 0, low, top).astype(BF)
            theirs[...] = jnp.where(meta_ref[0] == 0, top, low).astype(BF)

        return small(kernel, [meta] + terms, [(shard, terms[0].shape[-1])] * 2, "halves")

    def rest(self, dtype=BF):
        while self.groups:
            self.spread([[self.keep] + self.got])
        return merge([[self.keep] + self.got], 1, True, "add_last", dtype)[0][0]


def other_core(x):
    return lax.ppermute(x, "seq", [(0, 1), (1, 0)])


def place(refs, pos, side, rows, dst, lane, skip=0):
    at = 0
    for ref in refs:
        cols = ref.shape[2] - skip
        for b in range(ref.shape[0]):
            row = pl.multiple_of(pos[side, at] * rows, rows)
            dst[pl.ds(row, rows), lane : lane + cols] = ref[b, :, skip:]
            at += 1


def second_kernel(meta, w_out, w_in, mine, theirs, *, hid_rows, dp):
    s = meta[0]
    half = w_out.shape[1] // 2
    low, top = w_out[:, :half], w_out[:, half:]
    mine[:, :half] = jnp.where(s == 0, low, top)
    theirs[:, :half] = jnp.where(s == 0, top, low)
    for c in range(dp):
        at, to = 2 * c * hid_rows, half + c * hid_rows
        low, top = w_in[:, at : at + hid_rows], w_in[:, at + hid_rows : at + 2 * hid_rows]
        mine[:, to : to + hid_rows] = jnp.where(s == 0, low, top)
        theirs[:, to : to + hid_rows] = jnp.where(s == 0, top, low)


def qkv_kernel(meta, pos, x_own, x_oth, buckets, hsel, bsel, *rest, rows, cut, width, nl, nr):
    left, right = rest[:nl], rest[nl : nl + nr]
    q_ref, k_ref, v_ref, norm_ref, misc, peroff, w_far, w, sem = rest[nl + nr :]
    s = meta[0]
    half = width // 2
    n = pl.program_id(0)
    copy = pltpu.make_async_copy(w, w_far, sem)

    @pl.when(n == 0)
    def _():
        place(left, pos, 0, rows, w, 0)
        place(right, pos, 1, rows, w, cut)
        copy.start()
        extra = w[:, 3 * half :].astype(F32)
        misc[...] = extra.T[:8]
        spread = (extra[:, 2:3] * bsel[...]).astype(BF)
        table = nn(hsel[s].astype(BF), spread)
        one_hot = (
            lax.broadcasted_iota(jnp.int32, (LANES, buckets.shape[1]), 0) == buckets[...]
        ).astype(F32)
        peroff[...] = nn(table.astype(BF), one_hot.astype(BF))

    gain = misc[0:1, :]
    count = x_own.shape[1]
    for side, x_ref in ((0, x_own), (1, x_oth)):
        x = x_ref[0].astype(F32)
        scale = lax.rsqrt(jnp.mean(x * x, axis=-1, keepdims=True) + EPSILON)
        normed = (x * scale * gain).astype(BF)
        at = pl.ds(pl.multiple_of((s if side == 0 else 1 - s) * count, count), count)
        norm_ref[0, at, :] = normed
        q_ref[0, at, :] = nn(normed, w[:, :half]).astype(BF)
        k_ref[0, at, :] = nn(normed, w[:, half : 2 * half]).astype(BF)
        v_ref[0, at, :] = nn(normed, w[:, 2 * half : 3 * half]).astype(BF)

    @pl.when(n == pl.num_programs(0) - 1)
    def _():
        copy.wait()


def lane_half(shape, which):
    lane = lax.broadcasted_iota(jnp.int32, shape, 1)
    return (lane < HEAD_DIM) if which == 0 else (lane >= HEAD_DIM)


def attend_kernel(meta, q_ref, k_ref, v_ref, mask_ref, peroff, own_ref, oth_ref, e_far, inv_far, grid, ctx, table, e_buf, inv_buf, sems, inv_sems):
    s = meta[0]
    nseq, length, width = q_ref.shape
    step = LANES
    rows = step // 2
    half = length // 2
    span = grid.shape[-1]
    zero, one = jnp.zeros((), BF), jnp.ones((), BF)
    first = lane_half((length, LANES), 0)
    heads = width // HEAD_DIM
    for h in range(heads):
        wide = jnp.broadcast_to(peroff[h : h + 1, :], (step, span))
        grid[h] = pltpu.roll(wide, span - step + 1, 1, stride=1, stride_axis=0)
    items = [(hp, n, hh) for hp in range(heads // 2) for n in range(nseq) for hh in range(2)]

    def product(i):
        hp, n, hh = items[i]
        lanes = slice(hp * LANES, (hp + 1) * LANES)
        head = jnp.where(first if hh == 0 else ~first, q_ref[n, :, lanes], zero)
        table[i % 2] = nt(head, k_ref[n, :, lanes])

    def stores(i):
        hp, n, _ = items[2 * i]
        inv_dst = inv_far.at[n, :, pl.ds(hp * LANES, LANES)]
        return (
            pltpu.make_async_copy(e_buf.at[i % 3], e_far.at[n, hp], sems.at[i % 3]),
            pltpu.make_async_copy(inv_buf.at[i % 3], inv_dst, inv_sems.at[i % 3]),
        )

    product(0)
    sums = [None, None]
    for i, (hp, n, hh) in enumerate(items):
        lanes = slice(hp * LANES, (hp + 1) * LANES)
        e_ref = e_buf.at[i // 2 % 3]
        if i + 1 < len(items):
            product(i + 1)
        if hh == 0 and i >= 6:
            for copy in stores(i // 2 - 3):
                copy.wait()
        for at in range(0, length, rows):
            base, within = length - step - at // step * step, at % step
            bias = grid[2 * hp + hh, within : within + rows, base : base + length]
            scores = table[i % 2, at : at + rows] + (bias + mask_ref[n])
            top = jnp.max(scores, axis=-1, keepdims=True)
            e_ref[hh, at : at + rows, :] = jnp.exp(scores - top).astype(BF)
        sums[hh] = nn(e_ref[hh], jnp.where(first if hh == 0 else ~first, v_ref[n, :, lanes], one))
        if hh == 1:
            num = jnp.where(first, sums[0], sums[1])
            den = pltpu.roll(jnp.where(first, sums[1], sums[0]), HEAD_DIM, 1)
            inv = 1.0 / den
            inv_buf[i // 2 % 3] = inv
            for copy in stores(i // 2):
                copy.start()
            ctx[...] = (num * inv).astype(BF)
            own_ref[n, :, lanes] = ctx[pl.ds(pl.multiple_of(s * half, half), half), :]
            oth_ref[n, :, lanes] = ctx[pl.ds(pl.multiple_of((1 - s) * half, half), half), :]
    for i in range(max(0, len(items) // 2 - 3), len(items) // 2):
        for copy in stores(i):
            copy.wait()


def middle_kernel(meta, pos, x_ref, own_ref, oth_ref, misc, own_w, oth_w, mid_far, norm_ref, w_far, w, mid, sem, mid_sems, *, rows):
    s = meta[0]
    half = w.shape[2]
    place([own_w], pos, 0, rows, w.at[s], 0)
    place([oth_w], pos, 0, rows, w.at[1 - s], 0)
    copy = pltpu.make_async_copy(w, w_far, sem)
    copy.start()
    at_own = pl.ds(pl.multiple_of(s * half, half), half)
    at_oth = pl.ds(pl.multiple_of((1 - s) * half, half), half)
    for n in range(x_ref.shape[0]):
        x = x_ref[n].astype(F32)
        parts = []
        for c in range(2):
            part = nn(own_ref[n], w[c, at_own, :]) + nn(oth_ref[n], w[c, at_oth, :])
            parts.append(x[:, c * half : (c + 1) * half] + part)
        middle = jnp.concatenate(parts, axis=-1)
        mid[n] = middle
        pltpu.make_async_copy(mid.at[n], mid_far.at[n], mid_sems.at[n]).start()
        scale = lax.rsqrt(jnp.mean(middle * middle, axis=-1, keepdims=True) + EPSILON)
        norm_ref[n] = (middle * scale * misc[1:2, :]).astype(BF)
    copy.wait()
    for n in range(x_ref.shape[0]):
        pltpu.make_async_copy(mid.at[n], mid_far.at[n], mid_sems.at[n]).wait()


def hidden_kernel(pos, own_ref, oth_ref, *rest, rows, skip, cut, nl, nr):
    left, right = rest[:nl], rest[nl : nl + nr]
    act_ref, slope_ref, w = rest[nl + nr :]

    @pl.when(pl.program_id(0) == 0)
    def _():
        place(left, pos, 0, rows, w, 0, skip)
        place(right, pos, 1, rows, w, cut - skip)

    count = own_ref.shape[1]
    width = w.shape[1]
    step = 768
    for side, ref in ((0, own_ref), (1, oth_ref)):
        at = slice(side * count, (side + 1) * count)
        for c in range(0, width, step):
            v = nn(ref[0], w[:, c : c + step])
            square = v * v
            p = 0.5 + 0.5 * jnp.tanh(v * (GELU_A + (GELU_A * GELU_B) * square))
            act = v * p
            slope = p + act * ((1.0 - p) * (2.0 * GELU_A + (6.0 * GELU_A * GELU_B) * square))
            act_ref[0, at, c : c + step] = act.astype(BF)
            slope_ref[0, at, c : c + step] = slope.astype(BF)


def wgrad_kernel(meta, *rest, rows, cut, dp, na=1):
    a_refs, b_ref, rest = rest[:na], rest[na], rest[na + 1 :]
    grad, at = 0.0, 0
    for a_ref in a_refs:
        a = a_ref[...].reshape(-1, a_ref.shape[-1])
        b = b_ref[:, at : at + a_ref.shape[1], :].reshape(a.shape[0], -1)
        grad, at = grad + tn(a, b), at + a_ref.shape[1]
    if dp == 0:
        rest[0][...] = grad.astype(BF)
    else:
        rest[-1][...] = grad.astype(BF)
        store_relative(meta, rest[-1], *rest[:4], rows, cut, dp)


def store_relative(meta, total, ls, lk, rs, rk, rows, cut, dp):
    d = meta[1]
    for rel in range(dp):
        x, y, high = rel & 1, (rel >> 1) & 1, rel >> 2
        at = pl.ds(pl.multiple_of((d ^ rel) * rows, rows), rows)
        (ls if y else lk)[x, high] = total[at, :cut]
        (rs if x else rk)[y, high] = total[at, cut:]


def ffn_back_kernel(pos, g_ref, act_ref, slope_ref, w_in, *rest, rows, cut, nl, nr):
    left, right = rest[:nl], rest[nl : nl + nr]
    pre_ref, own_ref, oth_ref, out_own, out_oth, w = rest[nl + nr :]

    @pl.when(pl.program_id(0) == 0)
    def _():
        place(left, pos, 0, rows, w, 0)
        place(right, pos, 1, rows, w, cut)

    count = own_ref.shape[1]
    width = w.shape[0]
    step = 512
    for c in range(0, width, step):
        grad = nt(g_ref[0], w[c : c + step, :])
        pre_ref[0, :, c : c + step] = (grad * slope_ref[0, :, c : c + step].astype(F32)).astype(BF)
    oth_ref[0] = nt(pre_ref[0, count:, :], w_in[...]).astype(BF)
    own_ref[0] = nt(pre_ref[0, :count, :], w_in[...])
    out_own[0] = nn(act_ref[0, :count, :], w[...])
    out_oth[0] = nn(act_ref[0, count:, :], w[...]).astype(BF)


def middle_back_kernel(meta, g_ref, mid_ref, own_ref, oth_ref, misc, w, gm_ref, low_ref, cown_ref, coth_ref):
    s = meta[0]
    half = w.shape[2]
    middle = mid_ref[0]
    scale = lax.rsqrt(jnp.mean(middle * middle, axis=-1, keepdims=True) + EPSILON)
    grad = own_ref[0] + oth_ref[0].astype(F32)
    scaled = grad * misc[1:2, :]
    inner = jnp.mean(scaled * middle, axis=-1, keepdims=True)
    grad_middle = g_ref[0].astype(F32) + scale * scaled - middle * (scale * scale * scale) * inner
    gm_ref[0] = grad_middle
    low = grad_middle.astype(BF)
    low_ref[0] = low
    for ref, which in ((cown_ref, s), (coth_ref, 1 - s)):
        at = pl.ds(pl.multiple_of(which * half, half), half)
        out = nt(low[:, :half], w[0, at, :]) + nt(low[:, half:], w[1, at, :])
        ref[0] = out.astype(BF)


def wo_grad_kernel(meta, own_ref, oth_ref, low_ref, keep_ref, send_ref, total, *, rows, dp):
    s, d = meta[0], meta[1]
    half = own_ref.shape[-1]
    low = low_ref[...].reshape(-1, low_ref.shape[-1])
    for ref, which in ((own_ref, s), (oth_ref, 1 - s)):
        at = pl.ds(pl.multiple_of(which * half, half), half)
        grad = tn(ref[...].reshape(low.shape[0], half), low)
        total[0, at, :] = grad[:, :half]
        total[1, at, :] = grad[:, half:]
    for rel in range(dp):
        at = pl.ds(pl.multiple_of((d ^ rel) * rows, rows), rows)
        keep_ref[rel] = total[s, at, :].astype(BF)
        send_ref[rel] = total[1 - s, at, :].astype(BF)


def attend_back_kernel(meta, q_ref, k_ref, v_ref, e_ref, inv_ref, own_ref, oth_ref, grad_ref, off_ref, diag, dctx, table, low):
    s = meta[0]
    nseq, length, width = q_ref.shape
    half = length // 2
    step = LANES
    rows = step // 4
    span = diag.shape[-1]
    zero = jnp.zeros((), BF)
    first = lane_half((length, LANES), 0)
    for hp in range(width // LANES):
        lanes = slice(hp * LANES, (hp + 1) * LANES)
        diag[...] = jnp.zeros_like(diag)
        for n in range(nseq):
            q, k, v, inv = (ref[n, :, lanes] for ref in (q_ref, k_ref, v_ref, inv_ref))
            dctx[pl.ds(pl.multiple_of(s * half, half), half), :] = own_ref[n, :, lanes]
            dctx[pl.ds(pl.multiple_of((1 - s) * half, half), half), :] = oth_ref[n, :, lanes]
            scaled = (dctx[...].astype(F32) * inv).astype(BF)
            for hh in range(2):
                table[hh] = nt(jnp.where(first if hh == 0 else ~first, scaled, zero), v)
            q_t, c_t = q.astype(F32).T.astype(BF), scaled.astype(F32).T.astype(BF)
            dq, dk, dv = [], [], []
            for hh in range(2):
                lane = hh * HEAD_DIM
                for at in range(0, length, rows):
                    base, within = length - step - at // step * step, at % step
                    e = e_ref[n, hp, hh, at : at + rows, :].astype(F32)
                    term = e * table[hh, at : at + rows]
                    delta = jnp.sum(term, axis=-1, keepdims=True) * inv[at : at + rows, lane : lane + 1]
                    grad = term - e * delta
                    diag[hh, within : within + rows, base : base + length] += grad
                    low[hh, at : at + rows] = grad.astype(BF)
                grad_low = low[hh]
                dq.append(nn(grad_low, jnp.where(first if hh == 0 else ~first, k, zero)))
                dk.append(nn(q_t[lane : lane + HEAD_DIM], grad_low))
                dv.append(nn(c_t[lane : lane + HEAD_DIM], e_ref[n, hp, hh]))
            dk, dv = (jnp.concatenate(x, axis=0).T for x in (dk, dv))
            for c, x in enumerate((dq[0] + dq[1], dk, dv)):
                grad_ref[n, :, c * width + hp * LANES : c * width + (hp + 1) * LANES] = x.astype(BF)
        for hh in range(2):
            acc = jnp.zeros((8, span), F32)
            for g in range(step // 8):
                part = diag[hh, 8 * g : 8 * g + 8, :]
                shift = step - 8 - 8 * g
                acc = acc + (pltpu.roll(part, shift, 1) if shift else part)
            out = acc[7:8]
            for b in range(7):
                out = out + pltpu.roll(acc[b : b + 1], 7 - b, 1)
            off_ref[2 * hp + hh : 2 * hp + hh + 1, :] = out
    off_ref[width // HEAD_DIM :, :] = jnp.zeros((off_ref.shape[0] - width // HEAD_DIM, span), F32)


def qkv_grad_kernel(meta, norm_ref, grad_ref, off_ref, buckets, hsel, bsel, *rest, rows, cut, dp):
    s = meta[0]
    three = grad_ref.shape[-1]
    a = norm_ref[...].reshape(-1, norm_ref.shape[-1])
    total = rest[0] if dp == 0 else rest[-1]
    total[:, :three] = tn(a, grad_ref[...].reshape(a.shape[0], three)).astype(BF)
    one_hot = (
        lax.broadcasted_iota(jnp.int32, (LANES, buckets.shape[1]), 0) == buckets[...]
    ).astype(F32)
    per_bucket = lax.dot_general(
        off_ref[...], one_hot, (((1,), (1,)), ((), ())), precision=lax.Precision.HIGHEST, preferred_element_type=F32
    )
    spread = lax.dot_general(
        hsel[s], per_bucket, (((0,), (0,)), ((), ())), precision=lax.Precision.HIGHEST, preferred_element_type=F32
    )
    column = jnp.sum(spread * bsel[...], axis=-1, keepdims=True)
    total[:, three:] = jnp.broadcast_to(column, (column.shape[0], LANES)).astype(BF)
    if dp:
        store_relative(meta, total, *rest[:4], rows, cut, dp)


def input_grad_kernel(meta, grad_ref, w, own_ref, oth_ref):
    s = meta[0]
    three = grad_ref.shape[-1]
    count = own_ref.shape[1]
    for side, ref in ((0, own_ref), (1, oth_ref)):
        at = pl.ds(pl.multiple_of((s if side == 0 else 1 - s) * count, count), count)
        ref[0] = nt(grad_ref[0, at, :], w[:, :three]).astype(ref.dtype)


def layer_out_kernel(mid_ref, own_ref, oth_ref, out_ref):
    out_ref[0] = (mid_ref[0] + own_ref[0] + oth_ref[0].astype(F32)).astype(BF)


def last_kernel(x_ref, gm_ref, own_ref, oth_ref, misc, out_ref):
    x = x_ref[0].astype(F32)
    scale = lax.rsqrt(jnp.mean(x * x, axis=-1, keepdims=True) + EPSILON)
    scaled = (own_ref[0] + oth_ref[0].astype(F32)) * misc[0:1, :]
    inner = jnp.mean(scaled * x, axis=-1, keepdims=True)
    out_ref[0] = (gm_ref[0] + scale * scaled - x * (scale * scale * scale) * inner).astype(BF)


def finish_kernel(meta, mine_ref, oth_ref, wq_ref, wk_ref, wv_ref, gain_ref, gq_ref, gk_ref, gv_ref, gain_out, bias_out, square, *, dp, table_rows):
    s, d = meta[0], meta[1]
    shard = mine_ref.shape[0]
    width = wq_ref.shape[1]
    half = width // 2
    mine, oth = mine_ref[...].astype(F32), oth_ref[...].astype(F32)
    low, top = jnp.where(s == 0, mine, oth), jnp.where(s == 0, oth, mine)
    total = jnp.zeros((shard, 1), F32)
    for c, (w_ref, out) in enumerate(((wq_ref, gq_ref), (wk_ref, gk_ref), (wv_ref, gv_ref))):
        grad = jnp.concatenate([x[:, c * half : (c + 1) * half] for x in (low, top)], axis=1)
        out[...] = grad
        total = total + jnp.sum(w_ref[...].astype(F32) * grad, axis=1, keepdims=True)
    lane = lax.broadcasted_iota(jnp.int32, (shard, LANES), 1)
    bias = jnp.where(2 * d < dp, low[:, 3 * half :], top[:, 3 * half :])
    square[...] = jnp.zeros_like(square)
    square[:shard, :] = jnp.where(lane == 0, total, bias)
    turned = square[...].T
    gain_out[...] = turned[0:1, :shard] / gain_ref[...].astype(F32)
    bias_out[...] = turned[1:2, :table_rows]


def finish_in_kernel(meta, mine_ref, oth_ref, w_ref, gain_ref, in_ref, out_ref, gain_out, square, *, in_cut, wo_cut, hid_rows, dp):
    s = meta[0]
    shard = mine_ref.shape[0]
    hid = hid_rows * dp
    mine, oth = mine_ref[...].astype(F32), oth_ref[...].astype(F32)
    halves = jnp.where(s == 0, mine, oth), jnp.where(s == 0, oth, mine)
    for c in range(dp):
        at = c * hid_rows
        at = at if at < in_cut else at + wo_cut
        for core, half in enumerate(halves):
            to = (2 * c + core) * hid_rows
            in_ref[:, to : to + hid_rows] = half[:, at : at + hid_rows]
    parts = [x[:, cut] for x in halves for cut in (slice(in_cut, in_cut + wo_cut), slice(hid + wo_cut, None))]
    out_ref[...] = jnp.concatenate(parts, axis=1)
    total = jnp.sum(w_ref[...].astype(F32) * in_ref[...], axis=1, keepdims=True)
    square[...] = jnp.zeros_like(square)
    square[:shard, :] = jnp.broadcast_to(total, (shard, LANES))
    gain_out[...] = square[...].T[0:1, :shard] / gain_ref[...].astype(F32)


def body(
    layer_input,
    gain_attn,
    w_query,
    w_key,
    w_value,
    w_output,
    bias_table,
    gain_ffn,
    ffn_in,
    ffn_out,
    buckets,
    keep_mask,
    out_grad,
):
    dp = lax.axis_size("dp")
    s = lax.axis_index("seq")
    d = lax.axis_index("dp")
    nseq, count, width = layer_input.shape
    length = 2 * count
    span = 2 * length
    half = width // 2
    shard = w_query.shape[0]
    rows = 2 * shard
    hid_rows = ffn_out.shape[0]
    hid = hid_rows * dp
    table_rows = bias_table.shape[0]
    tok = nseq * length
    pairs = half // LANES
    meta = jnp.stack([s, d]).astype(jnp.int32)
    aligned = rows % 16 == 0 and hid_rows % 16 == 0

    def sds(shape, dtype=BF):
        return jax.ShapeDtypeStruct(shape, dtype)

    def far(shape, dtype=BF):
        return pltpu.HBM(shape, dtype)

    def first_columns(h):
        cut = [lax.dynamic_slice_in_dim(w, h * half, half, 1) for w in (w_query, w_key, w_value)]
        table = jnp.pad(bias_table, (0, shard - table_rows))
        extra = jnp.stack([gain_attn, gain_ffn, table], axis=1)
        return jnp.concatenate(cut + [jnp.pad(extra, ((0, 0), (0, LANES - 3)))], axis=1)

    def swapped(mine, theirs):
        theirs = other_core(theirs)
        return jnp.where(s == 0, jnp.concatenate([mine, theirs]), jnp.concatenate([theirs, mine]))

    first_cols = 3 * half + LANES
    second_cols = half + hid
    first_cut = (first_cols // LANES // 2) * LANES
    second_cut = (second_cols // LANES // 2) * LANES
    third_cut = (width // LANES // 2) * LANES

    first = Gather(swapped(first_columns(s), first_columns(1 - s)), first_cut, dp)
    first.high()
    x_oth = other_core(after(layer_input, first.have))
    second_block = swapped(
        *small(
            functools.partial(second_kernel, hid_rows=hid_rows, dp=dp),
            (meta, w_output, ffn_in),
            [(shard, second_cols)] * 2,
            "second_columns",
        )
    )
    x_oth, second_block = meet((x_oth, second_block), (first, "have got"))
    second = Gather(second_block, second_cut, dp)
    first.first()
    second.begin()
    meet((), (first, "left right left_x right_y"), (second, "near"))
    first.second()
    second.high()
    g_oth = other_core(out_grad)
    keep_oth = other_core(keep_mask.astype(BF))
    keep = keep_mask.astype(BF)
    keep = jnp.where(s == 0, jnp.concatenate([keep, keep_oth], 1), jnp.concatenate([keep_oth, keep], 1))
    mask = ((keep.astype(F32) - 1.0) * 1e9)[:, None, :]
    g_both = jnp.concatenate([out_grad, g_oth], axis=1)

    high = dp // 4
    orders = [np.array([(h << 2) | low for low in lows for h in range(high)], np.int32) for lows in ((0, 1, 2, 3), (0, 2, 1, 3))]
    pos_l, pos_r = ((d ^ jnp.asarray(order)).astype(jnp.int32) for order in orders)
    pos = pos_l

    def settle(pieces, places=pos_l):
        if aligned:
            return pieces
        every = jnp.concatenate(pieces, axis=0)
        order = jnp.argsort(places)
        return [every[order].reshape(1, -1, every.shape[-1])]

    def settle_both(gather):
        left, right = gather.pieces()
        return settle(left), settle(right, pos_r)

    if not aligned:
        pos_k, rows_k, hid_rows_k, nblk, dp_k = jnp.zeros((2, 1), jnp.int32), width, hid, 1, 1
    else:
        pos_k, rows_k, hid_rows_k, nblk, dp_k = jnp.stack([pos_l, pos_r]), rows, hid_rows, dp, dp

    feature = np.arange(width)
    chunk, within = feature // rows, feature % rows
    entry = np.where(within % shard < table_rows, table_rows * chunk + within % shard, -1)
    head, bucket = entry // BUCKETS, entry % BUCKETS
    half_heads = HEADS // 2
    hsel = np.zeros((2, 8, width), np.float32)
    bsel = np.zeros((width, LANES), np.float32)
    for f in range(width):
        if entry[f] >= 0:
            hsel[head[f] // half_heads, head[f] % half_heads, f] = 1.0
            bsel[f, bucket[f]] = 1.0
    bsel_once = jnp.asarray(np.where(within[:, None] < shard, bsel, 0.0))
    hsel, bsel = jnp.asarray(hsel), jnp.asarray(bsel)
    padded = jnp.concatenate([buckets, jnp.full((span - buckets.shape[0],), -1, jnp.int32)])[None]

    seq_block = lambda shape: pl.BlockSpec((1,) + shape, lambda n: (n, 0, 0))
    VMEM = pl.BlockSpec(memory_space=pltpu.VMEM)
    rel = dp if aligned else 0

    def block_shapes(block_rows, cut, cols):
        if aligned:
            left, right = (2, high, block_rows, cut), (2, high, block_rows, cols - cut)
            return [left, left, right, right]
        return [(dp * block_rows, cols)]

    def in_relative(parts, block_rows, cut):
        if aligned:
            return parts
        blocks = parts[0].reshape(dp, block_rows, -1)[pos_l].reshape(2, 2, high, block_rows, -1)
        left, right = blocks[..., :cut], blocks[..., cut:]
        return left[1], left[0], right[:, 1], right[:, 0]

    def gradient(kernel, inputs, block_rows, cut, cols, name, earlier=()):
        shapes = block_shapes(block_rows, cut, cols)

        def ordered(meta_ref, *refs):
            kernel(meta_ref, *refs[len(earlier) :], rows=block_rows, cut=cut, dp=rel)

        parts = pl.pallas_call(
            ordered,
            in_specs=[SMEM] + [ANY] * len(earlier) + [VMEM] * len(inputs),
            out_specs=[VMEM] * len(shapes),
            out_shape=[sds(x) for x in shapes],
            scratch_shapes=[pltpu.VMEM((dp * block_rows, cols), BF)] if aligned else [],
            compiler_params=params(10),
            name=name,
            cost_estimate=cost(name),
        )(meta, *earlier, *inputs)
        return in_relative(parts, block_rows, cut)

    x_oth, ffn_out, mask, g_both = meet(
        (x_oth, ffn_out, mask, g_both), (first, "left right left_far right_far"), (second, "have got")
    )
    second.first()
    third = Gather(ffn_out, third_cut, dp)
    left, right = settle_both(first)
    q, k, v, normed_attn, misc, peroff, w_qkv = pl.pallas_call(
        functools.partial(qkv_kernel, rows=rows_k, cut=first_cut, width=width, nl=len(left), nr=len(right)),
        grid=(nseq,),
        in_specs=[SMEM, SMEM, seq_block((count, width)), seq_block((count, width)), whole((1, span)), whole(hsel.shape), whole(bsel.shape)]
        + [whole(x.shape) for x in left + right],
        out_specs=[seq_block((length, half))] * 3 + [seq_block((length, width)), whole((8, width)), whole((8, span)), ANY],
        out_shape=[sds((nseq, length, half))] * 3
        + [far((nseq, length, width)), sds((8, width), F32), sds((8, span), F32), far((width, first_cols))],
        scratch_shapes=[pltpu.VMEM((width, first_cols), BF), pltpu.SemaphoreType.DMA],
        compiler_params=params(8),
        name="qkv",
        cost_estimate=cost("qkv"),
    )(meta, pos_k, layer_input, x_oth, padded, hsel, bsel_once, *left, *right)

    q, k, v = meet((q, k, v), (second, "left right left_x right_y"))
    second.second()
    third.high()
    ctx_own, ctx_send, expo, inv = pl.pallas_call(
        attend_kernel,
        in_specs=[SMEM] + [VMEM] * 5,
        out_specs=[VMEM, VMEM, ANY, ANY],
        out_shape=[
            sds((nseq, count, half)),
            sds((nseq, count, half)),
            far((nseq, pairs, 2, length, length)),
            far((nseq, length, half), F32),
        ],
        scratch_shapes=[
            pltpu.VMEM((half_heads, LANES, span), F32),
            pltpu.VMEM((length, LANES), BF),
            pltpu.VMEM((2, length, length), F32),
            pltpu.VMEM((3, 2, length, length), BF),
            pltpu.VMEM((3, length, LANES), F32),
            pltpu.SemaphoreType.DMA((3,)),
            pltpu.SemaphoreType.DMA((3,)),
        ],
        compiler_params=params(12),
        name="attend",
        cost_estimate=cost("attend"),
    )(meta, q, k, v, mask, peroff)

    ctx_own, ctx_send = meet((ctx_own, ctx_send), (second, "left right left_far right_far"), (third, "have got"))
    ctx_oth = other_core(ctx_send)
    wo_own = stack(second.pieces()[0], half, "output_columns")[0]
    wo_oth = other_core(wo_own)
    third.first()
    wo_own, wo_oth = settle([wo_own])[0], settle([wo_oth])[0]
    middle, normed_own, w_o = pl.pallas_call(
        functools.partial(middle_kernel, rows=rows_k),
        in_specs=[SMEM, SMEM] + [VMEM] * 6,
        out_specs=[ANY, VMEM, ANY],
        out_shape=[far((nseq, count, width), F32), sds((nseq, count, width)), far((2, width, half))],
        scratch_shapes=[
            pltpu.VMEM((2, width, half), BF),
            pltpu.VMEM((nseq, count, width), F32),
            pltpu.SemaphoreType.DMA,
            pltpu.SemaphoreType.DMA((nseq,)),
        ],
        compiler_params=params(8),
        name="middle",
        cost_estimate=cost("middle"),
    )(meta, pos_k, layer_input, ctx_own, ctx_oth, misc, wo_own, wo_oth)

    middle, normed_own = meet((middle, normed_own), (third, "left right left_x right_y"))
    third.second()
    normed_oth = other_core(normed_own)
    left, right = settle_both(second)
    act, slope, w_in = pl.pallas_call(
        functools.partial(hidden_kernel, rows=rows_k, skip=half, cut=second_cut, nl=len(left), nr=len(right)),
        grid=(nseq,),
        in_specs=[SMEM, seq_block((count, width)), seq_block((count, width))] + [whole(x.shape) for x in left + right],
        out_specs=[seq_block((length, hid)), seq_block((length, hid)), whole((width, hid))],
        out_shape=[sds((nseq, length, hid)), sds((nseq, length, hid)), sds((width, hid))],
        compiler_params=params(),
        name="hidden",
        cost_estimate=cost("hidden"),
    )(pos_k, normed_own, normed_oth, *left, *right)
    out_parts = gradient(wgrad_kernel, (act, g_both), hid_rows, third_cut, width, "grad_ffn_out")

    out_parts, slope, act = meet((out_parts, slope, act), (third, "left right left_far right_far"))
    out_sum = Scatter(out_parts, dp, 1)
    out_sum.first()
    left, right = settle_both(third)
    seq_half = seq_block((count, width))
    grad_pre, back_own, back_send, out_own, out_send = pl.pallas_call(
        functools.partial(ffn_back_kernel, rows=hid_rows_k, cut=third_cut, nl=len(left), nr=len(right)),
        grid=(nseq,),
        in_specs=[SMEM, seq_block((length, width)), seq_block((length, hid)), seq_block((length, hid)), whole((width, hid))]
        + [whole(x.shape) for x in left + right],
        out_specs=[seq_block((length, hid))] + [seq_half] * 4,
        out_shape=[sds((nseq, length, hid)), sds((nseq, count, width), F32), sds((nseq, count, width))]
        + [far((nseq, count, width), F32), far((nseq, count, width))],
        scratch_shapes=[pltpu.VMEM((hid, width), BF)],
        input_output_aliases={3: 0},
        compiler_params=params(8),
        name="ffn_back",
        cost_estimate=cost("ffn_back"),
    )(pos_k, g_both, act, slope, w_in, *left, *right)

    grad_pre, back_own, back_send, out_own, out_send = meet(
        (grad_pre, back_own, back_send, out_own, out_send), (out_sum, "left_got right_got")
    )
    out_sum.second()
    back_oth, out_oth = other_core(back_send), other_core(out_send)
    in_cut = (hid // LANES // 2) * LANES
    in_parts = gradient(
        functools.partial(wgrad_kernel, na=2),
        (normed_own, normed_oth, grad_pre),
        rows,
        in_cut,
        hid,
        "grad_ffn_in",
        (out_sum.left_send, out_sum.right_send),
    )

    in_parts, back_own, back_oth, out_oth = meet(
        (in_parts, back_own, back_oth, out_oth), (out_sum, "left_got right_got")
    )
    grad_middle, middle_low, dctx_own, dctx_send = pl.pallas_call(
        middle_back_kernel,
        grid=(nseq,),
        in_specs=[SMEM] + [seq_block((count, width))] * 4 + [whole((8, width)), whole((2, width, half))],
        out_specs=[seq_block((count, width)), seq_block((count, width)), seq_block((count, half)), seq_block((count, half))],
        out_shape=[
            far((nseq, count, width), F32),
            sds((nseq, count, width)),
            sds((nseq, count, half)),
            sds((nseq, count, half)),
        ],
        compiler_params=params(8),
        name="middle_back",
        cost_estimate=cost("middle_back"),
    )(meta, out_grad, middle, back_own, back_oth, misc, w_o)
    dctx_oth = other_core(dctx_send)
    rel_meta = meta if aligned else jnp.stack([s, jnp.zeros_like(d)]).astype(jnp.int32)
    wo_keep, wo_send = pl.pallas_call(
        functools.partial(wo_grad_kernel, rows=rows_k, dp=dp_k),
        out_shape=[sds((dp_k, rows_k, half))] * 2,
        in_specs=[SMEM] + [VMEM] * 3,
        out_specs=[VMEM] * 2,
        scratch_shapes=[pltpu.VMEM((2, width, half), F32)],
        compiler_params=params(),
        name="grad_output",
        cost_estimate=cost("grad_output"),
    )(rel_meta, ctx_own, ctx_oth, middle_low)
    wo_got = other_core(wo_send)
    if not aligned:
        wo_keep, wo_got = (x.reshape(dp, rows, half)[d ^ jnp.arange(dp)] for x in (wo_keep, wo_got))
    wo_cut = (half // LANES // 2) * LANES

    wo_keep, wo_got, dctx_own, dctx_oth = meet((wo_keep, wo_got, dctx_own, dctx_oth))
    out_sum.high()
    in_sum = Scatter(with_output_columns(in_parts, wo_keep, wo_got, wo_cut), dp)
    in_sum.first()
    dqkv, off = pl.pallas_call(
        attend_back_kernel,
        in_specs=[SMEM] + [VMEM] * 7,
        out_specs=[VMEM] * 2,
        out_shape=[sds((nseq, length, 3 * half)), sds((8, span), F32)],
        scratch_shapes=[
            pltpu.VMEM((2, LANES, span), F32),
            pltpu.VMEM((length, LANES), BF),
            pltpu.VMEM((2, length, length), F32),
            pltpu.VMEM((2, length, length), BF),
        ],
        compiler_params=params(8),
        name="attend_back",
        cost_estimate=cost("attend_back"),
    )(meta, q, k, v, expo, inv, dctx_own, dctx_oth)
    dqkv, off = meet((dqkv, off), (out_sum, "got"), (in_sum, "left_got right_got"))
    in_sum.second()
    qkv_parts = gradient(
        qkv_grad_kernel,
        (normed_attn, dqkv, off, padded, hsel, bsel),
        rows,
        first_cut,
        first_cols,
        "grad_qkv",
        (in_sum.left_send, in_sum.right_send),
    )

    qkv_parts, dqkv, w_qkv = meet((qkv_parts, dqkv, w_qkv))
    qkv_sum = Scatter(qkv_parts, dp)
    qkv_sum.first()
    in_sum.high()
    dn_own, dn_send = pl.pallas_call(
        input_grad_kernel,
        grid=(nseq,),
        in_specs=[SMEM, seq_block((length, 3 * half)), whole((width, first_cols))],
        out_specs=[seq_half] * 2,
        out_shape=[far((nseq, count, width), F32), sds((nseq, count, width))],
        compiler_params=params(8),
        name="input_grad",
        cost_estimate=cost("input_grad"),
    )(meta, dqkv, w_qkv)
    dn_own, dn_send, in_sum.got[:2] = meet((dn_own, dn_send, in_sum.got[:2]), (qkv_sum, "left_got right_got"))
    qkv_sum.second()
    dn_oth = other_core(dn_send)
    kept = [grad_middle, dn_own] + [pltpu.with_memory_space_constraint(x, pltpu.HBM) for x in (middle, out_own, out_oth)]
    grad_input = pl.pallas_call(
        last_kernel,
        grid=(nseq,),
        in_specs=[seq_half] * 4 + [whole((8, width))],
        out_specs=seq_half,
        out_shape=sds((nseq, count, width)),
        compiler_params=params(10),
        name="last",
        cost_estimate=cost("last"),
    )(layer_input, *kept[:2], dn_oth, misc)
    grad_input, kept = meet((grad_input, kept), (qkv_sum, "left_got right_got"))
    qkv_sum.high()
    grad_ffn_out = out_sum.rest(F32)
    layer_out = pl.pallas_call(
        layer_out_kernel,
        grid=(nseq,),
        in_specs=[seq_half] * 3,
        out_specs=seq_half,
        out_shape=sds((nseq, count, width)),
        compiler_params=params(10),
        name="layer_out",
        cost_estimate=cost("last"),
    )(*kept[2:])
    in_sum.got = after(in_sum.got, qkv_sum.left_got, qkv_sum.right_got)
    mine, theirs = in_sum.halves(meta, shard)
    theirs = other_core(theirs)
    grad_ffn_in, grad_output, gain_ffn_row = pl.pallas_call(
        functools.partial(finish_in_kernel, in_cut=in_cut, wo_cut=wo_cut, hid_rows=hid_rows, dp=dp),
        in_specs=[SMEM] + [VMEM] * 4,
        out_specs=[VMEM] * 3,
        out_shape=[sds((shard, 2 * hid), F32), sds((shard, width), F32), sds((1, shard), F32)],
        scratch_shapes=[pltpu.VMEM((LANES, LANES), F32)],
        compiler_params=params(),
        name="finish_in",
        cost_estimate=cost("finish"),
    )(meta, mine, theirs, ffn_in, gain_ffn[None])
    layer_out, grad_ffn_in, grad_output, gain_ffn_row, grad_ffn_out = meet(
        (layer_out, grad_ffn_in, grad_output, gain_ffn_row, grad_ffn_out), (qkv_sum, "got")
    )

    mine, theirs = qkv_sum.halves(meta, shard)
    theirs = other_core(theirs)
    grad_query, grad_key, grad_value, gain_row, bias_row = pl.pallas_call(
        functools.partial(finish_kernel, dp=dp, table_rows=table_rows),
        in_specs=[SMEM] + [VMEM] * 6,
        out_specs=[VMEM] * 5,
        out_shape=[sds((shard, width), F32)] * 3 + [sds((1, shard), F32), sds((1, table_rows), F32)],
        scratch_shapes=[pltpu.VMEM((LANES, LANES), F32)],
        compiler_params=params(),
        name="finish",
        cost_estimate=cost("finish"),
    )(meta, mine, theirs, w_query, w_key, w_value, gain_attn[None])
    return (
        layer_out,
        grad_input,
        gain_row.reshape(shard),
        grad_query,
        grad_key,
        grad_value,
        grad_output,
        bias_row.reshape(table_rows),
        gain_ffn_row.reshape(shard),
        grad_ffn_in,
        grad_ffn_out,
    )


def solution(mesh):
    both = ("dp", "seq")
    return jax.shard_map(
        body,
        mesh=mesh,
        in_specs=(
            P("dp", "seq", None),
            P(both),
            P(both, None),
            P(both, None),
            P(both, None),
            P(both, None),
            P("dp"),
            P(both),
            P(both, None),
            P(both, None),
            P(),
            P("dp", "seq"),
            P("dp", "seq", None),
        ),
        out_specs=(
            P("dp", "seq", None),
            P("dp", "seq", None),
            P(both),
            P(both, None),
            P(both, None),
            P(both, None),
            P(both, None),
            P("dp"),
            P(both),
            P(both, None),
            P(both, None),
        ),
        check_vma=False,
    )
```

```python
import functools
import math

import jax
import jax.numpy as jnp
import numpy as np
from jax import lax
from jax.experimental import pallas as pl
from jax.experimental.pallas import tpu as pltpu
from jax.sharding import PartitionSpec as P

HEADS = 12
HEAD_DIM = 64
BUCKETS = 32
EPSILON = 1e-06
LANES = 128
BF = jnp.bfloat16
F32 = jnp.float32
GELU_A = math.sqrt(2.0 / math.pi)
GELU_B = 0.044715

ANY = pl.BlockSpec(memory_space=pl.ANY)
SMEM = pl.BlockSpec(memory_space=pltpu.SMEM)
FAR = pl.BlockSpec(memory_space=pltpu.HBM)


def whole(shape):
    zeros = (0,) * len(shape)
    return pl.BlockSpec(shape, lambda *_: zeros)


def params(mib=6):
    return pltpu.CompilerParams(vmem_limit_bytes=mib * 1024 * 1024)


MICROS = {
    "qkv": 7, "attend": 10, "middle": 4, "hidden": 8, "grad_ffn_out": 5, "grad_ffn_in": 5, "ffn_back": 9, "ffn_out": 5,
    "middle_back": 4, "grad_output": 2, "attend_back": 14, "grad_qkv": 5, "input_grad": 5, "last": 3, "finish": 1,
}


def cost(name):
    return pl.CostEstimate(flops=int(MICROS[name] * 1e4), bytes_accessed=0, transcendentals=0)


def nn(a, b):
    return lax.dot_general(a, b, (((1,), (0,)), ((), ())), preferred_element_type=F32)


def nt(a, b):
    return lax.dot_general(a, b, (((1,), (1,)), ((), ())), preferred_element_type=F32)


def tn(a, b):
    return lax.dot_general(a, b, (((0,), (0,)), ((), ())), preferred_element_type=F32)


def flip(x, axis, bit, count):
    return lax.ppermute(x, axis, [(i, i ^ bit) for i in range(count)])


def after(values, *others):
    return lax.optimization_barrier((values, others))[0]


def meet(values, *fields):
    held = [[getattr(owner, name) for name in names.split()] for owner, names in fields]
    values, held = lax.optimization_barrier((values, held))
    for (owner, names), got in zip(fields, held):
        for name, value in zip(names.split(), got):
            setattr(owner, name, value)
    return values


def bit_groups(dp, most=2):
    bits, groups = dp.bit_length() - 3, []
    at = 2
    while bits > 0:
        groups.append((1 << at, 1 << min(bits, most)))
        at, bits = at + most, bits - most
    return groups


def small(kernel, inputs, shapes, name, dtype=BF):
    return pl.pallas_call(
        kernel,
        in_specs=[SMEM if x.ndim == 1 else pl.BlockSpec(memory_space=pltpu.VMEM) for x in inputs],
        out_specs=[pl.BlockSpec(memory_space=pltpu.VMEM)] * len(shapes),
        out_shape=[jax.ShapeDtypeStruct(x, dtype) for x in shapes],
        compiler_params=params(),
        name=name,
        cost_estimate=pl.CostEstimate(flops=10**4, bytes_accessed=0, transcendentals=0),
    )(*inputs)


def total_of(refs, at, dtype=BF):
    return functools.reduce(lambda x, y: x + y, (ref[at].astype(F32) for ref in refs)).astype(dtype)


def merge(sides, size, joined, name, dtype=BF):
    counts = [len(side) for side in sides]
    k, rows, _ = sides[0][0].shape
    widths = [side[0].shape[2] for side in sides]
    part = k // size
    shapes = [(part, rows, sum(widths))] * size if joined else [(part, rows, w) for w in widths for _ in range(size)]

    def kernel(*refs):
        ins, outs = refs[: sum(counts)], refs[sum(counts) :]
        at, lane = 0, 0
        for i, (count, width) in enumerate(zip(counts, widths)):
            for j in range(k):
                out = outs[j // part] if joined else outs[i * size + j // part]
                out[j % part, :, lane : lane + width] = total_of(ins[at : at + count], j, dtype)
            at += count
            lane = lane + width if joined else 0

    return small(kernel, [x for side in sides for x in side], shapes, name, dtype)


def either(meta, near, mid, name):
    def kernel(meta_ref, near_ref, mid_ref, down, up):
        place_z = meta_ref[1] >> 2
        down[...] = jnp.where(place_z == 1, mid_ref[...], near_ref[...])
        up[...] = jnp.where(place_z == 2, mid_ref[...], near_ref[...])

    return small(kernel, (meta, near, mid), [near.shape] * 2, name)


def stack_line(meta, have, near, mid, down, up, far, cut, name):
    _, rows, cols = have.shape

    def kernel(meta_ref, have_ref, near_ref, mid_ref, down_ref, up_ref, far_ref, left, right):
        place_z = meta_ref[1] >> 2
        inner = jnp.logical_or(place_z == 1, place_z == 2)
        blocks = (
            have_ref[0],
            near_ref[0],
            jnp.where(place_z < 2, down_ref[0], up_ref[0]),
            jnp.where(inner, mid_ref[0], far_ref[0]),
        )
        for i, block in enumerate(blocks):
            left[i] = block[:, :cut]
            right[i] = block[:, cut:]

    return small(kernel, (meta, have, near, mid, down, up, far), [(4, rows, cut), (4, rows, cols - cut)], name)


def stack(pieces, cut, name):
    ks = [x.shape[0] for x in pieces]
    rows, cols = pieces[0].shape[1:]

    def kernel(*refs):
        left, right = refs[len(ks) :]
        at = 0
        for ref, k in zip(refs, ks):
            left[at : at + k] = ref[:, :, :cut]
            right[at : at + k] = ref[:, :, cut:]
            at += k

    return small(kernel, pieces, [(sum(ks), rows, cut), (sum(ks), rows, cols - cut)], name)


def pair_up(a, b, c, d, name):
    k = a.shape[0]

    def kernel(a_ref, b_ref, c_ref, d_ref, ab, cd):
        ab[:k], ab[k:] = a_ref[...], b_ref[...]
        cd[:k], cd[k:] = c_ref[...], d_ref[...]

    return small(kernel, (a, b, c, d), [(2 * k,) + a.shape[1:], (2 * k,) + c.shape[1:]], name)


def with_output_columns(parts, keep, got, cut):
    count, _, half = keep.shape
    widths = [x.shape[-1] for x in parts]
    extra = (cut, cut, half - cut, half - cut)
    shapes = [x.shape[:-1] + (w + more,) for x, w, more in zip(parts, widths, extra)]

    def kernel(*refs):
        ins, keep_ref, got_ref, outs = refs[:4], refs[4], refs[5], refs[6:]
        for ref, out, w in zip(ins, outs, widths):
            out[..., :w] = ref[...]
        for rel in range(count):
            x, y, high = rel & 1, (rel >> 1) & 1, rel >> 2
            block = total_of((keep_ref, got_ref), rel)
            i = 0 if y else 1
            outs[i][x, high, :, widths[i] :] = block[:, :cut]
            i = 2 if x else 3
            outs[i][y, high, :, widths[i] :] = block[:, cut:]

    return small(kernel, (*parts, keep, got), shapes, "output_parts")


class Gather:
    def __init__(self, block, cut, dp):
        self.have, self.cut, self.dp = block[None], cut, dp
        self.near = None

    def begin(self):
        self.near = flip(self.have, "dp", 4, self.dp)

    def high(self):
        self.got = []
        groups = bit_groups(self.dp)
        for i, (bit, size) in enumerate(groups):
            first = [self.near] if bit == 4 and self.near is not None else [flip(self.have, "dp", bit, self.dp)]
            self.got = first + [flip(self.have, "dp", bit * k, self.dp) for k in range(2, size)]
            if i + 1 < len(groups):
                self.have = jnp.concatenate([self.have] + self.got, axis=0)

    def first(self):
        self.left, self.right = stack([self.have] + self.got, self.cut, "stack")
        self.left_x = flip(self.left, "dp", 1, self.dp)
        self.right_y = flip(self.right, "dp", 2, self.dp)

    def second(self):
        self.left, self.right = pair_up(self.left, self.left_x, self.right, self.right_y, "pair_up")
        self.left_far = flip(self.left, "dp", 2, self.dp)
        self.right_far = flip(self.right, "dp", 1, self.dp)

    def pieces(self):
        return [self.left, self.left_far], [self.right, self.right_far]


class LineGather(Gather):
    def __init__(self, block, cut, dp, meta):
        super().__init__(block, cut, dp)
        self.meta = meta

    def along(self, x, pairs):
        return lax.ppermute(x, "dp", [(4 * a + low, 4 * b + low) for a, b in pairs for low in range(4)])

    def begin(self):
        self.near = flip(self.have, "dp", 4, self.dp)
        self.mid = self.along(self.have, ((1, 2), (2, 1)))

    def high(self):
        down, up = either(self.meta, self.near, self.mid, "either")
        self.got = [
            self.along(down, ((1, 0), (2, 1))),
            self.along(up, ((2, 3), (1, 2))),
            self.along(self.near, ((2, 0), (1, 3))),
        ]

    def first(self):
        self.left, self.right = stack_line(
            self.meta, self.have, self.near, self.mid, *self.got, self.cut, "stack_line"
        )
        self.left_x = flip(self.left, "dp", 1, self.dp)
        self.right_y = flip(self.right, "dp", 2, self.dp)


class Scatter:
    def __init__(self, parts, dp, most=2):
        flat = [x.reshape((-1,) + x.shape[2:]) for x in parts]
        self.left_send, self.left_keep, self.right_send, self.right_keep = flat
        self.dp, self.groups = dp, bit_groups(dp, most)

    def first(self):
        self.left_got = flip(self.left_send, "dp", 2, self.dp)
        self.right_got = flip(self.right_send, "dp", 1, self.dp)

    def second(self):
        self.left, self.left_send, self.right, self.right_send = merge(
            [[self.left_keep, self.left_got], [self.right_keep, self.right_got]], 2, False, "add_second"
        )
        self.left_got = flip(self.left_send, "dp", 1, self.dp)
        self.right_got = flip(self.right_send, "dp", 2, self.dp)

    def spread(self, sides):
        bit, size = self.groups.pop()
        self.keep, *parts = merge(sides, size, True, "add_high")
        self.got = [flip(x, "dp", bit * (k + 1), self.dp) for k, x in enumerate(parts)]

    def high(self):
        self.spread([[self.left, self.left_got], [self.right, self.right_got]])

    def halves(self, meta, shard):
        while self.groups:
            self.spread([[self.keep] + self.got])
        terms = [self.keep] + self.got

        def kernel(meta_ref, *refs):
            ins, (mine, theirs) = refs[:-2], refs[-2:]
            total = functools.reduce(lambda x, y: x + y, (ref[0].astype(F32) for ref in ins))
            low, top = total[:shard], total[shard:]
            mine[...] = jnp.where(meta_ref[0] == 0, low, top).astype(BF)
            theirs[...] = jnp.where(meta_ref[0] == 0, top, low).astype(BF)

        return small(kernel, [meta] + terms, [(shard, terms[0].shape[-1])] * 2, "halves")

    def rest(self, dtype=BF):
        while self.groups:
            self.spread([[self.keep] + self.got])
        return merge([[self.keep] + self.got], 1, True, "add_last", dtype)[0][0]


def other_core(x):
    return lax.ppermute(x, "seq", [(0, 1), (1, 0)])


def place(refs, pos, side, rows, dst, lane, skip=0):
    at = 0
    for ref in refs:
        cols = ref.shape[2] - skip
        for b in range(ref.shape[0]):
            row = pl.multiple_of(pos[side, at] * rows, rows)
            dst[pl.ds(row, rows), lane : lane + cols] = ref[b, :, skip:]
            at += 1


def second_kernel(meta, w_out, w_in, mine, theirs, *, hid_rows, dp):
    s = meta[0]
    half = w_out.shape[1] // 2
    low, top = w_out[:, :half], w_out[:, half:]
    mine[:, :half] = jnp.where(s == 0, low, top)
    theirs[:, :half] = jnp.where(s == 0, top, low)
    for c in range(dp):
        at, to = 2 * c * hid_rows, half + c * hid_rows
        low, top = w_in[:, at : at + hid_rows], w_in[:, at + hid_rows : at + 2 * hid_rows]
        mine[:, to : to + hid_rows] = jnp.where(s == 0, low, top)
        theirs[:, to : to + hid_rows] = jnp.where(s == 0, top, low)


def qkv_kernel(meta, pos, x_own, x_oth, buckets, hsel, bsel, *rest, rows, cut, width, nl, nr):
    left, right = rest[:nl], rest[nl : nl + nr]
    q_ref, k_ref, v_ref, norm_ref, misc, peroff, w_far, w, sem = rest[nl + nr :]
    s = meta[0]
    half = width // 2
    n = pl.program_id(0)
    copy = pltpu.make_async_copy(w, w_far, sem)

    @pl.when(n == 0)
    def _():
        place(left, pos, 0, rows, w, 0)
        place(right, pos, 1, rows, w, cut)
        copy.start()
        extra = w[:, 3 * half :].astype(F32)
        misc[...] = extra.T[:8]
        spread = (extra[:, 2:3] * bsel[...]).astype(BF)
        table = nn(hsel[s].astype(BF), spread)
        one_hot = (
            lax.broadcasted_iota(jnp.int32, (LANES, buckets.shape[1]), 0) == buckets[...]
        ).astype(F32)
        peroff[...] = nn(table.astype(BF), one_hot.astype(BF))

    gain = misc[0:1, :]
    count = x_own.shape[1]
    for side, x_ref in ((0, x_own), (1, x_oth)):
        x = x_ref[0].astype(F32)
        scale = lax.rsqrt(jnp.mean(x * x, axis=-1, keepdims=True) + EPSILON)
        normed = (x * scale * gain).astype(BF)
        at = pl.ds(pl.multiple_of((s if side == 0 else 1 - s) * count, count), count)
        norm_ref[0, at, :] = normed
        q_ref[0, at, :] = nn(normed, w[:, :half]).astype(BF)
        k_ref[0, at, :] = nn(normed, w[:, half : 2 * half]).astype(BF)
        v_ref[0, at, :] = nn(normed, w[:, 2 * half : 3 * half]).astype(BF)

    @pl.when(n == pl.num_programs(0) - 1)
    def _():
        copy.wait()


def lane_half(shape, which):
    lane = lax.broadcasted_iota(jnp.int32, shape, 1)
    return (lane < HEAD_DIM) if which == 0 else (lane >= HEAD_DIM)


def attend_kernel(meta, q_ref, k_ref, v_ref, mask_ref, peroff, own_ref, oth_ref, e_far, inv_far, grid, ctx, table, e_buf, inv_buf, sems, inv_sems):
    s = meta[0]
    nseq, length, width = q_ref.shape
    step = LANES
    rows = step // 2
    half = length // 2
    span = grid.shape[-1]
    zero, one = jnp.zeros((), BF), jnp.ones((), BF)
    first = lane_half((length, LANES), 0)
    heads = width // HEAD_DIM
    for h in range(heads):
        wide = jnp.broadcast_to(peroff[h : h + 1, :], (step, span))
        grid[h] = pltpu.roll(wide, span - step + 1, 1, stride=1, stride_axis=0)
    items = [(hp, n, hh) for hp in range(heads // 2) for n in range(nseq) for hh in range(2)]

    def product(i):
        hp, n, hh = items[i]
        lanes = slice(hp * LANES, (hp + 1) * LANES)
        head = jnp.where(first if hh == 0 else ~first, q_ref[n, :, lanes], zero)
        table[i % 2] = nt(head, k_ref[n, :, lanes])

    def stores(i):
        hp, n, _ = items[2 * i]
        inv_dst = inv_far.at[n, :, pl.ds(hp * LANES, LANES)]
        return (
            pltpu.make_async_copy(e_buf.at[i % 3], e_far.at[n, hp], sems.at[i % 3]),
            pltpu.make_async_copy(inv_buf.at[i % 3], inv_dst, inv_sems.at[i % 3]),
        )

    product(0)
    sums = [None, None]
    for i, (hp, n, hh) in enumerate(items):
        lanes = slice(hp * LANES, (hp + 1) * LANES)
        e_ref = e_buf.at[i // 2 % 3]
        if i + 1 < len(items):
            product(i + 1)
        if hh == 0 and i >= 6:
            for copy in stores(i // 2 - 3):
                copy.wait()
        for at in range(0, length, rows):
            base, within = length - step - at // step * step, at % step
            bias = grid[2 * hp + hh, within : within + rows, base : base + length]
            scores = table[i % 2, at : at + rows] + (bias + mask_ref[n])
            top = jnp.max(scores, axis=-1, keepdims=True)
            e_ref[hh, at : at + rows, :] = jnp.exp(scores - top).astype(BF)
        sums[hh] = nn(e_ref[hh], jnp.where(first if hh == 0 else ~first, v_ref[n, :, lanes], one))
        if hh == 1:
            num = jnp.where(first, sums[0], sums[1])
            den = pltpu.roll(jnp.where(first, sums[1], sums[0]), HEAD_DIM, 1)
            inv = 1.0 / den
            inv_buf[i // 2 % 3] = inv
            for copy in stores(i // 2):
                copy.start()
            ctx[...] = (num * inv).astype(BF)
            own_ref[n, :, lanes] = ctx[pl.ds(pl.multiple_of(s * half, half), half), :]
            oth_ref[n, :, lanes] = ctx[pl.ds(pl.multiple_of((1 - s) * half, half), half), :]
    for i in range(max(0, len(items) // 2 - 3), len(items) // 2):
        for copy in stores(i):
            copy.wait()


def middle_kernel(meta, pos, x_ref, own_ref, oth_ref, misc, own_w, oth_w, mid_far, norm_ref, w_far, w, mid, sem, mid_sems, *, rows):
    s = meta[0]
    half = w.shape[2]
    place([own_w], pos, 0, rows, w.at[s], 0)
    place([oth_w], pos, 0, rows, w.at[1 - s], 0)
    copy = pltpu.make_async_copy(w, w_far, sem)
    copy.start()
    at_own = pl.ds(pl.multiple_of(s * half, half), half)
    at_oth = pl.ds(pl.multiple_of((1 - s) * half, half), half)
    for n in range(x_ref.shape[0]):
        x = x_ref[n].astype(F32)
        parts = []
        for c in range(2):
            part = nn(own_ref[n], w[c, at_own, :]) + nn(oth_ref[n], w[c, at_oth, :])
            parts.append(x[:, c * half : (c + 1) * half] + part)
        middle = jnp.concatenate(parts, axis=-1)
        mid[n] = middle
        pltpu.make_async_copy(mid.at[n], mid_far.at[n], mid_sems.at[n]).start()
        scale = lax.rsqrt(jnp.mean(middle * middle, axis=-1, keepdims=True) + EPSILON)
        norm_ref[n] = (middle * scale * misc[1:2, :]).astype(BF)
    copy.wait()
    for n in range(x_ref.shape[0]):
        pltpu.make_async_copy(mid.at[n], mid_far.at[n], mid_sems.at[n]).wait()


def hidden_kernel(pos, own_ref, oth_ref, *rest, rows, skip, cut, nl, nr):
    left, right = rest[:nl], rest[nl : nl + nr]
    act_ref, slope_ref, w = rest[nl + nr :]

    @pl.when(pl.program_id(0) == 0)
    def _():
        place(left, pos, 0, rows, w, 0, skip)
        place(right, pos, 1, rows, w, cut - skip)

    count = own_ref.shape[1]
    width = w.shape[1]
    step = 768
    for side, ref in ((0, own_ref), (1, oth_ref)):
        at = slice(side * count, (side + 1) * count)
        for c in range(0, width, step):
            v = nn(ref[0], w[:, c : c + step])
            square = v * v
            p = 0.5 + 0.5 * jnp.tanh(v * (GELU_A + (GELU_A * GELU_B) * square))
            act = v * p
            slope = p + act * ((1.0 - p) * (2.0 * GELU_A + (6.0 * GELU_A * GELU_B) * square))
            act_ref[0, at, c : c + step] = act.astype(BF)
            slope_ref[0, at, c : c + step] = slope.astype(BF)


def wgrad_kernel(meta, *rest, rows, cut, dp, na=1):
    a_refs, b_ref, rest = rest[:na], rest[na], rest[na + 1 :]
    grad, at = 0.0, 0
    for a_ref in a_refs:
        a = a_ref[...].reshape(-1, a_ref.shape[-1])
        b = b_ref[:, at : at + a_ref.shape[1], :].reshape(a.shape[0], -1)
        grad, at = grad + tn(a, b), at + a_ref.shape[1]
    if dp == 0:
        rest[0][...] = grad.astype(BF)
    else:
        rest[-1][...] = grad.astype(BF)
        store_relative(meta, rest[-1], *rest[:4], rows, cut, dp)


def store_relative(meta, total, ls, lk, rs, rk, rows, cut, dp):
    d = meta[1]
    for rel in range(dp):
        x, y, high = rel & 1, (rel >> 1) & 1, rel >> 2
        at = pl.ds(pl.multiple_of((d ^ rel) * rows, rows), rows)
        (ls if y else lk)[x, high] = total[at, :cut]
        (rs if x else rk)[y, high] = total[at, cut:]


def ffn_back_kernel(pos, g_ref, act_ref, slope_ref, w_in, *rest, rows, cut, nl, nr):
    left, right = rest[:nl], rest[nl : nl + nr]
    pre_ref, own_ref, oth_ref, out_own, out_oth, w = rest[nl + nr :]

    @pl.when(pl.program_id(0) == 0)
    def _():
        place(left, pos, 0, rows, w, 0)
        place(right, pos, 1, rows, w, cut)

    count = own_ref.shape[1]
    width = w.shape[0]
    step = 512
    for c in range(0, width, step):
        grad = nt(g_ref[0], w[c : c + step, :])
        pre_ref[0, :, c : c + step] = (grad * slope_ref[0, :, c : c + step].astype(F32)).astype(BF)
    oth_ref[0] = nt(pre_ref[0, count:, :], w_in[...]).astype(BF)
    own_ref[0] = nt(pre_ref[0, :count, :], w_in[...])
    out_own[0] = nn(act_ref[0, :count, :], w[...])
    out_oth[0] = nn(act_ref[0, count:, :], w[...]).astype(BF)


def middle_back_kernel(meta, g_ref, mid_ref, own_ref, oth_ref, misc, w, gm_ref, low_ref, cown_ref, coth_ref):
    s = meta[0]
    half = w.shape[2]
    middle = mid_ref[0]
    scale = lax.rsqrt(jnp.mean(middle * middle, axis=-1, keepdims=True) + EPSILON)
    grad = own_ref[0] + oth_ref[0].astype(F32)
    scaled = grad * misc[1:2, :]
    inner = jnp.mean(scaled * middle, axis=-1, keepdims=True)
    grad_middle = g_ref[0].astype(F32) + scale * scaled - middle * (scale * scale * scale) * inner
    gm_ref[0] = grad_middle
    low = grad_middle.astype(BF)
    low_ref[0] = low
    for ref, which in ((cown_ref, s), (coth_ref, 1 - s)):
        at = pl.ds(pl.multiple_of(which * half, half), half)
        out = nt(low[:, :half], w[0, at, :]) + nt(low[:, half:], w[1, at, :])
        ref[0] = out.astype(BF)


def wo_grad_kernel(meta, own_ref, oth_ref, low_ref, keep_ref, send_ref, total, *, rows, dp):
    s, d = meta[0], meta[1]
    half = own_ref.shape[-1]
    low = low_ref[...].reshape(-1, low_ref.shape[-1])
    for ref, which in ((own_ref, s), (oth_ref, 1 - s)):
        at = pl.ds(pl.multiple_of(which * half, half), half)
        grad = tn(ref[...].reshape(low.shape[0], half), low)
        total[0, at, :] = grad[:, :half]
        total[1, at, :] = grad[:, half:]
    for rel in range(dp):
        at = pl.ds(pl.multiple_of((d ^ rel) * rows, rows), rows)
        keep_ref[rel] = total[s, at, :].astype(BF)
        send_ref[rel] = total[1 - s, at, :].astype(BF)


def attend_back_kernel(meta, q_ref, k_ref, v_ref, e_ref, inv_ref, own_ref, oth_ref, grad_ref, off_ref, diag, dctx, table, low):
    s = meta[0]
    nseq, length, width = q_ref.shape
    half = length // 2
    step = LANES
    rows = step // 4
    span = diag.shape[-1]
    zero = jnp.zeros((), BF)
    first = lane_half((length, LANES), 0)
    for hp in range(width // LANES):
        lanes = slice(hp * LANES, (hp + 1) * LANES)
        diag[...] = jnp.zeros_like(diag)
        for n in range(nseq):
            q, k, v, inv = (ref[n, :, lanes] for ref in (q_ref, k_ref, v_ref, inv_ref))
            dctx[pl.ds(pl.multiple_of(s * half, half), half), :] = own_ref[n, :, lanes]
            dctx[pl.ds(pl.multiple_of((1 - s) * half, half), half), :] = oth_ref[n, :, lanes]
            scaled = (dctx[...].astype(F32) * inv).astype(BF)
            for hh in range(2):
                table[hh] = nt(jnp.where(first if hh == 0 else ~first, scaled, zero), v)
            q_t, c_t = q.astype(F32).T.astype(BF), scaled.astype(F32).T.astype(BF)
            dq, dk, dv = [], [], []
            for hh in range(2):
                lane = hh * HEAD_DIM
                for at in range(0, length, rows):
                    base, within = length - step - at // step * step, at % step
                    e = e_ref[n, hp, hh, at : at + rows, :].astype(F32)
                    term = e * table[hh, at : at + rows]
                    delta = jnp.sum(term, axis=-1, keepdims=True) * inv[at : at + rows, lane : lane + 1]
                    grad = term - e * delta
                    diag[hh, within : within + rows, base : base + length] += grad
                    low[hh, at : at + rows] = grad.astype(BF)
                grad_low = low[hh]
                dq.append(nn(grad_low, jnp.where(first if hh == 0 else ~first, k, zero)))
                dk.append(nn(q_t[lane : lane + HEAD_DIM], grad_low))
                dv.append(nn(c_t[lane : lane + HEAD_DIM], e_ref[n, hp, hh]))
            dk, dv = (jnp.concatenate(x, axis=0).T for x in (dk, dv))
            for c, x in enumerate((dq[0] + dq[1], dk, dv)):
                grad_ref[n, :, c * width + hp * LANES : c * width + (hp + 1) * LANES] = x.astype(BF)
        for hh in range(2):
            acc = jnp.zeros((8, span), F32)
            for g in range(step // 8):
                part = diag[hh, 8 * g : 8 * g + 8, :]
                shift = step - 8 - 8 * g
                acc = acc + (pltpu.roll(part, shift, 1) if shift else part)
            out = acc[7:8]
            for b in range(7):
                out = out + pltpu.roll(acc[b : b + 1], 7 - b, 1)
            off_ref[2 * hp + hh : 2 * hp + hh + 1, :] = out
    off_ref[width // HEAD_DIM :, :] = jnp.zeros((off_ref.shape[0] - width // HEAD_DIM, span), F32)


def qkv_grad_kernel(meta, norm_ref, grad_ref, off_ref, buckets, hsel, bsel, *rest, rows, cut, dp):
    s = meta[0]
    three = grad_ref.shape[-1]
    a = norm_ref[...].reshape(-1, norm_ref.shape[-1])
    total = rest[0] if dp == 0 else rest[-1]
    total[:, :three] = tn(a, grad_ref[...].reshape(a.shape[0], three)).astype(BF)
    one_hot = (
        lax.broadcasted_iota(jnp.int32, (LANES, buckets.shape[1]), 0) == buckets[...]
    ).astype(F32)
    per_bucket = lax.dot_general(
        off_ref[...], one_hot, (((1,), (1,)), ((), ())), precision=lax.Precision.HIGHEST, preferred_element_type=F32
    )
    spread = lax.dot_general(
        hsel[s], per_bucket, (((0,), (0,)), ((), ())), precision=lax.Precision.HIGHEST, preferred_element_type=F32
    )
    column = jnp.sum(spread * bsel[...], axis=-1, keepdims=True)
    total[:, three:] = jnp.broadcast_to(column, (column.shape[0], LANES)).astype(BF)
    if dp:
        store_relative(meta, total, *rest[:4], rows, cut, dp)


def input_grad_kernel(meta, grad_ref, w, own_ref, oth_ref):
    s = meta[0]
    three = grad_ref.shape[-1]
    count = own_ref.shape[1]
    for side, ref in ((0, own_ref), (1, oth_ref)):
        at = pl.ds(pl.multiple_of((s if side == 0 else 1 - s) * count, count), count)
        ref[0] = nt(grad_ref[0, at, :], w[:, :three]).astype(ref.dtype)


def layer_out_kernel(mid_ref, own_ref, oth_ref, out_ref):
    out_ref[0] = (mid_ref[0] + own_ref[0] + oth_ref[0].astype(F32)).astype(BF)


def last_kernel(x_ref, gm_ref, own_ref, oth_ref, misc, out_ref):
    x = x_ref[0].astype(F32)
    scale = lax.rsqrt(jnp.mean(x * x, axis=-1, keepdims=True) + EPSILON)
    scaled = (own_ref[0] + oth_ref[0].astype(F32)) * misc[0:1, :]
    inner = jnp.mean(scaled * x, axis=-1, keepdims=True)
    out_ref[0] = (gm_ref[0] + scale * scaled - x * (scale * scale * scale) * inner).astype(BF)


def finish_kernel(meta, mine_ref, oth_ref, wq_ref, wk_ref, wv_ref, gain_ref, gq_ref, gk_ref, gv_ref, gain_out, bias_out, square, *, dp, table_rows):
    s, d = meta[0], meta[1]
    shard = mine_ref.shape[0]
    width = wq_ref.shape[1]
    half = width // 2
    mine, oth = mine_ref[...].astype(F32), oth_ref[...].astype(F32)
    low, top = jnp.where(s == 0, mine, oth), jnp.where(s == 0, oth, mine)
    total = jnp.zeros((shard, 1), F32)
    for c, (w_ref, out) in enumerate(((wq_ref, gq_ref), (wk_ref, gk_ref), (wv_ref, gv_ref))):
        grad = jnp.concatenate([x[:, c * half : (c + 1) * half] for x in (low, top)], axis=1)
        out[...] = grad
        total = total + jnp.sum(w_ref[...].astype(F32) * grad, axis=1, keepdims=True)
    lane = lax.broadcasted_iota(jnp.int32, (shard, LANES), 1)
    bias = jnp.where(2 * d < dp, low[:, 3 * half :], top[:, 3 * half :])
    square[...] = jnp.zeros_like(square)
    square[:shard, :] = jnp.where(lane == 0, total, bias)
    turned = square[...].T
    gain_out[...] = turned[0:1, :shard] / gain_ref[...].astype(F32)
    bias_out[...] = turned[1:2, :table_rows]


def finish_in_kernel(meta, mine_ref, oth_ref, w_ref, gain_ref, in_ref, out_ref, gain_out, square, *, in_cut, wo_cut, hid_rows, dp):
    s = meta[0]
    shard = mine_ref.shape[0]
    hid = hid_rows * dp
    mine, oth = mine_ref[...].astype(F32), oth_ref[...].astype(F32)
    halves = jnp.where(s == 0, mine, oth), jnp.where(s == 0, oth, mine)
    for c in range(dp):
        at = c * hid_rows
        at = at if at < in_cut else at + wo_cut
        for core, half in enumerate(halves):
            to = (2 * c + core) * hid_rows
            in_ref[:, to : to + hid_rows] = half[:, at : at + hid_rows]
    parts = [x[:, cut] for x in halves for cut in (slice(in_cut, in_cut + wo_cut), slice(hid + wo_cut, None))]
    out_ref[...] = jnp.concatenate(parts, axis=1)
    total = jnp.sum(w_ref[...].astype(F32) * in_ref[...], axis=1, keepdims=True)
    square[...] = jnp.zeros_like(square)
    square[:shard, :] = jnp.broadcast_to(total, (shard, LANES))
    gain_out[...] = square[...].T[0:1, :shard] / gain_ref[...].astype(F32)


def body(
    layer_input,
    gain_attn,
    w_query,
    w_key,
    w_value,
    w_output,
    bias_table,
    gain_ffn,
    ffn_in,
    ffn_out,
    buckets,
    keep_mask,
    out_grad,
):
    dp = lax.axis_size("dp")
    s = lax.axis_index("seq")
    d = lax.axis_index("dp")
    nseq, count, width = layer_input.shape
    length = 2 * count
    span = 2 * length
    half = width // 2
    shard = w_query.shape[0]
    rows = 2 * shard
    hid_rows = ffn_out.shape[0]
    hid = hid_rows * dp
    table_rows = bias_table.shape[0]
    tok = nseq * length
    pairs = half // LANES
    meta = jnp.stack([s, d]).astype(jnp.int32)
    aligned = rows % 16 == 0 and hid_rows % 16 == 0

    def sds(shape, dtype=BF):
        return jax.ShapeDtypeStruct(shape, dtype)

    def far(shape, dtype=BF):
        return pltpu.HBM(shape, dtype)

    def first_columns(h):
        cut = [lax.dynamic_slice_in_dim(w, h * half, half, 1) for w in (w_query, w_key, w_value)]
        table = jnp.pad(bias_table, (0, shard - table_rows))
        extra = jnp.stack([gain_attn, gain_ffn, table], axis=1)
        return jnp.concatenate(cut + [jnp.pad(extra, ((0, 0), (0, LANES - 3)))], axis=1)

    def swapped(mine, theirs):
        theirs = other_core(theirs)
        return jnp.where(s == 0, jnp.concatenate([mine, theirs]), jnp.concatenate([theirs, mine]))

    first_cols = 3 * half + LANES
    second_cols = half + hid
    first_cut = (first_cols // LANES // 2) * LANES
    second_cut = (second_cols // LANES // 2) * LANES
    third_cut = (width // LANES // 2) * LANES

    first = Gather(swapped(first_columns(s), first_columns(1 - s)), first_cut, dp)
    first.high()
    x_oth = other_core(after(layer_input, first.have))
    second_block = swapped(
        *small(
            functools.partial(second_kernel, hid_rows=hid_rows, dp=dp),
            (meta, w_output, ffn_in),
            [(shard, second_cols)] * 2,
            "second_columns",
        )
    )
    x_oth, second_block = meet((x_oth, second_block), (first, "have got"))
    line = dp == 16
    second = LineGather(second_block, second_cut, dp, meta) if line else Gather(second_block, second_cut, dp)
    first.first()
    second.begin()
    meet((), (first, "left right left_x right_y"), (second, "near mid" if line else "near"))
    first.second()
    second.high()
    g_oth = other_core(out_grad)
    keep_oth = other_core(keep_mask.astype(BF))
    keep = keep_mask.astype(BF)
    keep = jnp.where(s == 0, jnp.concatenate([keep, keep_oth], 1), jnp.concatenate([keep_oth, keep], 1))
    mask = ((keep.astype(F32) - 1.0) * 1e9)[:, None, :]
    g_both = jnp.concatenate([out_grad, g_oth], axis=1)

    high = dp // 4
    orders = [np.array([(h << 2) | low for low in lows for h in range(high)], np.int32) for lows in ((0, 1, 2, 3), (0, 2, 1, 3))]
    pos_l, pos_r = ((d ^ jnp.asarray(order)).astype(jnp.int32) for order in orders)
    pos = pos_l

    def settle(pieces, places=pos_l):
        if aligned:
            return pieces
        every = jnp.concatenate(pieces, axis=0)
        order = jnp.argsort(places)
        return [every[order].reshape(1, -1, every.shape[-1])]

    def settle_both(gather):
        left, right = gather.pieces()
        return settle(left), settle(right, pos_r)

    if not aligned:
        pos_k, rows_k, hid_rows_k, nblk, dp_k = jnp.zeros((2, 1), jnp.int32), width, hid, 1, 1
    else:
        pos_k, rows_k, hid_rows_k, nblk, dp_k = jnp.stack([pos_l, pos_r]), rows, hid_rows, dp, dp

    feature = np.arange(width)
    chunk, within = feature // rows, feature % rows
    entry = np.where(within % shard < table_rows, table_rows * chunk + within % shard, -1)
    head, bucket = entry // BUCKETS, entry % BUCKETS
    half_heads = HEADS // 2
    hsel = np.zeros((2, 8, width), np.float32)
    bsel = np.zeros((width, LANES), np.float32)
    for f in range(width):
        if entry[f] >= 0:
            hsel[head[f] // half_heads, head[f] % half_heads, f] = 1.0
            bsel[f, bucket[f]] = 1.0
    bsel_once = jnp.asarray(np.where(within[:, None] < shard, bsel, 0.0))
    hsel, bsel = jnp.asarray(hsel), jnp.asarray(bsel)
    padded = jnp.concatenate([buckets, jnp.full((span - buckets.shape[0],), -1, jnp.int32)])[None]

    seq_block = lambda shape: pl.BlockSpec((1,) + shape, lambda n: (n, 0, 0))
    VMEM = pl.BlockSpec(memory_space=pltpu.VMEM)
    rel = dp if aligned else 0

    def block_shapes(block_rows, cut, cols):
        if aligned:
            left, right = (2, high, block_rows, cut), (2, high, block_rows, cols - cut)
            return [left, left, right, right]
        return [(dp * block_rows, cols)]

    def in_relative(parts, block_rows, cut):
        if aligned:
            return parts
        blocks = parts[0].reshape(dp, block_rows, -1)[pos_l].reshape(2, 2, high, block_rows, -1)
        left, right = blocks[..., :cut], blocks[..., cut:]
        return left[1], left[0], right[:, 1], right[:, 0]

    def gradient(kernel, inputs, block_rows, cut, cols, name, earlier=()):
        shapes = block_shapes(block_rows, cut, cols)

        def ordered(meta_ref, *refs):
            kernel(meta_ref, *refs[len(earlier) :], rows=block_rows, cut=cut, dp=rel)

        parts = pl.pallas_call(
            ordered,
            in_specs=[SMEM] + [ANY] * len(earlier) + [VMEM] * len(inputs),
            out_specs=[VMEM] * len(shapes),
            out_shape=[sds(x) for x in shapes],
            scratch_shapes=[pltpu.VMEM((dp * block_rows, cols), BF)] if aligned else [],
            compiler_params=params(10),
            name=name,
            cost_estimate=cost(name),
        )(meta, *earlier, *inputs)
        return in_relative(parts, block_rows, cut)

    x_oth, ffn_out, mask, g_both = meet(
        (x_oth, ffn_out, mask, g_both), (first, "left right left_far right_far"), (second, "have got")
    )
    second.first()
    third = Gather(ffn_out, third_cut, dp)
    left, right = settle_both(first)
    q, k, v, normed_attn, misc, peroff, w_qkv = pl.pallas_call(
        functools.partial(qkv_kernel, rows=rows_k, cut=first_cut, width=width, nl=len(left), nr=len(right)),
        grid=(nseq,),
        in_specs=[SMEM, SMEM, seq_block((count, width)), seq_block((count, width)), whole((1, span)), whole(hsel.shape), whole(bsel.shape)]
        + [whole(x.shape) for x in left + right],
        out_specs=[seq_block((length, half))] * 3 + [seq_block((length, width)), whole((8, width)), whole((8, span)), ANY],
        out_shape=[sds((nseq, length, half))] * 3
        + [far((nseq, length, width)), sds((8, width), F32), sds((8, span), F32), far((width, first_cols))],
        scratch_shapes=[pltpu.VMEM((width, first_cols), BF), pltpu.SemaphoreType.DMA],
        compiler_params=params(8),
        name="qkv",
        cost_estimate=cost("qkv"),
    )(meta, pos_k, layer_input, x_oth, padded, hsel, bsel_once, *left, *right)

    q, k, v = meet((q, k, v), (second, "left right left_x right_y"))
    second.second()
    third.high()
    ctx_own, ctx_send, expo, inv = pl.pallas_call(
        attend_kernel,
        in_specs=[SMEM] + [VMEM] * 5,
        out_specs=[VMEM, VMEM, ANY, ANY],
        out_shape=[
            sds((nseq, count, half)),
            sds((nseq, count, half)),
            far((nseq, pairs, 2, length, length)),
            far((nseq, length, half), F32),
        ],
        scratch_shapes=[
            pltpu.VMEM((half_heads, LANES, span), F32),
            pltpu.VMEM((length, LANES), BF),
            pltpu.VMEM((2, length, length), F32),
            pltpu.VMEM((3, 2, length, length), BF),
            pltpu.VMEM((3, length, LANES), F32),
            pltpu.SemaphoreType.DMA((3,)),
            pltpu.SemaphoreType.DMA((3,)),
        ],
        compiler_params=params(12),
        name="attend",
        cost_estimate=cost("attend"),
    )(meta, q, k, v, mask, peroff)

    ctx_own, ctx_send = meet((ctx_own, ctx_send), (second, "left right left_far right_far"), (third, "have got"))
    ctx_oth = other_core(ctx_send)
    wo_own = stack(second.pieces()[0], half, "output_columns")[0]
    wo_oth = other_core(wo_own)
    third.first()
    wo_own, wo_oth = settle([wo_own])[0], settle([wo_oth])[0]
    middle, normed_own, w_o = pl.pallas_call(
        functools.partial(middle_kernel, rows=rows_k),
        in_specs=[SMEM, SMEM] + [VMEM] * 6,
        out_specs=[ANY, VMEM, ANY],
        out_shape=[far((nseq, count, width), F32), sds((nseq, count, width)), far((2, width, half))],
        scratch_shapes=[
            pltpu.VMEM((2, width, half), BF),
            pltpu.VMEM((nseq, count, width), F32),
            pltpu.SemaphoreType.DMA,
            pltpu.SemaphoreType.DMA((nseq,)),
        ],
        compiler_params=params(8),
        name="middle",
        cost_estimate=cost("middle"),
    )(meta, pos_k, layer_input, ctx_own, ctx_oth, misc, wo_own, wo_oth)

    middle, normed_own = meet((middle, normed_own), (third, "left right left_x right_y"))
    third.second()
    normed_oth = other_core(normed_own)
    left, right = settle_both(second)
    act, slope, w_in = pl.pallas_call(
        functools.partial(hidden_kernel, rows=rows_k, skip=half, cut=second_cut, nl=len(left), nr=len(right)),
        grid=(nseq,),
        in_specs=[SMEM, seq_block((count, width)), seq_block((count, width))] + [whole(x.shape) for x in left + right],
        out_specs=[seq_block((length, hid)), seq_block((length, hid)), whole((width, hid))],
        out_shape=[sds((nseq, length, hid)), sds((nseq, length, hid)), sds((width, hid))],
        compiler_params=params(),
        name="hidden",
        cost_estimate=cost("hidden"),
    )(pos_k, normed_own, normed_oth, *left, *right)
    out_parts = gradient(wgrad_kernel, (act, g_both), hid_rows, third_cut, width, "grad_ffn_out")

    out_parts, slope, act = meet((out_parts, slope, act), (third, "left right left_far right_far"))
    out_sum = Scatter(out_parts, dp, 1)
    out_sum.first()
    left, right = settle_both(third)
    seq_half = seq_block((count, width))
    grad_pre, back_own, back_send, out_own, out_send = pl.pallas_call(
        functools.partial(ffn_back_kernel, rows=hid_rows_k, cut=third_cut, nl=len(left), nr=len(right)),
        grid=(nseq,),
        in_specs=[SMEM, seq_block((length, width)), seq_block((length, hid)), seq_block((length, hid)), whole((width, hid))]
        + [whole(x.shape) for x in left + right],
        out_specs=[seq_block((length, hid))] + [seq_half] * 4,
        out_shape=[sds((nseq, length, hid)), sds((nseq, count, width), F32), sds((nseq, count, width))]
        + [far((nseq, count, width), F32), far((nseq, count, width))],
        scratch_shapes=[pltpu.VMEM((hid, width), BF)],
        input_output_aliases={3: 0},
        compiler_params=params(8),
        name="ffn_back",
        cost_estimate=cost("ffn_back"),
    )(pos_k, g_both, act, slope, w_in, *left, *right)

    grad_pre, back_own, back_send, out_own, out_send = meet(
        (grad_pre, back_own, back_send, out_own, out_send), (out_sum, "left_got right_got")
    )
    out_sum.second()
    back_oth, out_oth = other_core(back_send), other_core(out_send)
    in_cut = (hid // LANES // 2) * LANES
    in_parts = gradient(
        functools.partial(wgrad_kernel, na=2),
        (normed_own, normed_oth, grad_pre),
        rows,
        in_cut,
        hid,
        "grad_ffn_in",
        (out_sum.left_send, out_sum.right_send),
    )

    back_own, back_oth, out_oth = meet((back_own, back_oth, out_oth))
    grad_middle, middle_low, dctx_own, dctx_send = pl.pallas_call(
        middle_back_kernel,
        grid=(nseq,),
        in_specs=[SMEM] + [seq_block((count, width))] * 4 + [whole((8, width)), whole((2, width, half))],
        out_specs=[seq_block((count, width)), seq_block((count, width)), seq_block((count, half)), seq_block((count, half))],
        out_shape=[
            far((nseq, count, width), F32),
            sds((nseq, count, width)),
            sds((nseq, count, half)),
            sds((nseq, count, half)),
        ],
        compiler_params=params(8),
        name="middle_back",
        cost_estimate=cost("middle_back"),
    )(meta, out_grad, middle, back_own, back_oth, misc, w_o)
    in_parts, dctx_own, dctx_send, middle_low = meet(
        (in_parts, dctx_own, dctx_send, middle_low), (out_sum, "left_got right_got")
    )
    dctx_oth = other_core(dctx_send)
    rel_meta = meta if aligned else jnp.stack([s, jnp.zeros_like(d)]).astype(jnp.int32)
    wo_keep, wo_send = pl.pallas_call(
        functools.partial(wo_grad_kernel, rows=rows_k, dp=dp_k),
        out_shape=[sds((dp_k, rows_k, half))] * 2,
        in_specs=[SMEM] + [VMEM] * 3,
        out_specs=[VMEM] * 2,
        scratch_shapes=[pltpu.VMEM((2, width, half), F32)],
        compiler_params=params(),
        name="grad_output",
        cost_estimate=cost("grad_output"),
    )(rel_meta, ctx_own, ctx_oth, middle_low)
    wo_got = other_core(wo_send)
    if not aligned:
        wo_keep, wo_got = (x.reshape(dp, rows, half)[d ^ jnp.arange(dp)] for x in (wo_keep, wo_got))
    wo_cut = (half // LANES // 2) * LANES

    wo_keep, wo_got, dctx_own, dctx_oth = meet((wo_keep, wo_got, dctx_own, dctx_oth))
    out_sum.high()
    in_sum = Scatter(with_output_columns(in_parts, wo_keep, wo_got, wo_cut), dp)
    in_sum.first()
    dqkv, off = pl.pallas_call(
        attend_back_kernel,
        in_specs=[SMEM] + [VMEM] * 7,
        out_specs=[VMEM] * 2,
        out_shape=[sds((nseq, length, 3 * half)), sds((8, span), F32)],
        scratch_shapes=[
            pltpu.VMEM((2, LANES, span), F32),
            pltpu.VMEM((length, LANES), BF),
            pltpu.VMEM((2, length, length), F32),
            pltpu.VMEM((2, length, length), BF),
        ],
        compiler_params=params(8),
        name="attend_back",
        cost_estimate=cost("attend_back"),
    )(meta, q, k, v, expo, inv, dctx_own, dctx_oth)
    dqkv, off = meet((dqkv, off), (out_sum, "got"), (in_sum, "left_got right_got"))
    in_sum.second()
    qkv_parts = gradient(
        qkv_grad_kernel,
        (normed_attn, dqkv, off, padded, hsel, bsel),
        rows,
        first_cut,
        first_cols,
        "grad_qkv",
        (in_sum.left_send, in_sum.right_send),
    )

    qkv_parts, dqkv, w_qkv = meet((qkv_parts, dqkv, w_qkv))
    qkv_sum = Scatter(qkv_parts, dp)
    qkv_sum.first()
    in_sum.high()
    dn_own, dn_send = pl.pallas_call(
        input_grad_kernel,
        grid=(nseq,),
        in_specs=[SMEM, seq_block((length, 3 * half)), whole((width, first_cols))],
        out_specs=[seq_half] * 2,
        out_shape=[far((nseq, count, width), F32), sds((nseq, count, width))],
        compiler_params=params(8),
        name="input_grad",
        cost_estimate=cost("input_grad"),
    )(meta, dqkv, w_qkv)
    dn_own, dn_send, in_sum.got[:2] = meet((dn_own, dn_send, in_sum.got[:2]), (qkv_sum, "left_got right_got"))
    qkv_sum.second()
    dn_oth = other_core(dn_send)
    kept = [grad_middle, dn_own] + [pltpu.with_memory_space_constraint(x, pltpu.HBM) for x in (middle, out_own, out_oth)]
    grad_input = pl.pallas_call(
        last_kernel,
        grid=(nseq,),
        in_specs=[seq_half] * 4 + [whole((8, width))],
        out_specs=seq_half,
        out_shape=sds((nseq, count, width)),
        compiler_params=params(10),
        name="last",
        cost_estimate=cost("last"),
    )(layer_input, *kept[:2], dn_oth, misc)
    grad_input, kept = meet((grad_input, kept), (qkv_sum, "left_got right_got"))
    qkv_sum.high()
    grad_ffn_out = out_sum.rest(F32)
    layer_out = pl.pallas_call(
        layer_out_kernel,
        grid=(nseq,),
        in_specs=[seq_half] * 3,
        out_specs=seq_half,
        out_shape=sds((nseq, count, width)),
        compiler_params=params(10),
        name="layer_out",
        cost_estimate=cost("last"),
    )(*kept[2:])
    in_sum.got = after(in_sum.got, qkv_sum.left_got, qkv_sum.right_got)
    mine, theirs = in_sum.halves(meta, shard)
    theirs = other_core(theirs)
    grad_ffn_in, grad_output, gain_ffn_row = pl.pallas_call(
        functools.partial(finish_in_kernel, in_cut=in_cut, wo_cut=wo_cut, hid_rows=hid_rows, dp=dp),
        in_specs=[SMEM] + [VMEM] * 4,
        out_specs=[VMEM] * 3,
        out_shape=[sds((shard, 2 * hid), F32), sds((shard, width), F32), sds((1, shard), F32)],
        scratch_shapes=[pltpu.VMEM((LANES, LANES), F32)],
        compiler_params=params(),
        name="finish_in",
        cost_estimate=cost("finish"),
    )(meta, mine, theirs, ffn_in, gain_ffn[None])
    layer_out, grad_ffn_in, grad_output, gain_ffn_row, grad_ffn_out = meet(
        (layer_out, grad_ffn_in, grad_output, gain_ffn_row, grad_ffn_out), (qkv_sum, "got")
    )

    mine, theirs = qkv_sum.halves(meta, shard)
    theirs = other_core(theirs)
    grad_query, grad_key, grad_value, gain_row, bias_row = pl.pallas_call(
        functools.partial(finish_kernel, dp=dp, table_rows=table_rows),
        in_specs=[SMEM] + [VMEM] * 6,
        out_specs=[VMEM] * 5,
        out_shape=[sds((shard, width), F32)] * 3 + [sds((1, shard), F32), sds((1, table_rows), F32)],
        scratch_shapes=[pltpu.VMEM((LANES, LANES), F32)],
        compiler_params=params(),
        name="finish",
        cost_estimate=cost("finish"),
    )(meta, mine, theirs, w_query, w_key, w_value, gain_attn[None])
    return (
        layer_out,
        grad_input,
        gain_row.reshape(shard),
        grad_query,
        grad_key,
        grad_value,
        grad_output,
        bias_row.reshape(table_rows),
        gain_ffn_row.reshape(shard),
        grad_ffn_in,
        grad_ffn_out,
    )


def solution(mesh):
    both = ("dp", "seq")
    return jax.shard_map(
        body,
        mesh=mesh,
        in_specs=(
            P("dp", "seq", None),
            P(both),
            P(both, None),
            P(both, None),
            P(both, None),
            P(both, None),
            P("dp"),
            P(both),
            P(both, None),
            P(both, None),
            P(),
            P("dp", "seq"),
            P("dp", "seq", None),
        ),
        out_specs=(
            P("dp", "seq", None),
            P("dp", "seq", None),
            P(both),
            P(both, None),
            P(both, None),
            P(both, None),
            P(both, None),
            P("dp"),
            P(both),
            P(both, None),
            P(both, None),
        ),
        check_vma=False,
    )
```

```python
import functools
import math

import jax
import jax.numpy as jnp
import numpy as np
from jax import lax
from jax.experimental import pallas as pl
from jax.experimental.pallas import tpu as pltpu
from jax.sharding import PartitionSpec as P

HEADS = 12
HEAD_DIM = 64
BUCKETS = 32
EPSILON = 1e-06
LANES = 128
BF = jnp.bfloat16
F32 = jnp.float32
GELU_A = math.sqrt(2.0 / math.pi)
GELU_B = 0.044715

ANY = pl.BlockSpec(memory_space=pl.ANY)
SMEM = pl.BlockSpec(memory_space=pltpu.SMEM)
FAR = pl.BlockSpec(memory_space=pltpu.HBM)


def whole(shape):
    zeros = (0,) * len(shape)
    return pl.BlockSpec(shape, lambda *_: zeros)


def params(mib=6):
    return pltpu.CompilerParams(vmem_limit_bytes=mib * 1024 * 1024)


MICROS = {
    "qkv": 7, "attend": 10, "middle": 4, "hidden": 8, "grad_ffn_out": 5, "grad_ffn_in": 5, "ffn_back": 9, "ffn_out": 5,
    "middle_back": 4, "grad_output": 2, "attend_back": 14, "grad_qkv": 5, "input_grad": 5, "last": 3, "finish": 1,
}


def cost(name):
    return pl.CostEstimate(flops=int(MICROS[name] * 1e4), bytes_accessed=0, transcendentals=0)


def nn(a, b):
    return lax.dot_general(a, b, (((1,), (0,)), ((), ())), preferred_element_type=F32)


def nt(a, b):
    return lax.dot_general(a, b, (((1,), (1,)), ((), ())), preferred_element_type=F32)


def tn(a, b):
    return lax.dot_general(a, b, (((0,), (0,)), ((), ())), preferred_element_type=F32)


def flip(x, axis, bit, count):
    return lax.ppermute(x, axis, [(i, i ^ bit) for i in range(count)])


def after(values, *others):
    return lax.optimization_barrier((values, others))[0]


def meet(values, *fields):
    held = [[getattr(owner, name) for name in names.split()] for owner, names in fields]
    values, held = lax.optimization_barrier((values, held))
    for (owner, names), got in zip(fields, held):
        for name, value in zip(names.split(), got):
            setattr(owner, name, value)
    return values


def bit_groups(dp, most=2):
    bits, groups = dp.bit_length() - 3, []
    at = 2
    while bits > 0:
        groups.append((1 << at, 1 << min(bits, most)))
        at, bits = at + most, bits - most
    return groups


def small(kernel, inputs, shapes, name, dtype=BF):
    return pl.pallas_call(
        kernel,
        in_specs=[SMEM if x.ndim == 1 else pl.BlockSpec(memory_space=pltpu.VMEM) for x in inputs],
        out_specs=[pl.BlockSpec(memory_space=pltpu.VMEM)] * len(shapes),
        out_shape=[jax.ShapeDtypeStruct(x, dtype) for x in shapes],
        compiler_params=params(),
        name=name,
        cost_estimate=pl.CostEstimate(flops=10**4, bytes_accessed=0, transcendentals=0),
    )(*inputs)


def total_of(refs, at, dtype=BF):
    return functools.reduce(lambda x, y: x + y, (ref[at].astype(F32) for ref in refs)).astype(dtype)


def merge(sides, size, joined, name, dtype=BF):
    counts = [len(side) for side in sides]
    k, rows, _ = sides[0][0].shape
    widths = [side[0].shape[2] for side in sides]
    part = k // size
    shapes = [(part, rows, sum(widths))] * size if joined else [(part, rows, w) for w in widths for _ in range(size)]

    def kernel(*refs):
        ins, outs = refs[: sum(counts)], refs[sum(counts) :]
        at, lane = 0, 0
        for i, (count, width) in enumerate(zip(counts, widths)):
            for j in range(k):
                out = outs[j // part] if joined else outs[i * size + j // part]
                out[j % part, :, lane : lane + width] = total_of(ins[at : at + count], j, dtype)
            at += count
            lane = lane + width if joined else 0

    return small(kernel, [x for side in sides for x in side], shapes, name, dtype)


def either(meta, near, mid, name):
    def kernel(meta_ref, near_ref, mid_ref, down, up):
        place_z = meta_ref[1] >> 2
        down[...] = jnp.where(place_z == 1, mid_ref[...], near_ref[...])
        up[...] = jnp.where(place_z == 2, mid_ref[...], near_ref[...])

    return small(kernel, (meta, near, mid), [near.shape] * 2, name)


def stack_line(meta, have, near, mid, down, up, far, cut, name):
    _, rows, cols = have.shape

    def kernel(meta_ref, have_ref, near_ref, mid_ref, down_ref, up_ref, far_ref, left, right):
        place_z = meta_ref[1] >> 2
        inner = jnp.logical_or(place_z == 1, place_z == 2)
        blocks = (
            have_ref[0],
            near_ref[0],
            jnp.where(place_z < 2, down_ref[0], up_ref[0]),
            jnp.where(inner, mid_ref[0], far_ref[0]),
        )
        for i, block in enumerate(blocks):
            left[i] = block[:, :cut]
            right[i] = block[:, cut:]

    return small(kernel, (meta, have, near, mid, down, up, far), [(4, rows, cut), (4, rows, cols - cut)], name)


def stack(pieces, cut, name):
    ks = [x.shape[0] for x in pieces]
    rows, cols = pieces[0].shape[1:]

    def kernel(*refs):
        left, right = refs[len(ks) :]
        at = 0
        for ref, k in zip(refs, ks):
            left[at : at + k] = ref[:, :, :cut]
            right[at : at + k] = ref[:, :, cut:]
            at += k

    return small(kernel, pieces, [(sum(ks), rows, cut), (sum(ks), rows, cols - cut)], name)


def front(pieces, cut, name):
    ks = [x.shape[0] for x in pieces]

    def kernel(*refs):
        at = 0
        for ref, k in zip(refs, ks):
            refs[-1][at : at + k] = ref[:, :, :cut]
            at += k

    return small(kernel, pieces, [(sum(ks), pieces[0].shape[1], cut)], name)[0]


def pair_up(a, b, c, d, name):
    k = a.shape[0]

    def kernel(a_ref, b_ref, c_ref, d_ref, ab, cd):
        ab[:k], ab[k:] = a_ref[...], b_ref[...]
        cd[:k], cd[k:] = c_ref[...], d_ref[...]

    return small(kernel, (a, b, c, d), [(2 * k,) + a.shape[1:], (2 * k,) + c.shape[1:]], name)


def with_output_columns(parts, keep, got, cut):
    count, _, half = keep.shape
    widths = [x.shape[-1] for x in parts]
    extra = (cut, cut, half - cut, half - cut)
    shapes = [x.shape[:-1] + (w + more,) for x, w, more in zip(parts, widths, extra)]

    def kernel(*refs):
        ins, keep_ref, got_ref, outs = refs[:4], refs[4], refs[5], refs[6:]
        for ref, out, w in zip(ins, outs, widths):
            out[..., :w] = ref[...]
        for rel in range(count):
            x, y, high = rel & 1, (rel >> 1) & 1, rel >> 2
            block = total_of((keep_ref, got_ref), rel)
            i = 0 if y else 1
            outs[i][x, high, :, widths[i] :] = block[:, :cut]
            i = 2 if x else 3
            outs[i][y, high, :, widths[i] :] = block[:, cut:]

    return small(kernel, (*parts, keep, got), shapes, "output_parts")


class Gather:
    def __init__(self, block, cut, dp, most=2):
        self.have, self.cut, self.dp, self.most = block[None], cut, dp, most
        self.near = None

    def begin(self):
        self.near = flip(self.have, "dp", 4, self.dp)

    def high(self):
        self.got = []
        groups = bit_groups(self.dp, self.most)
        for i, (bit, size) in enumerate(groups):
            first = [self.near] if bit == 4 and self.near is not None else [flip(self.have, "dp", bit, self.dp)]
            self.got = first + [flip(self.have, "dp", bit * k, self.dp) for k in range(2, size)]
            if i + 1 < len(groups):
                self.have = front([self.have] + self.got, self.have.shape[2], "join")

    def first(self):
        self.left, self.right = stack([self.have] + self.got, self.cut, "stack")
        self.left_x = flip(self.left, "dp", 1, self.dp)
        self.right_y = flip(self.right, "dp", 2, self.dp)

    def second(self):
        self.left, self.right = pair_up(self.left, self.left_x, self.right, self.right_y, "pair_up")
        self.left_far = flip(self.left, "dp", 2, self.dp)
        self.right_far = flip(self.right, "dp", 1, self.dp)

    def pieces(self):
        return [self.left, self.left_far], [self.right, self.right_far]


class LineGather(Gather):
    def __init__(self, block, cut, dp, meta):
        super().__init__(block, cut, dp)
        self.meta = meta

    def along(self, x, pairs):
        return lax.ppermute(x, "dp", [(4 * a + low, 4 * b + low) for a, b in pairs for low in range(4)])

    def begin(self):
        self.near = flip(self.have, "dp", 4, self.dp)
        self.mid = self.along(self.have, ((1, 2), (2, 1)))

    def high(self):
        down, up = either(self.meta, self.near, self.mid, "either")
        self.got = [
            self.along(down, ((1, 0), (2, 1))),
            self.along(up, ((2, 3), (1, 2))),
            self.along(self.near, ((2, 0), (1, 3))),
        ]

    def first(self):
        self.left, self.right = stack_line(
            self.meta, self.have, self.near, self.mid, *self.got, self.cut, "stack_line"
        )
        self.left_x = flip(self.left, "dp", 1, self.dp)
        self.right_y = flip(self.right, "dp", 2, self.dp)


class Scatter:
    def __init__(self, parts, dp, most=2):
        flat = [x.reshape((-1,) + x.shape[2:]) for x in parts]
        self.left_send, self.left_keep, self.right_send, self.right_keep = flat
        self.dp, self.groups = dp, bit_groups(dp, most)

    def first(self):
        self.left_got = flip(self.left_send, "dp", 2, self.dp)
        self.right_got = flip(self.right_send, "dp", 1, self.dp)

    def second(self):
        self.left, self.left_send, self.right, self.right_send = merge(
            [[self.left_keep, self.left_got], [self.right_keep, self.right_got]], 2, False, "add_second"
        )
        self.left_got = flip(self.left_send, "dp", 1, self.dp)
        self.right_got = flip(self.right_send, "dp", 2, self.dp)

    def spread(self, sides):
        bit, size = self.groups.pop()
        self.keep, *parts = merge(sides, size, True, "add_high")
        self.got = [flip(x, "dp", bit * (k + 1), self.dp) for k, x in enumerate(parts)]

    def high(self):
        self.spread([[self.left, self.left_got], [self.right, self.right_got]])

    def halves(self, meta, shard):
        while self.groups:
            self.spread([[self.keep] + self.got])
        terms = [self.keep] + self.got

        def kernel(meta_ref, *refs):
            ins, (mine, theirs) = refs[:-2], refs[-2:]
            total = functools.reduce(lambda x, y: x + y, (ref[0].astype(F32) for ref in ins))
            low, top = total[:shard], total[shard:]
            mine[...] = jnp.where(meta_ref[0] == 0, low, top).astype(BF)
            theirs[...] = jnp.where(meta_ref[0] == 0, top, low).astype(BF)

        return small(kernel, [meta] + terms, [(shard, terms[0].shape[-1])] * 2, "halves")

    def rest(self, dtype=BF):
        while self.groups:
            self.spread([[self.keep] + self.got])
        return merge([[self.keep] + self.got], 1, True, "add_last", dtype)[0][0]


def other_core(x):
    return lax.ppermute(x, "seq", [(0, 1), (1, 0)])


def place(refs, pos, side, rows, dst, lane, skip=0):
    at = 0
    for ref in refs:
        cols = ref.shape[2] - skip
        for b in range(ref.shape[0]):
            row = pl.multiple_of(pos[side, at] * rows, rows)
            dst[pl.ds(row, rows), lane : lane + cols] = ref[b, :, skip:]
            at += 1


def second_kernel(meta, w_out, w_in, mine, theirs, *, hid_rows, dp):
    s = meta[0]
    half = w_out.shape[1] // 2
    low, top = w_out[:, :half], w_out[:, half:]
    mine[:, :half] = jnp.where(s == 0, low, top)
    theirs[:, :half] = jnp.where(s == 0, top, low)
    for c in range(dp):
        at, to = 2 * c * hid_rows, half + c * hid_rows
        low, top = w_in[:, at : at + hid_rows], w_in[:, at + hid_rows : at + 2 * hid_rows]
        mine[:, to : to + hid_rows] = jnp.where(s == 0, low, top)
        theirs[:, to : to + hid_rows] = jnp.where(s == 0, top, low)


def qkv_kernel(meta, pos, x_own, x_oth, buckets, hsel, bsel, *rest, rows, cut, width, nl, nr):
    left, right = rest[:nl], rest[nl : nl + nr]
    q_ref, k_ref, v_ref, norm_ref, misc, peroff, w_far, w, sem = rest[nl + nr :]
    s = meta[0]
    half = width // 2
    n = pl.program_id(0)
    copy = pltpu.make_async_copy(w, w_far, sem)

    @pl.when(n == 0)
    def _():
        place(left, pos, 0, rows, w, 0)
        place(right, pos, 1, rows, w, cut)
        copy.start()
        extra = w[:, 3 * half :].astype(F32)
        misc[...] = extra.T[:8]
        spread = (extra[:, 2:3] * bsel[...]).astype(BF)
        table = nn(hsel[s].astype(BF), spread)
        one_hot = (
            lax.broadcasted_iota(jnp.int32, (LANES, buckets.shape[1]), 0) == buckets[...]
        ).astype(F32)
        peroff[...] = nn(table.astype(BF), one_hot.astype(BF))

    gain = misc[0:1, :]
    count = x_own.shape[1]
    for side, x_ref in ((0, x_own), (1, x_oth)):
        x = x_ref[0].astype(F32)
        scale = lax.rsqrt(jnp.mean(x * x, axis=-1, keepdims=True) + EPSILON)
        normed = (x * scale * gain).astype(BF)
        at = pl.ds(pl.multiple_of((s if side == 0 else 1 - s) * count, count), count)
        norm_ref[0, at, :] = normed
        q_ref[0, at, :] = nn(normed, w[:, :half]).astype(BF)
        k_ref[0, at, :] = nn(normed, w[:, half : 2 * half]).astype(BF)
        v_ref[0, at, :] = nn(normed, w[:, 2 * half : 3 * half]).astype(BF)

    @pl.when(n == pl.num_programs(0) - 1)
    def _():
        copy.wait()


def lane_half(shape, which):
    lane = lax.broadcasted_iota(jnp.int32, shape, 1)
    return (lane < HEAD_DIM) if which == 0 else (lane >= HEAD_DIM)


def attend_kernel(meta, q_ref, k_ref, v_ref, mask_ref, peroff, own_ref, oth_ref, e_far, inv_far, grid, ctx, table, e_buf, inv_buf, sems, inv_sems):
    s = meta[0]
    nseq, length, width = q_ref.shape
    step = LANES
    rows = step // 2
    half = length // 2
    span = grid.shape[-1]
    zero, one = jnp.zeros((), BF), jnp.ones((), BF)
    first = lane_half((length, LANES), 0)
    heads = width // HEAD_DIM
    for h in range(heads):
        wide = jnp.broadcast_to(peroff[h : h + 1, :], (step, span))
        grid[h] = pltpu.roll(wide, span - step + 1, 1, stride=1, stride_axis=0)
    items = [(hp, n, hh) for hp in range(heads // 2) for n in range(nseq) for hh in range(2)]

    def product(i):
        hp, n, hh = items[i]
        lanes = slice(hp * LANES, (hp + 1) * LANES)
        head = jnp.where(first if hh == 0 else ~first, q_ref[n, :, lanes], zero)
        table[i % 2] = nt(head, k_ref[n, :, lanes])

    def stores(i):
        hp, n, _ = items[2 * i]
        inv_dst = inv_far.at[n, :, pl.ds(hp * LANES, LANES)]
        return (
            pltpu.make_async_copy(e_buf.at[i % 3], e_far.at[n, hp], sems.at[i % 3]),
            pltpu.make_async_copy(inv_buf.at[i % 3], inv_dst, inv_sems.at[i % 3]),
        )

    product(0)
    sums = [None, None]
    for i, (hp, n, hh) in enumerate(items):
        lanes = slice(hp * LANES, (hp + 1) * LANES)
        e_ref = e_buf.at[i // 2 % 3]
        if i + 1 < len(items):
            product(i + 1)
        if hh == 0 and i >= 6:
            for copy in stores(i // 2 - 3):
                copy.wait()
        for at in range(0, length, rows):
            base, within = length - step - at // step * step, at % step
            bias = grid[2 * hp + hh, within : within + rows, base : base + length]
            scores = table[i % 2, at : at + rows] + (bias + mask_ref[n])
            top = jnp.max(scores, axis=-1, keepdims=True)
            e_ref[hh, at : at + rows, :] = jnp.exp(scores - top).astype(BF)
        sums[hh] = nn(e_ref[hh], jnp.where(first if hh == 0 else ~first, v_ref[n, :, lanes], one))
        if hh == 1:
            num = jnp.where(first, sums[0], sums[1])
            den = pltpu.roll(jnp.where(first, sums[1], sums[0]), HEAD_DIM, 1)
            inv = 1.0 / den
            inv_buf[i // 2 % 3] = inv
            for copy in stores(i // 2):
                copy.start()
            ctx[...] = (num * inv).astype(BF)
            own_ref[n, :, lanes] = ctx[pl.ds(pl.multiple_of(s * half, half), half), :]
            oth_ref[n, :, lanes] = ctx[pl.ds(pl.multiple_of((1 - s) * half, half), half), :]
    for i in range(max(0, len(items) // 2 - 3), len(items) // 2):
        for copy in stores(i):
            copy.wait()


def middle_kernel(meta, pos, x_ref, own_ref, oth_ref, misc, own_w, oth_w, mid_far, norm_ref, w_far, w, mid, sem, mid_sems, *, rows):
    s = meta[0]
    half = w.shape[2]
    place([own_w], pos, 0, rows, w.at[s], 0)
    place([oth_w], pos, 0, rows, w.at[1 - s], 0)
    copy = pltpu.make_async_copy(w, w_far, sem)
    copy.start()
    at_own = pl.ds(pl.multiple_of(s * half, half), half)
    at_oth = pl.ds(pl.multiple_of((1 - s) * half, half), half)
    for n in range(x_ref.shape[0]):
        x = x_ref[n].astype(F32)
        parts = []
        for c in range(2):
            part = nn(own_ref[n], w[c, at_own, :]) + nn(oth_ref[n], w[c, at_oth, :])
            parts.append(x[:, c * half : (c + 1) * half] + part)
        middle = jnp.concatenate(parts, axis=-1)
        mid[n] = middle
        pltpu.make_async_copy(mid.at[n], mid_far.at[n], mid_sems.at[n]).start()
        scale = lax.rsqrt(jnp.mean(middle * middle, axis=-1, keepdims=True) + EPSILON)
        norm_ref[n] = (middle * scale * misc[1:2, :]).astype(BF)
    copy.wait()
    for n in range(x_ref.shape[0]):
        pltpu.make_async_copy(mid.at[n], mid_far.at[n], mid_sems.at[n]).wait()


def hidden_kernel(pos, own_ref, oth_ref, *rest, rows, skip, cut, nl, nr):
    left, right = rest[:nl], rest[nl : nl + nr]
    act_ref, slope_ref, w = rest[nl + nr :]

    @pl.when(pl.program_id(0) == 0)
    def _():
        place(left, pos, 0, rows, w, 0, skip)
        place(right, pos, 1, rows, w, cut - skip)

    count = own_ref.shape[1]
    width = w.shape[1]
    step = 768
    for side, ref in ((0, own_ref), (1, oth_ref)):
        at = slice(side * count, (side + 1) * count)
        for c in range(0, width, step):
            v = nn(ref[0], w[:, c : c + step])
            square = v * v
            p = 0.5 + 0.5 * jnp.tanh(v * (GELU_A + (GELU_A * GELU_B) * square))
            act = v * p
            slope = p + act * ((1.0 - p) * (2.0 * GELU_A + (6.0 * GELU_A * GELU_B) * square))
            act_ref[0, at, c : c + step] = act.astype(BF)
            slope_ref[0, at, c : c + step] = slope.astype(BF)


def wgrad_kernel(meta, *rest, rows, cut, dp, na=1):
    a_refs, b_ref, rest = rest[:na], rest[na], rest[na + 1 :]
    grad, at = 0.0, 0
    for a_ref in a_refs:
        a = a_ref[...].reshape(-1, a_ref.shape[-1])
        b = b_ref[:, at : at + a_ref.shape[1], :].reshape(a.shape[0], -1)
        grad, at = grad + tn(a, b), at + a_ref.shape[1]
    if dp == 0:
        rest[0][...] = grad.astype(BF)
    else:
        rest[-1][...] = grad.astype(BF)
        store_relative(meta, rest[-1], *rest[:4], rows, cut, dp)


def store_relative(meta, total, ls, lk, rs, rk, rows, cut, dp):
    d = meta[1]
    for rel in range(dp):
        x, y, high = rel & 1, (rel >> 1) & 1, rel >> 2
        at = pl.ds(pl.multiple_of((d ^ rel) * rows, rows), rows)
        (ls if y else lk)[x, high] = total[at, :cut]
        (rs if x else rk)[y, high] = total[at, cut:]


def ffn_back_kernel(pos, g_ref, act_ref, slope_ref, w_in, *rest, rows, cut, nl, nr):
    left, right = rest[:nl], rest[nl : nl + nr]
    pre_ref, own_ref, oth_ref, out_own, out_oth, w = rest[nl + nr :]

    @pl.when(pl.program_id(0) == 0)
    def _():
        place(left, pos, 0, rows, w, 0)
        place(right, pos, 1, rows, w, cut)

    count = own_ref.shape[1]
    width = w.shape[0]
    step = 512
    for c in range(0, width, step):
        grad = nt(g_ref[0], w[c : c + step, :])
        pre_ref[0, :, c : c + step] = (grad * slope_ref[0, :, c : c + step].astype(F32)).astype(BF)
    oth_ref[0] = nt(pre_ref[0, count:, :], w_in[...]).astype(BF)
    own_ref[0] = nt(pre_ref[0, :count, :], w_in[...])
    out_own[0] = nn(act_ref[0, :count, :], w[...])
    out_oth[0] = nn(act_ref[0, count:, :], w[...]).astype(BF)


def middle_back_kernel(meta, g_ref, mid_ref, own_ref, oth_ref, misc, w, gm_ref, low_ref, cown_ref, coth_ref):
    s = meta[0]
    half = w.shape[2]
    middle = mid_ref[0]
    scale = lax.rsqrt(jnp.mean(middle * middle, axis=-1, keepdims=True) + EPSILON)
    grad = own_ref[0] + oth_ref[0].astype(F32)
    scaled = grad * misc[1:2, :]
    inner = jnp.mean(scaled * middle, axis=-1, keepdims=True)
    grad_middle = g_ref[0].astype(F32) + scale * scaled - middle * (scale * scale * scale) * inner
    gm_ref[0] = grad_middle
    low = grad_middle.astype(BF)
    low_ref[0] = low
    for ref, which in ((cown_ref, s), (coth_ref, 1 - s)):
        at = pl.ds(pl.multiple_of(which * half, half), half)
        out = nt(low[:, :half], w[0, at, :]) + nt(low[:, half:], w[1, at, :])
        ref[0] = out.astype(BF)


def wo_grad_kernel(meta, own_ref, oth_ref, low_ref, keep_ref, send_ref, total, *, rows, dp):
    s, d = meta[0], meta[1]
    half = own_ref.shape[-1]
    low = low_ref[...].reshape(-1, low_ref.shape[-1])
    for ref, which in ((own_ref, s), (oth_ref, 1 - s)):
        at = pl.ds(pl.multiple_of(which * half, half), half)
        grad = tn(ref[...].reshape(low.shape[0], half), low)
        total[0, at, :] = grad[:, :half]
        total[1, at, :] = grad[:, half:]
    for rel in range(dp):
        at = pl.ds(pl.multiple_of((d ^ rel) * rows, rows), rows)
        keep_ref[rel] = total[s, at, :].astype(BF)
        send_ref[rel] = total[1 - s, at, :].astype(BF)


def attend_back_kernel(meta, q_ref, k_ref, v_ref, e_ref, inv_ref, own_ref, oth_ref, grad_ref, off_ref, diag, dctx, table, low):
    s = meta[0]
    nseq, length, width = q_ref.shape
    half = length // 2
    step = LANES
    rows = step // 4
    span = diag.shape[-1]
    zero = jnp.zeros((), BF)
    first = lane_half((length, LANES), 0)
    for hp in range(width // LANES):
        lanes = slice(hp * LANES, (hp + 1) * LANES)
        diag[...] = jnp.zeros_like(diag)
        for n in range(nseq):
            q, k, v, inv = (ref[n, :, lanes] for ref in (q_ref, k_ref, v_ref, inv_ref))
            dctx[pl.ds(pl.multiple_of(s * half, half), half), :] = own_ref[n, :, lanes]
            dctx[pl.ds(pl.multiple_of((1 - s) * half, half), half), :] = oth_ref[n, :, lanes]
            scaled = (dctx[...].astype(F32) * inv).astype(BF)
            for hh in range(2):
                table[hh] = nt(jnp.where(first if hh == 0 else ~first, scaled, zero), v)
            q_t, c_t = q.astype(F32).T.astype(BF), scaled.astype(F32).T.astype(BF)
            dq, dk, dv = [], [], []
            for hh in range(2):
                lane = hh * HEAD_DIM
                for at in range(0, length, rows):
                    base, within = length - step - at // step * step, at % step
                    e = e_ref[n, hp, hh, at : at + rows, :].astype(F32)
                    term = e * table[hh, at : at + rows]
                    delta = jnp.sum(term, axis=-1, keepdims=True) * inv[at : at + rows, lane : lane + 1]
                    grad = term - e * delta
                    diag[hh, within : within + rows, base : base + length] += grad
                    low[hh, at : at + rows] = grad.astype(BF)
                grad_low = low[hh]
                dq.append(nn(grad_low, jnp.where(first if hh == 0 else ~first, k, zero)))
                dk.append(nn(q_t[lane : lane + HEAD_DIM], grad_low))
                dv.append(nn(c_t[lane : lane + HEAD_DIM], e_ref[n, hp, hh]))
            dk, dv = (jnp.concatenate(x, axis=0).T for x in (dk, dv))
            for c, x in enumerate((dq[0] + dq[1], dk, dv)):
                grad_ref[n, :, c * width + hp * LANES : c * width + (hp + 1) * LANES] = x.astype(BF)
        for hh in range(2):
            acc = jnp.zeros((8, span), F32)
            for g in range(step // 8):
                part = diag[hh, 8 * g : 8 * g + 8, :]
                shift = step - 8 - 8 * g
                acc = acc + (pltpu.roll(part, shift, 1) if shift else part)
            out = acc[7:8]
            for b in range(7):
                out = out + pltpu.roll(acc[b : b + 1], 7 - b, 1)
            off_ref[2 * hp + hh : 2 * hp + hh + 1, :] = out
    off_ref[width // HEAD_DIM :, :] = jnp.zeros((off_ref.shape[0] - width // HEAD_DIM, span), F32)


def qkv_grad_kernel(meta, norm_ref, grad_ref, off_ref, buckets, hsel, bsel, *rest, rows, cut, dp):
    s = meta[0]
    three = grad_ref.shape[-1]
    a = norm_ref[...].reshape(-1, norm_ref.shape[-1])
    total = rest[0] if dp == 0 else rest[-1]
    total[:, :three] = tn(a, grad_ref[...].reshape(a.shape[0], three)).astype(BF)
    one_hot = (
        lax.broadcasted_iota(jnp.int32, (LANES, buckets.shape[1]), 0) == buckets[...]
    ).astype(F32)
    per_bucket = lax.dot_general(
        off_ref[...], one_hot, (((1,), (1,)), ((), ())), precision=lax.Precision.HIGHEST, preferred_element_type=F32
    )
    spread = lax.dot_general(
        hsel[s], per_bucket, (((0,), (0,)), ((), ())), precision=lax.Precision.HIGHEST, preferred_element_type=F32
    )
    column = jnp.sum(spread * bsel[...], axis=-1, keepdims=True)
    total[:, three:] = jnp.broadcast_to(column, (column.shape[0], LANES)).astype(BF)
    if dp:
        store_relative(meta, total, *rest[:4], rows, cut, dp)


def input_grad_kernel(meta, grad_ref, w, own_ref, oth_ref):
    s = meta[0]
    three = grad_ref.shape[-1]
    count = own_ref.shape[1]
    for side, ref in ((0, own_ref), (1, oth_ref)):
        at = pl.ds(pl.multiple_of((s if side == 0 else 1 - s) * count, count), count)
        ref[0] = nt(grad_ref[0, at, :], w[:, :three]).astype(ref.dtype)


def layer_out_kernel(mid_ref, own_ref, oth_ref, out_ref):
    out_ref[0] = (mid_ref[0] + own_ref[0] + oth_ref[0].astype(F32)).astype(BF)


def last_kernel(x_ref, gm_ref, own_ref, oth_ref, misc, out_ref):
    x = x_ref[0].astype(F32)
    scale = lax.rsqrt(jnp.mean(x * x, axis=-1, keepdims=True) + EPSILON)
    scaled = (own_ref[0] + oth_ref[0].astype(F32)) * misc[0:1, :]
    inner = jnp.mean(scaled * x, axis=-1, keepdims=True)
    out_ref[0] = (gm_ref[0] + scale * scaled - x * (scale * scale * scale) * inner).astype(BF)


def finish_kernel(meta, mine_ref, oth_ref, wq_ref, wk_ref, wv_ref, gain_ref, gq_ref, gk_ref, gv_ref, gain_out, bias_out, square, *, dp, table_rows):
    s, d = meta[0], meta[1]
    shard = mine_ref.shape[0]
    width = wq_ref.shape[1]
    half = width // 2
    mine, oth = mine_ref[...].astype(F32), oth_ref[...].astype(F32)
    low, top = jnp.where(s == 0, mine, oth), jnp.where(s == 0, oth, mine)
    total = jnp.zeros((shard, 1), F32)
    for c, (w_ref, out) in enumerate(((wq_ref, gq_ref), (wk_ref, gk_ref), (wv_ref, gv_ref))):
        grad = jnp.concatenate([x[:, c * half : (c + 1) * half] for x in (low, top)], axis=1)
        out[...] = grad
        total = total + jnp.sum(w_ref[...].astype(F32) * grad, axis=1, keepdims=True)
    lane = lax.broadcasted_iota(jnp.int32, (shard, LANES), 1)
    bias = jnp.where(2 * d < dp, low[:, 3 * half :], top[:, 3 * half :])
    square[...] = jnp.zeros_like(square)
    square[:shard, :] = jnp.where(lane == 0, total, bias)
    turned = square[...].T
    gain_out[...] = turned[0:1, :shard] / gain_ref[...].astype(F32)
    bias_out[...] = turned[1:2, :table_rows]


def finish_in_kernel(meta, mine_ref, oth_ref, w_ref, gain_ref, in_ref, out_ref, gain_out, square, *, in_cut, wo_cut, hid_rows, dp):
    s = meta[0]
    shard = mine_ref.shape[0]
    hid = hid_rows * dp
    mine, oth = mine_ref[...].astype(F32), oth_ref[...].astype(F32)
    halves = jnp.where(s == 0, mine, oth), jnp.where(s == 0, oth, mine)
    for c in range(dp):
        at = c * hid_rows
        at = at if at < in_cut else at + wo_cut
        for core, half in enumerate(halves):
            to = (2 * c + core) * hid_rows
            in_ref[:, to : to + hid_rows] = half[:, at : at + hid_rows]
    parts = [x[:, cut] for x in halves for cut in (slice(in_cut, in_cut + wo_cut), slice(hid + wo_cut, None))]
    out_ref[...] = jnp.concatenate(parts, axis=1)
    total = jnp.sum(w_ref[...].astype(F32) * in_ref[...], axis=1, keepdims=True)
    square[...] = jnp.zeros_like(square)
    square[:shard, :] = jnp.broadcast_to(total, (shard, LANES))
    gain_out[...] = square[...].T[0:1, :shard] / gain_ref[...].astype(F32)


def body(
    layer_input,
    gain_attn,
    w_query,
    w_key,
    w_value,
    w_output,
    bias_table,
    gain_ffn,
    ffn_in,
    ffn_out,
    buckets,
    keep_mask,
    out_grad,
):
    dp = lax.axis_size("dp")
    s = lax.axis_index("seq")
    d = lax.axis_index("dp")
    nseq, count, width = layer_input.shape
    length = 2 * count
    span = 2 * length
    half = width // 2
    shard = w_query.shape[0]
    rows = 2 * shard
    hid_rows = ffn_out.shape[0]
    hid = hid_rows * dp
    table_rows = bias_table.shape[0]
    tok = nseq * length
    pairs = half // LANES
    meta = jnp.stack([s, d]).astype(jnp.int32)
    aligned = rows % 16 == 0 and hid_rows % 16 == 0

    def sds(shape, dtype=BF):
        return jax.ShapeDtypeStruct(shape, dtype)

    def far(shape, dtype=BF):
        return pltpu.HBM(shape, dtype)

    def first_columns(h):
        cut = [lax.dynamic_slice_in_dim(w, h * half, half, 1) for w in (w_query, w_key, w_value)]
        table = jnp.pad(bias_table, (0, shard - table_rows))
        extra = jnp.stack([gain_attn, gain_ffn, table], axis=1)
        return jnp.concatenate(cut + [jnp.pad(extra, ((0, 0), (0, LANES - 3)))], axis=1)

    def swapped(mine, theirs):
        theirs = other_core(theirs)
        return jnp.where(s == 0, jnp.concatenate([mine, theirs]), jnp.concatenate([theirs, mine]))

    first_cols = 3 * half + LANES
    second_cols = half + hid
    first_cut = (first_cols // LANES // 2) * LANES
    second_cut = (second_cols // LANES // 2) * LANES
    third_cut = (width // LANES // 2) * LANES

    first = Gather(swapped(first_columns(s), first_columns(1 - s)), first_cut, dp)
    first.high()
    x_oth = other_core(after(layer_input, first.have))
    second_block = swapped(
        *small(
            functools.partial(second_kernel, hid_rows=hid_rows, dp=dp),
            (meta, w_output, ffn_in),
            [(shard, second_cols)] * 2,
            "second_columns",
        )
    )
    x_oth, second_block = meet((x_oth, second_block), (first, "have got"))
    line = dp == 16
    second = LineGather(second_block, second_cut, dp, meta) if line else Gather(second_block, second_cut, dp)
    first.first()
    second.begin()
    meet((), (first, "left right left_x right_y"), (second, "near mid" if line else "near"))
    first.second()
    second.high()
    g_oth = other_core(out_grad)
    keep_oth = other_core(keep_mask.astype(BF))
    keep = keep_mask.astype(BF)
    keep = jnp.where(s == 0, jnp.concatenate([keep, keep_oth], 1), jnp.concatenate([keep_oth, keep], 1))
    mask = ((keep.astype(F32) - 1.0) * 1e9)[:, None, :]
    g_both = jnp.concatenate([out_grad, g_oth], axis=1)

    high = dp // 4
    orders = [np.array([(h << 2) | low for low in lows for h in range(high)], np.int32) for lows in ((0, 1, 2, 3), (0, 2, 1, 3))]
    pos_l, pos_r = ((d ^ jnp.asarray(order)).astype(jnp.int32) for order in orders)
    pos = pos_l

    def settle(pieces, places=pos_l):
        if aligned:
            return pieces
        every = jnp.concatenate(pieces, axis=0)
        order = jnp.argsort(places)
        return [every[order].reshape(1, -1, every.shape[-1])]

    def settle_both(gather):
        left, right = gather.pieces()
        return settle(left), settle(right, pos_r)

    if not aligned:
        pos_k, rows_k, hid_rows_k, nblk, dp_k = jnp.zeros((2, 1), jnp.int32), width, hid, 1, 1
    else:
        pos_k, rows_k, hid_rows_k, nblk, dp_k = jnp.stack([pos_l, pos_r]), rows, hid_rows, dp, dp

    feature = np.arange(width)
    chunk, within = feature // rows, feature % rows
    entry = np.where(within % shard < table_rows, table_rows * chunk + within % shard, -1)
    head, bucket = entry // BUCKETS, entry % BUCKETS
    half_heads = HEADS // 2
    hsel = np.zeros((2, 8, width), np.float32)
    bsel = np.zeros((width, LANES), np.float32)
    for f in range(width):
        if entry[f] >= 0:
            hsel[head[f] // half_heads, head[f] % half_heads, f] = 1.0
            bsel[f, bucket[f]] = 1.0
    bsel_once = jnp.asarray(np.where(within[:, None] < shard, bsel, 0.0))
    hsel, bsel = jnp.asarray(hsel), jnp.asarray(bsel)
    padded = jnp.concatenate([buckets, jnp.full((span - buckets.shape[0],), -1, jnp.int32)])[None]

    seq_block = lambda shape: pl.BlockSpec((1,) + shape, lambda n: (n, 0, 0))
    VMEM = pl.BlockSpec(memory_space=pltpu.VMEM)
    rel = dp if aligned else 0

    def block_shapes(block_rows, cut, cols):
        if aligned:
            left, right = (2, high, block_rows, cut), (2, high, block_rows, cols - cut)
            return [left, left, right, right]
        return [(dp * block_rows, cols)]

    def in_relative(parts, block_rows, cut):
        if aligned:
            return parts
        blocks = parts[0].reshape(dp, block_rows, -1)[pos_l].reshape(2, 2, high, block_rows, -1)
        left, right = blocks[..., :cut], blocks[..., cut:]
        return left[1], left[0], right[:, 1], right[:, 0]

    def gradient(kernel, inputs, block_rows, cut, cols, name, earlier=()):
        shapes = block_shapes(block_rows, cut, cols)

        def ordered(meta_ref, *refs):
            kernel(meta_ref, *refs[len(earlier) :], rows=block_rows, cut=cut, dp=rel)

        parts = pl.pallas_call(
            ordered,
            in_specs=[SMEM] + [ANY] * len(earlier) + [VMEM] * len(inputs),
            out_specs=[VMEM] * len(shapes),
            out_shape=[sds(x) for x in shapes],
            scratch_shapes=[pltpu.VMEM((dp * block_rows, cols), BF)] if aligned else [],
            compiler_params=params(10),
            name=name,
            cost_estimate=cost(name),
        )(meta, *earlier, *inputs)
        return in_relative(parts, block_rows, cut)

    x_oth, ffn_out, mask, g_both = meet(
        (x_oth, ffn_out, mask, g_both), (first, "left right left_far right_far"), (second, "have got")
    )
    second.first()
    third = Gather(ffn_out, third_cut, dp, 1)
    third.begin()
    left, right = settle_both(first)
    q, k, v, normed_attn, misc, peroff, w_qkv = pl.pallas_call(
        functools.partial(qkv_kernel, rows=rows_k, cut=first_cut, width=width, nl=len(left), nr=len(right)),
        grid=(nseq,),
        in_specs=[SMEM, SMEM, seq_block((count, width)), seq_block((count, width)), whole((1, span)), whole(hsel.shape), whole(bsel.shape)]
        + [whole(x.shape) for x in left + right],
        out_specs=[seq_block((length, half))] * 3 + [seq_block((length, width)), whole((8, width)), whole((8, span)), ANY],
        out_shape=[sds((nseq, length, half))] * 3
        + [far((nseq, length, width)), sds((8, width), F32), sds((8, span), F32), far((width, first_cols))],
        scratch_shapes=[pltpu.VMEM((width, first_cols), BF), pltpu.SemaphoreType.DMA],
        compiler_params=params(8),
        name="qkv",
        cost_estimate=cost("qkv"),
    )(meta, pos_k, layer_input, x_oth, padded, hsel, bsel_once, *left, *right)

    q, k, v = meet((q, k, v), (second, "left right left_x right_y"), (third, "near"))
    second.second()
    third.high()
    ctx_own, ctx_send, expo, inv = pl.pallas_call(
        attend_kernel,
        in_specs=[SMEM] + [VMEM] * 5,
        out_specs=[VMEM, VMEM, ANY, ANY],
        out_shape=[
            sds((nseq, count, half)),
            sds((nseq, count, half)),
            far((nseq, pairs, 2, length, length)),
            far((nseq, length, half), F32),
        ],
        scratch_shapes=[
            pltpu.VMEM((half_heads, LANES, span), F32),
            pltpu.VMEM((length, LANES), BF),
            pltpu.VMEM((2, length, length), F32),
            pltpu.VMEM((3, 2, length, length), BF),
            pltpu.VMEM((3, length, LANES), F32),
            pltpu.SemaphoreType.DMA((3,)),
            pltpu.SemaphoreType.DMA((3,)),
        ],
        compiler_params=params(12),
        name="attend",
        cost_estimate=cost("attend"),
    )(meta, q, k, v, mask, peroff)

    ctx_own, ctx_send = meet((ctx_own, ctx_send), (second, "left right left_far right_far"), (third, "have got"))
    ctx_oth = other_core(ctx_send)
    wo_own = front(second.pieces()[0], half, "output_columns")
    wo_oth = other_core(wo_own)
    third.first()
    wo_own, wo_oth = settle([wo_own])[0], settle([wo_oth])[0]
    middle, normed_own, w_o = pl.pallas_call(
        functools.partial(middle_kernel, rows=rows_k),
        in_specs=[SMEM, SMEM] + [VMEM] * 6,
        out_specs=[ANY, VMEM, ANY],
        out_shape=[far((nseq, count, width), F32), sds((nseq, count, width)), far((2, width, half))],
        scratch_shapes=[
            pltpu.VMEM((2, width, half), BF),
            pltpu.VMEM((nseq, count, width), F32),
            pltpu.SemaphoreType.DMA,
            pltpu.SemaphoreType.DMA((nseq,)),
        ],
        compiler_params=params(8),
        name="middle",
        cost_estimate=cost("middle"),
    )(meta, pos_k, layer_input, ctx_own, ctx_oth, misc, wo_own, wo_oth)

    middle, normed_own = meet((middle, normed_own), (third, "left right left_x right_y"))
    third.second()
    normed_oth = other_core(normed_own)
    left, right = settle_both(second)
    act, slope, w_in = pl.pallas_call(
        functools.partial(hidden_kernel, rows=rows_k, skip=half, cut=second_cut, nl=len(left), nr=len(right)),
        grid=(nseq,),
        in_specs=[SMEM, seq_block((count, width)), seq_block((count, width))] + [whole(x.shape) for x in left + right],
        out_specs=[seq_block((length, hid)), seq_block((length, hid)), whole((width, hid))],
        out_shape=[sds((nseq, length, hid)), sds((nseq, length, hid)), sds((width, hid))],
        compiler_params=params(),
        name="hidden",
        cost_estimate=cost("hidden"),
    )(pos_k, normed_own, normed_oth, *left, *right)
    out_parts = gradient(wgrad_kernel, (act, g_both), hid_rows, third_cut, width, "grad_ffn_out")

    out_parts, slope, act = meet((out_parts, slope, act), (third, "left right left_far right_far"))
    out_sum = Scatter(out_parts, dp, 1)
    out_sum.first()
    left, right = settle_both(third)
    seq_half = seq_block((count, width))
    grad_pre, back_own, back_send, out_own, out_send = pl.pallas_call(
        functools.partial(ffn_back_kernel, rows=hid_rows_k, cut=third_cut, nl=len(left), nr=len(right)),
        grid=(nseq,),
        in_specs=[SMEM, seq_block((length, width)), seq_block((length, hid)), seq_block((length, hid)), whole((width, hid))]
        + [whole(x.shape) for x in left + right],
        out_specs=[seq_block((length, hid))] + [seq_half] * 4,
        out_shape=[sds((nseq, length, hid)), sds((nseq, count, width), F32), sds((nseq, count, width))]
        + [far((nseq, count, width), F32), far((nseq, count, width))],
        scratch_shapes=[pltpu.VMEM((hid, width), BF)],
        input_output_aliases={3: 0},
        compiler_params=params(8),
        name="ffn_back",
        cost_estimate=cost("ffn_back"),
    )(pos_k, g_both, act, slope, w_in, *left, *right)

    grad_pre, back_own, back_send, out_own, out_send = meet(
        (grad_pre, back_own, back_send, out_own, out_send), (out_sum, "left_got right_got")
    )
    out_sum.second()
    back_oth, out_oth = other_core(back_send), other_core(out_send)
    in_cut = (hid // LANES // 2) * LANES
    in_parts = gradient(
        functools.partial(wgrad_kernel, na=2),
        (normed_own, normed_oth, grad_pre),
        rows,
        in_cut,
        hid,
        "grad_ffn_in",
        (out_sum.left_send, out_sum.right_send),
    )

    back_own, back_oth, out_oth = meet((back_own, back_oth, out_oth))
    grad_middle, middle_low, dctx_own, dctx_send = pl.pallas_call(
        middle_back_kernel,
        grid=(nseq,),
        in_specs=[SMEM] + [seq_block((count, width))] * 4 + [whole((8, width)), whole((2, width, half))],
        out_specs=[seq_block((count, width)), seq_block((count, width)), seq_block((count, half)), seq_block((count, half))],
        out_shape=[
            far((nseq, count, width), F32),
            sds((nseq, count, width)),
            sds((nseq, count, half)),
            sds((nseq, count, half)),
        ],
        compiler_params=params(8),
        name="middle_back",
        cost_estimate=cost("middle_back"),
    )(meta, out_grad, middle, back_own, back_oth, misc, w_o)
    in_parts, dctx_own, dctx_send, middle_low = meet(
        (in_parts, dctx_own, dctx_send, middle_low), (out_sum, "left_got right_got")
    )
    dctx_oth = other_core(dctx_send)
    rel_meta = meta if aligned else jnp.stack([s, jnp.zeros_like(d)]).astype(jnp.int32)
    wo_keep, wo_send = pl.pallas_call(
        functools.partial(wo_grad_kernel, rows=rows_k, dp=dp_k),
        out_shape=[sds((dp_k, rows_k, half))] * 2,
        in_specs=[SMEM] + [VMEM] * 3,
        out_specs=[VMEM] * 2,
        scratch_shapes=[pltpu.VMEM((2, width, half), F32)],
        compiler_params=params(),
        name="grad_output",
        cost_estimate=cost("grad_output"),
    )(rel_meta, ctx_own, ctx_oth, middle_low)
    wo_got = other_core(wo_send)
    if not aligned:
        wo_keep, wo_got = (x.reshape(dp, rows, half)[d ^ jnp.arange(dp)] for x in (wo_keep, wo_got))
    wo_cut = (half // LANES // 2) * LANES

    wo_keep, wo_got, dctx_own, dctx_oth = meet((wo_keep, wo_got, dctx_own, dctx_oth))
    out_sum.high()
    in_sum = Scatter(with_output_columns(in_parts, wo_keep, wo_got, wo_cut), dp)
    in_sum.first()
    dqkv, off = pl.pallas_call(
        attend_back_kernel,
        in_specs=[SMEM] + [VMEM] * 7,
        out_specs=[VMEM] * 2,
        out_shape=[sds((nseq, length, 3 * half)), sds((8, span), F32)],
        scratch_shapes=[
            pltpu.VMEM((2, LANES, span), F32),
            pltpu.VMEM((length, LANES), BF),
            pltpu.VMEM((2, length, length), F32),
            pltpu.VMEM((2, length, length), BF),
        ],
        compiler_params=params(8),
        name="attend_back",
        cost_estimate=cost("attend_back"),
    )(meta, q, k, v, expo, inv, dctx_own, dctx_oth)
    dqkv, off = meet((dqkv, off), (out_sum, "got"), (in_sum, "left_got right_got"))
    in_sum.second()
    qkv_parts = gradient(
        qkv_grad_kernel,
        (normed_attn, dqkv, off, padded, hsel, bsel),
        rows,
        first_cut,
        first_cols,
        "grad_qkv",
        (in_sum.left_send, in_sum.right_send),
    )

    qkv_parts, dqkv, w_qkv = meet((qkv_parts, dqkv, w_qkv))
    qkv_sum = Scatter(qkv_parts, dp)
    qkv_sum.first()
    in_sum.high()
    dn_own, dn_send = pl.pallas_call(
        input_grad_kernel,
        grid=(nseq,),
        in_specs=[SMEM, seq_block((length, 3 * half)), whole((width, first_cols))],
        out_specs=[seq_half] * 2,
        out_shape=[far((nseq, count, width), F32), sds((nseq, count, width))],
        compiler_params=params(8),
        name="input_grad",
        cost_estimate=cost("input_grad"),
    )(meta, dqkv, w_qkv)
    dn_own, dn_send, in_sum.got[:2] = meet((dn_own, dn_send, in_sum.got[:2]), (qkv_sum, "left_got right_got"))
    qkv_sum.second()
    dn_oth = other_core(dn_send)
    kept = [grad_middle, dn_own] + [pltpu.with_memory_space_constraint(x, pltpu.HBM) for x in (middle, out_own, out_oth)]
    grad_input = pl.pallas_call(
        last_kernel,
        grid=(nseq,),
        in_specs=[seq_half] * 4 + [whole((8, width))],
        out_specs=seq_half,
        out_shape=sds((nseq, count, width)),
        compiler_params=params(10),
        name="last",
        cost_estimate=cost("last"),
    )(layer_input, *kept[:2], dn_oth, misc)
    grad_input, kept = meet((grad_input, kept), (qkv_sum, "left_got right_got"))
    qkv_sum.high()
    grad_ffn_out = out_sum.rest(F32)
    layer_out = pl.pallas_call(
        layer_out_kernel,
        grid=(nseq,),
        in_specs=[seq_half] * 3,
        out_specs=seq_half,
        out_shape=sds((nseq, count, width)),
        compiler_params=params(10),
        name="layer_out",
        cost_estimate=cost("last"),
    )(*kept[2:])
    in_sum.got = after(in_sum.got, qkv_sum.left_got, qkv_sum.right_got)
    mine, theirs = in_sum.halves(meta, shard)
    theirs = other_core(theirs)
    grad_ffn_in, grad_output, gain_ffn_row = pl.pallas_call(
        functools.partial(finish_in_kernel, in_cut=in_cut, wo_cut=wo_cut, hid_rows=hid_rows, dp=dp),
        in_specs=[SMEM] + [VMEM] * 4,
        out_specs=[VMEM] * 3,
        out_shape=[sds((shard, 2 * hid), F32), sds((shard, width), F32), sds((1, shard), F32)],
        scratch_shapes=[pltpu.VMEM((LANES, LANES), F32)],
        compiler_params=params(),
        name="finish_in",
        cost_estimate=cost("finish"),
    )(meta, mine, theirs, ffn_in, gain_ffn[None])
    layer_out, grad_ffn_in, grad_output, gain_ffn_row, grad_ffn_out = meet(
        (layer_out, grad_ffn_in, grad_output, gain_ffn_row, grad_ffn_out), (qkv_sum, "got")
    )

    mine, theirs = qkv_sum.halves(meta, shard)
    theirs = other_core(theirs)
    grad_query, grad_key, grad_value, gain_row, bias_row = pl.pallas_call(
        functools.partial(finish_kernel, dp=dp, table_rows=table_rows),
        in_specs=[SMEM] + [VMEM] * 6,
        out_specs=[VMEM] * 5,
        out_shape=[sds((shard, width), F32)] * 3 + [sds((1, shard), F32), sds((1, table_rows), F32)],
        scratch_shapes=[pltpu.VMEM((LANES, LANES), F32)],
        compiler_params=params(),
        name="finish",
        cost_estimate=cost("finish"),
    )(meta, mine, theirs, w_query, w_key, w_value, gain_attn[None])
    return (
        layer_out,
        grad_input,
        gain_row.reshape(shard),
        grad_query,
        grad_key,
        grad_value,
        grad_output,
        bias_row.reshape(table_rows),
        gain_ffn_row.reshape(shard),
        grad_ffn_in,
        grad_ffn_out,
    )


def solution(mesh):
    both = ("dp", "seq")
    return jax.shard_map(
        body,
        mesh=mesh,
        in_specs=(
            P("dp", "seq", None),
            P(both),
            P(both, None),
            P(both, None),
            P(both, None),
            P(both, None),
            P("dp"),
            P(both),
            P(both, None),
            P(both, None),
            P(),
            P("dp", "seq"),
            P("dp", "seq", None),
        ),
        out_specs=(
            P("dp", "seq", None),
            P("dp", "seq", None),
            P(both),
            P(both, None),
            P(both, None),
            P(both, None),
            P(both, None),
            P("dp"),
            P(both),
            P(both, None),
            P(both, None),
        ),
        check_vma=False,
    )
```
